32 devices in a mesh: ctx: 8 (over y, x, core), exp: 4 (over z).
Axes of the slice: x: 2, y: 2, z: 4, core: 2. Of those that a mesh axis runs over, the one named last changes fastest.
Arguments:
- mixer_in: bfloat16 [1024, 16384], P('ctx', 'exp'), may hold values from -6 to 6
- gate_in: bfloat16 [1024, 16384], P('ctx', 'exp'), may hold values from -6 to 6
- delta_in: bfloat16 [1024, 16384], P('ctx', 'exp'), may hold values from -3 to 3
- b_proj: float32 [16, 1024], P(None, 'ctx'), may hold values from -0.6 to 0.6
- c_proj: float32 [16, 1024], P(None, 'ctx'), may hold values from -1.8 to 1.8
- conv_kernel: float32 [4, 16384], P(None, 'exp'), may hold values from -3 to 3
- conv_bias: float32 [16384], P('exp'), may hold values from -0.5 to 0.5
- delta_bias: float32 [16384], P('exp'), may hold values from -1 to 0
- decay_log: float32 [16, 16384], P(None, 'exp'), may hold values from -12 to -2
- skip_gain: float32 [16384], P('exp'), may hold values from 0.5 to 1.5
- prefix_state: float32 [16, 16384], P(None, 'exp'), may hold values from -6 to 6
- prefix_tail: bfloat16 [3, 16384], P(None, 'exp'), may hold values from -6 to 6
- out_proj: bfloat16 [16384, 8192], P('exp', 'ctx'), may hold values from -0.046875 to 0.046875
- residual: bfloat16 [1024, 8192], P('exp', 'ctx'), may hold values from -40 to 40
- norm_gain: float32 [8192], P('ctx'), may hold values from 0.1 to 1.9
- expert_gate: bfloat16 [4, 8192, 3072], P('exp', None, 'ctx'), may hold values from -0.0625 to 0.0625
- expert_up: bfloat16 [4, 8192, 3072], P('exp', None, 'ctx'), may hold values from -0.0625 to 0.0625
- expert_down: bfloat16 [4, 3072, 8192], P('exp', 'ctx'), may hold values from -0.15625 to 0.15625
- expert_ids: int32 [1024, 2], P('exp'), may hold values from 0 to 3, all different within a row; in each aligned block of 256 rows (0 to 255, 256 to 511, ...) at most 192 rows name the same one
- route_gates: float32 [1024, 2], P('exp'), may hold values from 0.2 to 1
Outputs:
- mixer_out: bfloat16 [1024, 8192], P('exp', 'ctx')
- block_out: bfloat16 [1024, 8192], P('exp', 'ctx')
The draws below stay inside these ranges and needn't reach their ends.
Inputs may be any that keep to these rules, and one draw needn't show every extreme that they name: `expert_ids`: each row names 2 different experts. Within each aligned block of 256 rows (the rows of one index of exp) no expert is named more than 192 times, and in every draw some expert is named exactly 192 times in some block.
All inputs are finite; a program needn't handle non-finite values.
Results may differ from the reference program's by a relative error of at most 0.015.
Values may be sent and summed in bfloat16 or wider, within the bound.
No kernel may reach another device: no remote copies, remote signals or barrier semaphores. Data moves between devices by JAX's collectives and lax.ppermute only.
A program may use at most 128 MiB of HBM per device.

```python
import math
import jax
import jax.numpy as jnp
import numpy as np
from jax import lax

D = 8192
DI = 16384
NS = 16
KC = 4
TOP = 2
FF_DEV = 384
SEQ_LEN = 1024
BLOCK = 256
EXPERTS = 4
CAP = 192
FF_WIN = 3072
N_CTX = 8
N_EXP = 4


def draw_decay_log(key, part):
    key = jax.random.fold_in(key, 11)
    subkeys = jax.random.split(key, 3)
    slow_share = 0.5
    slow_mask = jax.random.uniform(subkeys[0], (NS, DI), jnp.float32) < slow_share
    slow_log = jnp.log(jax.random.uniform(subkeys[1], (NS, DI), jnp.float32, 0.3, 1.5) / SEQ_LEN)
    fast_log = jnp.log(jax.random.uniform(subkeys[2], (NS, DI), jnp.float32, 0.025, 0.05))
    return jnp.where(slow_mask, slow_log, fast_log).astype(jnp.float32)


def draw_residual(key, part):
    key = jax.random.fold_in(key, 12)
    subkeys = jax.random.split(key, 2)
    row_scale = jnp.exp(jax.random.uniform(subkeys[0], (SEQ_LEN, 1), jnp.float32, jnp.log(0.3), jnp.log(3.0)))
    column_scale = 0.3 * jnp.power(10.0, jnp.arange(D, dtype=jnp.float32) / D)[None, :]
    base_value = jnp.clip(jax.random.normal(subkeys[1], (SEQ_LEN, D), jnp.float32), -4.0, 4.0)
    return (base_value * row_scale * column_scale).astype(jnp.bfloat16)


def strengthened(drawn, key, source, target, parts, factor):
    owner, partner = [(jnp.arange(drawn.shape[position]) // (drawn.shape[position] // parts)).reshape([-1 if axis == position else 1 for axis in range(drawn.ndim)]) for position in (source, target)]
    chosen = jax.random.permutation(key, parts)[partner]
    strong = (owner == chosen) | (owner == (partner + parts // 2) % parts)
    return jnp.where(strong, factor * drawn, drawn)


def shard_levels(own_key, dims, cuts, low, high):
    factor_of = 1.0
    for dim, parts in cuts:
        draws = jax.random.uniform(jax.random.fold_in(jax.random.fold_in(own_key, 6), dim), (parts,), jnp.float32, low / len(cuts), high / len(cuts))
        factor_of = factor_of * jnp.repeat(jnp.exp(draws), dims[dim] // parts).reshape((-1,) + (1,) * (len(dims) - 1 - dim))
    return factor_of


def assign_block(key, own, number, rows, count, top, reach, lean):
    sequence = jax.random.permutation(key, count)
    heavy_load, usual = load_shares(count, rows * top, reach, lean, True), load_shares(count, rows * top, reach, lean, False)
    places = jnp.arange(count)

    def named(tallies, turn):
        used = int((tallies > 0).sum())
        fixed = max(1, used // 4)
        passed = fixed + (places - fixed + turn * (used - fixed)) % max(1, count - fixed)
        return jnp.zeros((count,), jnp.int32).at[sequence[jnp.where(places < fixed, places, passed)]].set(jnp.asarray(tallies, jnp.int32))

    tallies = jnp.where(number % 4 == 0, named(heavy_load, number // 4), named(usual, number - number // 4 - 1))
    mixed = jax.random.permutation(jax.random.fold_in(own, 3), count)
    source_of, sink = mixed[0:count // 2 * 2:2], mixed[1:count // 2 * 2:2]
    slack = jnp.minimum(tallies[source_of] - 1, reach - tallies[sink]) // 2
    slack = jnp.where((source_of == sequence[0]) | (sink == sequence[0]) | (tallies[sink] == 0), 0, jnp.maximum(slack, 0))
    passed = jax.random.randint(jax.random.fold_in(own, 4), (count // 2,), 0, 1 << 20) % (slack + 1)
    tallies = tallies.at[source_of].add(-passed).at[sink].add(passed)
    members = jnp.searchsorted(jnp.cumsum(tallies), jnp.arange(rows * top), side="right").astype(jnp.int32)
    table = members.reshape(top, rows).T
    table = table[jax.random.permutation(jax.random.fold_in(own, 1), rows)]
    turn = jax.random.randint(jax.random.fold_in(own, 2), (rows, 1), 0, top)
    return jnp.take_along_axis(table, (jnp.arange(top)[None, :] + turn) % top, axis=1)


def load_shares(amount, total, bound, slope, full):
    loads = [(1 << 20) // math.isqrt(grade ** slope) + 1 for grade in range(1, amount + 1)]
    largest = bound if full else min(bound, max(-(-total // amount), total * loads[0] // sum(loads)))
    least = 1 if total - largest >= amount - 1 else 0
    holding, rest = [largest] + [least] * (amount - 1), total - largest - least * (amount - 1)
    while rest > 0:
        candidates = [i for i in range(1, amount) if holding[i] < largest] or [i for i in range(1, amount) if holding[i] < bound]
        pool, left = sum([loads[i] for i in candidates]), rest
        for i in candidates:
            extra = min(bound - holding[i], max(1, left * loads[i] // pool), rest)
            holding[i] = holding[i] + extra
            rest = rest - extra
    return np.array(holding)


def gaussian(key, shape, scale, reach, shards=(), held_as=jnp.bfloat16):
    loudness = shard_levels(key, shape, shards, -0.22, 0.18) if shards else 1.0
    drawn = jax.random.normal(key, shape, jnp.float32) * scale * loudness
    return jnp.minimum(jnp.maximum(drawn, -reach), reach).astype(held_as)


def bell_draw_with(own_key, extent, width, reach, cuts, heavy, kind=jnp.bfloat16):
    values = width * jax.random.normal(own_key, extent, jnp.float32)
    if cuts:
        values = values * shard_levels(own_key, extent, cuts, -0.22, 0.18)
    return jnp.clip(strengthened(values, jax.random.fold_in(own_key, 3), *heavy), -reach, reach).astype(kind)


def setup_inputs(seed: int = 0) -> dict:
    key_list = jax.random.split(jax.random.key(seed), 21)
    mixer_in = gaussian(key_list[0], (SEQ_LEN, DI), 1.0, 6.0, ((0, 8), (1, 4)))
    gate_in = gaussian(key_list[1], (SEQ_LEN, DI), 1.0, 6.0, ((0, 8), (1, 4)))
    delta_in = gaussian(key_list[2], (SEQ_LEN, DI), 0.5, 3.0, ((0, 8), (1, 4)))
    b_proj = gaussian(key_list[3], (NS, SEQ_LEN), 0.1, 0.6, ((1, 8),), jnp.float32)
    c_proj = gaussian(key_list[4], (NS, SEQ_LEN), 0.3, 1.8, ((1, 8),), jnp.float32)
    conv_kernel = gaussian(key_list[5], (KC, DI), KC ** -0.5, 3.0, ((1, 4),), jnp.float32)
    conv_bias = jnp.clip(jax.random.uniform(key_list[6], (DI,), jnp.float32, -0.5, 0.5) * shard_levels(key_list[6], (DI,), ((0, 4),), -0.4, 0.0), -0.5, 0.5)
    delta_bias = jnp.clip(-1.0 + 1.0 * jax.random.uniform(key_list[7], (DI,), jnp.float32) ** shard_levels(key_list[7], (DI,), ((0, 4),), -0.2, 0.2), -1.0, 0.0)
    decay_log = draw_decay_log(jax.random.fold_in(key_list[20], 71), 0)
    skip_gain = jnp.clip(0.5 + 1.0 * jax.random.uniform(key_list[9], (DI,), jnp.float32) ** shard_levels(key_list[9], (DI,), ((0, 4),), -0.2, 0.2), 0.5, 1.5)
    prefix_state = gaussian(key_list[10], (NS, DI), 1.0, 6.0, ((1, 4),), jnp.float32)
    prefix_tail = gaussian(key_list[11], (KC - 1, DI), 1.0, 6.0, ((1, 4),))
    out_proj = gaussian(key_list[12], (DI, D), DI ** -0.5, 0.046875, ((0, 4), (1, 8)))
    residual = draw_residual(jax.random.fold_in(key_list[20], 71), 0)
    norm_gain = jnp.clip(1.0 + 0.18 * jax.random.normal(key_list[14], (D,), jnp.float32), 0.1, 1.9)
    expert_gate = gaussian(key_list[15], (EXPERTS, D, FF_WIN), D ** -0.5, 0.0625, ((0, 4), (2, 8)))
    expert_up = gaussian(key_list[16], (EXPERTS, D, FF_WIN), D ** -0.5, 0.0625, ((0, 4), (2, 8)))
    expert_down = bell_draw_with(key_list[17], (EXPERTS, FF_WIN, D), FF_WIN ** -0.5, 0.15625, ((0, 4), (1, 8)), (1, 2, 8, 2.0))
    expert_ids_keys = jax.random.split(jax.random.fold_in(key_list[18], 1), SEQ_LEN // BLOCK)
    expert_ids_turns = jax.random.permutation(jax.random.fold_in(key_list[18], 3), SEQ_LEN // BLOCK)
    expert_ids = jax.vmap(lambda own, number: assign_block(jax.random.fold_in(key_list[18], 2), own, number, BLOCK, EXPERTS, TOP, CAP, 2))(expert_ids_keys, expert_ids_turns).reshape((SEQ_LEN, TOP))
    route_gates = jnp.clip(0.2 + 0.8 * jax.random.uniform(key_list[19], (SEQ_LEN, TOP), jnp.float32) ** shard_levels(key_list[19], (SEQ_LEN, TOP), ((0, 4),), -0.2, 0.2), 0.2, 1.0)
    return {"mixer_in": mixer_in, "gate_in": gate_in, "delta_in": delta_in, "b_proj": b_proj, "c_proj": c_proj, "conv_kernel": conv_kernel, "conv_bias": conv_bias, "delta_bias": delta_bias, "decay_log": decay_log, "skip_gain": skip_gain, "prefix_state": prefix_state, "prefix_tail": prefix_tail, "out_proj": out_proj, "residual": residual, "norm_gain": norm_gain, "expert_gate": expert_gate, "expert_up": expert_up, "expert_down": expert_down, "expert_ids": expert_ids, "route_gates": route_gates}


def mixer_layer(mixer_in, gate_in, delta_in, b_proj, c_proj, conv_kernel, conv_bias, delta_bias, decay_log, skip_gain, prefix_state, prefix_tail, out_proj, residual):
    padded = jnp.concatenate([prefix_tail, mixer_in], axis=0).astype(jnp.float32)
    convolved = conv_bias[None, :] + sum((conv_kernel[tap_index][None, :] * padded[tap_index:tap_index + SEQ_LEN] for tap_index in range(KC)))
    conv_act = jax.nn.silu(convolved)
    step_size = jax.nn.softplus(delta_in.astype(jnp.float32) + delta_bias[None, :])
    decay_rate = -jnp.exp(decay_log)
    driving = step_size * conv_act

    def advance(carry_state, inputs):
        step_row, drive_row, b_column, c_column = inputs
        carry_state = jnp.exp(step_row[None, :] * decay_rate) * carry_state + b_column[:, None] * drive_row[None, :]
        return (carry_state, lax.optimization_barrier(jnp.sum(c_column[:, None] * carry_state, axis=0)))
    final_state, scan_out = lax.scan(advance, prefix_state, (step_size, driving, b_proj.T, c_proj.T))
    mixed_out = scan_out + skip_gain[None, :] * conv_act
    gated_rows = (mixed_out * jax.nn.silu(gate_in.astype(jnp.float32))).astype(jnp.bfloat16)
    projected = jnp.dot(gated_rows, out_proj, preferred_element_type=jnp.float32)
    return (residual.astype(jnp.float32) + projected).astype(jnp.bfloat16)

def reference(mixer_in, gate_in, delta_in, b_proj, c_proj, conv_kernel, conv_bias, delta_bias, decay_log, skip_gain, prefix_state, prefix_tail, out_proj, residual, norm_gain, expert_gate, expert_up, expert_down, expert_ids, route_gates):
    mixer_out = mixer_layer(mixer_in, gate_in, delta_in, b_proj, c_proj, conv_kernel, conv_bias, delta_bias, decay_log, skip_gain, prefix_state, prefix_tail, out_proj, residual)
    mixer_wide = mixer_out.astype(jnp.float32)
    norm_scale = lax.rsqrt(lax.optimization_barrier(jnp.mean(mixer_wide * mixer_wide, axis=1, keepdims=True)) + 1e-05)
    normed = (mixer_wide * norm_scale * norm_gain[None, :]).astype(jnp.bfloat16)
    slot_total = N_EXP * CAP
    flat_choice = expert_ids.reshape(N_EXP, BLOCK * TOP)
    flat_gates = route_gates.reshape(-1)
    token_of = (jnp.arange(SEQ_LEN * TOP) // TOP).astype(jnp.int32)
    block_base = (jnp.arange(N_EXP) * CAP).astype(jnp.int32)[:, None]

    def one_expert(expert_num, totals):
        expert_index = jnp.asarray(expert_num).astype(jnp.int32)
        chosen = (flat_choice == expert_index).astype(jnp.int32)
        earlier_count = jnp.cumsum(chosen, axis=1).astype(jnp.int32) - 1
        places = jnp.where(chosen > 0, block_base + earlier_count, slot_total).astype(jnp.int32).reshape(-1)
        picks = jnp.zeros((slot_total,), jnp.int32).at[places].set(token_of, mode='drop')
        weights = jnp.zeros((slot_total,), jnp.float32).at[places].set(flat_gates, mode='drop')
        arrived = normed[picks]
        w_gate = lax.dynamic_index_in_dim(expert_gate, expert_index, 0, keepdims=False)
        w_up = lax.dynamic_index_in_dim(expert_up, expert_index, 0, keepdims=False)
        w_down = lax.dynamic_index_in_dim(expert_down, expert_index, 0, keepdims=False)
        gate_act = jnp.dot(arrived, w_gate, preferred_element_type=jnp.float32)
        up_act = jnp.dot(arrived, w_up, preferred_element_type=jnp.float32)
        hidden = (jax.nn.silu(gate_act) * up_act).astype(jnp.bfloat16)

        def add_share(share, accum):
            begin = (jnp.asarray(share) * FF_DEV).astype(jnp.int32)
            part_sum = jnp.dot(lax.dynamic_slice_in_dim(hidden, begin, FF_DEV, 1), lax.dynamic_slice_in_dim(w_down, begin, FF_DEV, 0), preferred_element_type=jnp.float32)
            return accum + lax.optimization_barrier(part_sum.astype(jnp.bfloat16)).astype(jnp.float32)
        expert_sum = lax.fori_loop(0, N_CTX, add_share, jnp.zeros((slot_total, D), jnp.float32))
        expert_out = lax.optimization_barrier(expert_sum.astype(jnp.bfloat16)).astype(jnp.float32)
        return totals.at[picks].add(weights[:, None] * expert_out)
    expert_mix = lax.fori_loop(0, EXPERTS, one_expert, jnp.zeros((SEQ_LEN, D), jnp.float32))
    block_out = (mixer_wide + expert_mix).astype(jnp.bfloat16)
    return (mixer_out, block_out)
```

```python
import functools

import jax
import jax.numpy as jnp
from jax import lax
from jax.experimental import pallas as pl
from jax.experimental.pallas import tpu as pltpu
from jax.sharding import PartitionSpec as P

D = 8192
LOG2E = 1.4426950408889634
LANES = 128
MIB = 1 << 20


def from_behind(array, axis, by):
    length = lax.axis_size(axis)
    pairs = [(i, i + by) for i in range(length) if 0 <= i + by < length]
    return lax.ppermute(array, axis, pairs)


def swap(array, axis, mask):
    return lax.ppermute(array, axis, [(i, i ^ mask) for i in range(lax.axis_size(axis))])


def halves_kernel(split_dim, first, second, low, high):
    half = low.shape[split_dim]
    if split_dim == 0:
        low[...] = first[0:half, :]
        high[...] = second[half:, :]
    else:
        low[...] = first[:, 0:half]
        high[...] = second[:, half:]


def halves(first, second, split_dim, after=()):
    shape = list(first.shape)
    shape[split_dim] //= 2
    whole = pl.BlockSpec(first.shape, lambda j: (0, 0))
    part = pl.BlockSpec(tuple(shape), lambda j: (0, 0))
    return launch(
        functools.partial(halves_kernel, split_dim),
        [],
        [first, second],
        [whole, whole],
        [part, part],
        [jax.ShapeDtypeStruct(tuple(shape), first.dtype)] * 2,
        after=after,
        limit=16,
        cost_estimate=cost(0, 6 * first.size),
        name="halves",
    )


def gather_parts(array, split_dim=None, after=()):
    count = lax.axis_size("ctx")
    if count != 8:
        return [(0, None, array)] + [(m, None, swap(array, "ctx", m)) for m in range(1, count)]
    over_a = swap(array, "ctx", 2)
    over_b = swap(array, "ctx", 4)
    if split_dim is None:
        crossed = [(6, None, swap(array, "ctx", 6))]
    else:
        low, high = halves(over_a, over_b, split_dim, after)
        crossed = [(6, 0, swap(low, "ctx", 4)), (6, 1, swap(high, "ctx", 2))]
    parts = []
    for mask, which, part in [(0, None, array), (2, None, over_a), (4, None, over_b)] + crossed:
        parts.append((mask, which, part))
        parts.append((mask + 1, which, swap(part, "ctx", 1)))
    return parts


def silu(value):
    return value / (1.0 + jnp.exp(-value))


def cost(flops, moved, transcendentals=0):
    return pl.CostEstimate(
        flops=int(flops), bytes_accessed=int(moved), transcendentals=int(transcendentals)
    )


ANY = pl.BlockSpec(memory_space=pl.ANY)


def launch(
    kernel, scalars, operands, in_specs, out_specs, out_shape, after=(), grid=(1,), scratch=(),
    limit=56, **rest
):
    taken = len(scalars) + len(operands)

    def body(*refs):
        kernel(*refs[:taken], *refs[taken + len(after) :])

    return pl.pallas_call(
        body,
        grid_spec=pltpu.PrefetchScalarGridSpec(
            num_scalar_prefetch=len(scalars),
            grid=grid,
            in_specs=list(in_specs) + [ANY] * len(after),
            out_specs=out_specs,
            scratch_shapes=list(scratch),
        ),
        out_shape=out_shape,
        compiler_params=pltpu.CompilerParams(vmem_limit_bytes=limit * MIB),
        **rest,
    )(*scalars, *operands, *after)


def cut_kernel(count, *refs):
    for source, out in zip(refs[-2 * count : -count], refs[-count:]):
        out[...] = source[...]


def cut_columns(me, rows, width, masks, after=()):
    step = rows.shape[0] // 3

    def block(mask):
        return pl.BlockSpec((step, width), lambda i, me: (i, me[0] ^ mask))

    return launch(
        functools.partial(cut_kernel, len(masks)),
        [me],
        [rows] * len(masks),
        [block(mask) for mask in masks],
        [pl.BlockSpec((step, width), lambda i, me: (i, 0))] * len(masks),
        [jax.ShapeDtypeStruct((rows.shape[0], width), rows.dtype)] * len(masks),
        after=after,
        grid=(3,),
        cost_estimate=cost(0, 4 * rows.shape[0] * width * len(masks)),
        name="cut_columns",
    )


def join_kernel(count, *refs):
    pieces, out, sems = refs[:count], refs[count], refs[count + 1]
    copies, row = [], 0
    for place, piece in enumerate(pieces):
        copies.append(
            pltpu.make_async_copy(piece, out.at[pl.ds(row, piece.shape[0]), :], sems.at[place])
        )
        row += piece.shape[0]
    for copy in copies:
        copy.start()
    for copy in copies:
        copy.wait()


def join(pieces, after=()):
    rows = sum(piece.shape[0] for piece in pieces)
    columns = pieces[0].shape[1]
    return launch(
        functools.partial(join_kernel, len(pieces)),
        [],
        list(pieces),
        [ANY] * len(pieces),
        pl.BlockSpec((rows, columns), lambda j: (0, 0)),
        jax.ShapeDtypeStruct((rows, columns), pieces[0].dtype),
        after=after,
        scratch=[pltpu.SemaphoreType.DMA((len(pieces),))],
        limit=16,
        cost_estimate=cost(0, 4 * rows * columns),
        name="join",
    )


BLOCK = 512


def by_blocks(kernel, split, *refs):
    width = next(ref for ref, cut in zip(refs, split) if cut).shape[1]

    def one(index, _):
        lanes = pl.ds(pl.multiple_of(index * BLOCK, BLOCK), BLOCK)
        kernel(*[ref.at[:, lanes] if cut else ref for ref, cut in zip(refs, split)])
        return 0

    lax.fori_loop(0, width // BLOCK, one, 0)


GROUP = 16
STATE_ROWS = 32


def state_kernel(
    mixer, rim, delta, kernel, bias, delta_bias, decay_log, extra, b_wide, step_out, conv_out,
    end_out, padded,
):
    tokens, width = mixer.shape
    blocks = width // LANES
    padded[0:8, :] = rim[...]
    padded[8:, :] = mixer[...].astype(jnp.float32)
    rate = [
        -jnp.exp(decay_log[:, k * LANES : (k + 1) * LANES]) * LOG2E for k in range(blocks)
    ]
    taps = kernel.shape[0]

    def group(index, carry):
        states, total = carry
        base = pl.multiple_of(index * GROUP, GROUP)
        window = padded[pl.ds(base, GROUP + 8), :]
        convolved = bias[...] + sum(
            kernel[k : k + 1, :] * window[9 - taps + k : 9 - taps + k + GROUP, :]
            for k in range(taps)
        )
        conv_act = silu(convolved)
        step = jnp.log(
            1.0 + jnp.exp(delta[pl.ds(base, GROUP), :].astype(jnp.float32) + delta_bias[...])
        )
        step_out[pl.ds(base, GROUP), :] = step
        conv_out[pl.ds(base, GROUP), :] = conv_act
        drive = step * conv_act
        states = list(states)
        for i in range(GROUP):
            b_tile = b_wide[pl.ds(pl.multiple_of((base + i) * 16, 16), 16), :]
            for k in range(blocks):
                lanes = slice(k * LANES, (k + 1) * LANES)
                states[k] = (
                    jnp.exp2(step[i : i + 1, lanes] * rate[k]) * states[k]
                    + b_tile * drive[i : i + 1, lanes]
                )
        return tuple(states), total + step[0:8, :] + step[8:16, :]

    start = tuple(jnp.zeros((16, LANES), jnp.float32) for _ in range(blocks))
    states, total = lax.fori_loop(
        0, tokens // GROUP, group, (start, jnp.zeros((8, width), jnp.float32))
    )
    for k in range(blocks):
        end_out[0:16, k * LANES : (k + 1) * LANES] = states[k].astype(end_out.dtype)
    total = jnp.sum(total, axis=0, keepdims=True)
    place = lax.broadcasted_iota(jnp.int32, (16, width), 0)
    pieces = jnp.where(place == 3, extra[...], 0.0)
    for row in range(3):
        piece = total.astype(jnp.bfloat16).astype(jnp.float32)
        pieces = jnp.where(place == row, piece, pieces)
        total = total - piece
    end_out[16:32, :] = pieces.astype(end_out.dtype)


def local_states(mixer_in, rim8, delta_in, kernel, bias, delta_bias, decay_log, extra, b_wide):
    tokens, channels = mixer_in.shape
    width = 1024
    rows = lambda n: pl.BlockSpec((n, width), lambda j: (0, j))
    return launch(
        functools.partial(by_blocks, state_kernel, [1] * 8 + [0] + [1] * 3 + [0]),
        [],
        [mixer_in, rim8, delta_in, kernel, bias, delta_bias, decay_log, extra, b_wide],
        [
            rows(tokens),
            rows(8),
            rows(tokens),
            rows(kernel.shape[0]),
            rows(1),
            rows(1),
            rows(16),
            rows(1),
            pl.BlockSpec((tokens * 16, LANES), lambda j: (0, 0)),
        ],
        [rows(tokens), rows(tokens), rows(STATE_ROWS)],
        [
            jax.ShapeDtypeStruct((tokens, channels), jnp.float32),
            jax.ShapeDtypeStruct((tokens, channels), jnp.float32),
            jax.ShapeDtypeStruct((STATE_ROWS, channels), jnp.bfloat16),
        ],
        grid=(channels // width,),
        scratch=[pltpu.VMEM((tokens + 8, BLOCK), jnp.float32)],
        cost_estimate=cost(
            tokens * channels * 16 * 5, tokens * channels * 12, tokens * channels * 18
        ),
        name="local_states",
    )


def gains_kernel(masks, me, *refs):
    parts, out = refs[: len(masks)], refs[-1]
    width = out.shape[2]
    for mask, part in zip(masks, parts):
        row = part[...].astype(jnp.float32)[3:4, :]
        gain = row[:, 0:width] + row[:, width : 2 * width] + row[:, 2 * width : 3 * width]
        out[me[0] ^ mask] = 1.0 / gain


def inverse_gains(me, ends, width):
    return launch(
        functools.partial(gains_kernel, [mask for mask, _, _ in ends]),
        [me],
        [end for _, _, end in ends],
        [pl.BlockSpec((16, 3 * width), lambda j, me: (1, 0))] * len(ends),
        pl.BlockSpec((len(ends), 1, width), lambda j, me: (0, 0, 0)),
        jax.ShapeDtypeStruct((len(ends), 1, width), jnp.float32),
        limit=16,
        name="inverse_gains",
    )


def fold_rows(tiles):
    place = lax.broadcasted_iota(jnp.int32, (8, LANES), 0)
    for shift in (1, 2, 4):
        first = (place & shift) == 0
        tiles = [
            jnp.where(first, a, b) + pltpu.roll(jnp.where(first, b, a), shift, 0)
            for a, b in zip(tiles[0::2], tiles[1::2])
        ]
    return tiles[0]


def readout_kernel(
    masks, me, step_in, conv_in, gate_in, decay_log, skip, b_wide, c_wide, entering, *refs
):
    ends = refs[: len(masks)]
    gated, leaving, scanned = refs[len(masks) : len(masks) + 3]
    tokens, width = step_in.shape
    blocks = width // LANES
    rate = [
        -jnp.exp(decay_log[:, k * LANES : (k + 1) * LANES]) * LOG2E for k in range(blocks)
    ]
    start = [entering[:, k * LANES : (k + 1) * LANES] for k in range(blocks)]
    if masks:
        held = refs[-1]
        for mask, end in zip(masks, ends):
            held[mask] = end[...].astype(jnp.float32)
        for owner in range(len(masks) - 1):
            end = held[me[0] ^ owner]
            total = end[16:17, :] + end[17:18, :] + end[18:19, :]
            for k in range(blocks):
                lanes = slice(k * LANES, (k + 1) * LANES)
                later = jnp.exp2(total[:, lanes] * rate[k]) * start[k] + end[0:16, lanes]
                start[k] = jnp.where(owner < me[0], later, start[k])

    def group(index, states):
        base = pl.multiple_of(index * GROUP, GROUP)
        step = step_in[pl.ds(base, GROUP), :]
        conv_act = conv_in[pl.ds(base, GROUP), :]
        drive = step * conv_act
        states = list(states)
        for half in range(GROUP // 8):
            tiles = [[] for _ in range(blocks)]
            for i in range(half * 8, half * 8 + 8):
                spot = pl.ds(pl.multiple_of((base + i) * 16, 16), 16)
                b_tile = b_wide[spot, :]
                c_tile = c_wide[spot, :]
                for k in range(blocks):
                    lanes = slice(k * LANES, (k + 1) * LANES)
                    states[k] = (
                        jnp.exp2(step[i : i + 1, lanes] * rate[k]) * states[k]
                        + b_tile * drive[i : i + 1, lanes]
                    )
                    read = c_tile * states[k]
                    tiles[k].append(read[0:8] + read[8:16])
            for k in range(blocks):
                scanned[
                    pl.ds(pl.multiple_of(base + half * 8, 8), 8), k * LANES : (k + 1) * LANES
                ] = fold_rows(tiles[k])
        gate = gate_in[pl.ds(base, GROUP), :].astype(jnp.float32)
        mixed = scanned[pl.ds(base, GROUP), :] + skip[...] * conv_act
        gated[pl.ds(base, GROUP), :] = (mixed * silu(gate)).astype(gated.dtype)
        return tuple(states)

    states = lax.fori_loop(0, tokens // GROUP, group, tuple(start))
    for k in range(blocks):
        leaving[:, k * LANES : (k + 1) * LANES] = states[k]


def read_out(
    me, chunk, chunks, step, conv_act, gate_in, decay_log, skip, b_wide, c_wide, entering, ends,
    after=(),
):
    tokens, channels = step.shape
    tokens = tokens // chunks
    width = 1024
    some = pl.BlockSpec((tokens, width), lambda j, me: (chunk, j))
    rows = lambda n: pl.BlockSpec((n, width), lambda j, me: (0, j))
    wide = pl.BlockSpec((tokens * 16, LANES), lambda j, me: (chunk, 0))
    masks = [mask for mask, _, _ in ends]
    scratch = [pltpu.VMEM((tokens, BLOCK), jnp.float32)]
    if ends:
        scratch.append(pltpu.VMEM((len(ends), STATE_ROWS, BLOCK), jnp.float32))
    split = [0] + [1] * 5 + [0, 0, 1] + [1] * len(ends) + [1, 1] + [0] * len(scratch)
    return launch(
        functools.partial(by_blocks, functools.partial(readout_kernel, masks), split),
        [me],
        [step, conv_act, gate_in, decay_log, skip, b_wide, c_wide, entering]
        + [end for _, _, end in ends],
        [some, some, some, rows(16), rows(1), wide, wide, rows(16)]
        + [rows(STATE_ROWS)] * len(ends),
        [rows(tokens), rows(16)],
        [
            jax.ShapeDtypeStruct((tokens, channels), jnp.bfloat16),
            jax.ShapeDtypeStruct((16, channels), jnp.float32),
        ],
        after=after,
        grid=(channels // width,),
        scratch=scratch,
        cost_estimate=cost(
            tokens * channels * 16 * 7, tokens * channels * 12, tokens * channels * 18
        ),
        name="read_out",
    )


def project_kernel(layout, me, weight, *refs):
    parts, (out, held, sems) = refs[: len(layout)], refs[len(layout) :]
    rows = held.shape[0] // (1 + max(mask for mask, _ in layout))

    @pl.when(pl.program_id(0) == 0)
    def _():
        copies = []
        for place, (mask, column) in enumerate(layout):
            part = parts[place]
            owner = me[0] ^ mask
            copies.append(
                pltpu.make_async_copy(
                    part,
                    held.at[
                        pl.ds(pl.multiple_of(owner * rows, rows), rows),
                        pl.ds(column, part.shape[1]),
                    ],
                    sems.at[place],
                )
            )
        for copy in copies:
            copy.start()
        for copy in copies:
            copy.wait()

    out[...] = jnp.dot(held[...], weight[...], preferred_element_type=jnp.float32).astype(
        out.dtype
    )


def project(me, parts, weight, after=()):
    depth, columns = weight.shape
    rows = parts[0][2].shape[0]
    total = rows * lax.axis_size("ctx")
    layout = [(mask, (which or 0) * depth // 2) for mask, which, _ in parts]
    tile = min(256, columns)
    return launch(
        functools.partial(project_kernel, layout),
        [me],
        [weight] + [part for _, _, part in parts],
        [pl.BlockSpec((depth, tile), lambda j, me: (0, j))] + [ANY] * len(parts),
        pl.BlockSpec((total, tile), lambda j, me: (0, j)),
        jax.ShapeDtypeStruct((total, columns), jnp.bfloat16),
        after=after,
        grid=(columns // tile,),
        scratch=[
            pltpu.VMEM((total, depth), jnp.bfloat16),
            pltpu.SemaphoreType.DMA((len(parts),)),
        ],
        limit=40,
        cost_estimate=cost(
            2 * total * depth * columns, 2 * (total * depth + depth * columns + total * columns)
        ),
        name="project",
    )


def hidden_kernel(layout, me, gain, gate_rows, up_rows, *refs):
    parts, (out, held, total, squares, sems) = refs[: len(layout)], refs[len(layout) :]
    turn = pl.program_id(0)

    def copy_of(place):
        mask, row = layout[place]
        part = parts[place]
        column = ((me[0] ^ mask) & 1) * part.shape[1]
        return pltpu.make_async_copy(
            part,
            held.at[
                mask // 2,
                pl.ds(row, part.shape[0]),
                pl.ds(pl.multiple_of(column, LANES), part.shape[1]),
            ],
            sems.at[place],
        )

    @pl.when(turn == 0)
    def _():
        for place in range(len(layout)):
            copy_of(place).start()
        total[...] = jnp.zeros_like(total)
        squares[...] = jnp.zeros_like(squares)

    for place, (mask, _) in enumerate(layout):

        @pl.when(turn == mask // 2)
        def _():
            copy_of(place).wait()

    width = out.shape[1]
    both = jnp.concatenate([gate_rows[...], up_rows[...]], axis=1)
    total[...] += jnp.dot(held[turn], both, preferred_element_type=jnp.float32)
    slots = out.shape[0]
    for row in range(0, slots, 64):
        mixer_square = squares[row : row + 64, :]
        for lane in range(0, held.shape[2], LANES):
            value = held[turn, row : row + 64, lane : lane + LANES].astype(jnp.float32)
            spot = lane % gain.shape[2]
            value = value * gain[lane // gain.shape[2], :, spot : spot + LANES]
            mixer_square += value * value
        squares[row : row + 64, :] = mixer_square

    @pl.when(turn == pl.num_programs(0) - 1)
    def _():
        def finish(index, _):
            spot = pl.ds(pl.multiple_of(index * 64, 64), 64)
            mean = jnp.sum(squares[spot, :], axis=1, keepdims=True) / D
            factor = lax.rsqrt(mean + 1e-05)
            gate_act = total[spot, 0:width] * factor
            up_act = total[spot, width:] * factor
            out[spot, :] = (silu(gate_act) * up_act).astype(out.dtype)
            return 0

        lax.fori_loop(0, out.shape[0] // 64, finish, 0)


def hidden_units(me, parts, one_over_gain, gate, up, after=()):
    slots, depth = parts[0][2].shape
    count = lax.axis_size("ctx")
    width = gate.shape[1]
    layout = [(mask, (which or 0) * slots // 2) for mask, which, _ in parts]
    block = pl.BlockSpec((2 * depth, width), lambda k, me: ((me[0] // 2) ^ k, 0))
    return launch(
        functools.partial(hidden_kernel, layout),
        [me],
        [one_over_gain, gate, up] + [part for _, _, part in parts],
        [
            pl.BlockSpec((2, 1, depth), lambda k, me: ((me[0] // 2) ^ k, 0, 0)),
            block,
            block,
        ] + [ANY] * len(parts),
        pl.BlockSpec((slots, width), lambda k, me: (0, 0)),
        jax.ShapeDtypeStruct((slots, width), jnp.bfloat16),
        after=after,
        grid=(count // 2,),
        scratch=[
            pltpu.VMEM((count // 2, slots, 2 * depth), jnp.bfloat16),
            pltpu.VMEM((slots, 2 * width), jnp.float32),
            pltpu.VMEM((slots, LANES), jnp.float32),
            pltpu.SemaphoreType.DMA((len(parts),)),
        ],
        limit=40,
        cost_estimate=cost(
            4 * slots * depth * count * width, 2 * count * depth * (slots + 2 * width)
        ),
        name="hidden_units",
    )


def down_kernel(count, *refs):
    units, weights, (out, held, sems) = refs[:count], refs[count : 2 * count], refs[2 * count :]
    width = weights[0].shape[0]

    @pl.when(pl.program_id(0) == 0)
    def _():
        copies = [
            pltpu.make_async_copy(
                unit, held.at[:, pl.ds(place * width, width)], sems.at[place]
            )
            for place, unit in enumerate(units)
        ]
        for copy in copies:
            copy.start()
        for copy in copies:
            copy.wait()

    tall = jnp.concatenate([weight[...] for weight in weights], axis=0)
    out[...] = jnp.dot(held[...], tall, preferred_element_type=jnp.float32).astype(out.dtype)


def down(units, weights, after=()):
    slots, width = units[0].shape
    columns = weights[0].shape[1]
    depth = width * len(weights)
    tile = min(256, columns)
    return launch(
        functools.partial(down_kernel, len(units)),
        [],
        list(units) + list(weights),
        [ANY] * len(units) + [pl.BlockSpec((width, tile), lambda j: (0, j))] * len(weights),
        pl.BlockSpec((slots, tile), lambda j: (0, j)),
        jax.ShapeDtypeStruct((slots, columns), jnp.bfloat16),
        after=after,
        grid=(columns // tile,),
        scratch=[
            pltpu.VMEM((slots, depth), jnp.bfloat16),
            pltpu.SemaphoreType.DMA((len(units),)),
        ],
        limit=40,
        cost_estimate=cost(
            2 * slots * depth * columns, 2 * (slots * depth + depth * columns + slots * columns)
        ),
        name="down",
    )


def pick_kernel(count, rows, *refs):
    for picks, out in zip(refs[:count], refs[count:]):
        out[...] = lax.dot_general(
            picks[...], rows[...], (((0,), (0,)), ((), ())), preferred_element_type=jnp.float32
        ).astype(out.dtype)


def pick_rows(picks, rows, after=()):
    shape = (picks[0].shape[1], rows.shape[1])
    whole = lambda shape: pl.BlockSpec(shape, lambda j: (0, 0))
    return launch(
        functools.partial(pick_kernel, len(picks)),
        [],
        [rows] + list(picks),
        [whole(rows.shape)] + [whole(pick.shape) for pick in picks],
        [whole(shape)] * len(picks),
        [jax.ShapeDtypeStruct(shape, rows.dtype)] * len(picks),
        after=after,
        limit=24,
        cost_estimate=cost(2 * rows.size * shape[0] * len(picks), 4 * rows.size),
        name="pick_rows",
    )


def combine_kernel(mixer, picks, gates, *refs):
    answers, out = refs[:-1], refs[-1]
    total = mixer[...].astype(jnp.float32)
    for place, answer in enumerate(answers):
        total += gates[place] * jnp.dot(
            picks[place], answer[...], preferred_element_type=jnp.float32
        )
    out[...] = total.astype(out.dtype)


def combine(mixer_out, picks, gates, answers):
    return pl.pallas_call(
        combine_kernel,
        out_shape=jax.ShapeDtypeStruct(mixer_out.shape, jnp.bfloat16),
        compiler_params=pltpu.CompilerParams(vmem_limit_bytes=24 * MIB),
        cost_estimate=cost(
            2 * mixer_out.size * answers[0].shape[0] * len(answers), 4 * mixer_out.size
        ),
        name="combine",
    )(mixer_out, picks, gates, *answers)


def shards(
    mixer_in,
    gate_in,
    delta_in,
    b_proj,
    c_proj,
    conv_kernel,
    conv_bias,
    delta_bias,
    decay_log,
    skip_gain,
    prefix_state,
    prefix_tail,
    out_proj,
    residual,
    norm_gain,
    expert_gate,
    expert_up,
    expert_down,
    expert_ids,
    route_gates,
):
    tokens = mixer_in.shape[0]
    rim = prefix_tail.shape[0]
    ctx_count = lax.axis_size("ctx")
    exp_count = lax.axis_size("exp")
    ctx_me = lax.axis_index("ctx")
    exp_me = lax.axis_index("exp")
    me = ctx_me.astype(jnp.int32).reshape(1)

    rim_rows = from_behind(mixer_in[tokens - rim :], "ctx", 1)
    rim_rows = jnp.where(ctx_me == 0, prefix_tail, rim_rows).astype(jnp.float32)
    rim8 = jnp.pad(rim_rows, ((8 - rim, 0), (0, 0)))

    width = out_proj.shape[1]
    down_rows = expert_down[0]
    down_parts = {}

    def send_columns(masks, after=()):
        for mask, cut in zip(masks, cut_columns(me, down_rows, width, masks, after)):
            down_parts[mask] = cut if mask == 0 else swap(cut, "ctx", mask)
        return tuple(down_parts[mask] for mask in masks)

    first = send_columns([2, 4])

    extra, left = [], norm_gain
    for _ in range(3):
        extra.append(lax.reduce_precision(left, 8, 7))
        left = left - extra[-1]
    extra = jnp.concatenate(extra)
    extra = jnp.pad(extra, (0, mixer_in.shape[1] - extra.shape[0]))[None, :]

    wide = lambda proj: jnp.broadcast_to(proj.T[:, :, None], (tokens, 16, LANES)).reshape(
        tokens * 16, LANES
    )
    b_wide, c_wide = wide(b_proj), wide(c_proj)
    step, conv_act, end = local_states(
        mixer_in,
        rim8,
        delta_in,
        conv_kernel,
        conv_bias[None, :],
        delta_bias[None, :],
        decay_log,
        extra,
        b_wide,
    )
    chunks = 2
    state, ends = prefix_state, gather_parts(join([end], first))
    one_over_gain = inverse_gains(me, ends, width)
    gated = []
    for chunk in range(chunks):
        rows, state = read_out(
            me,
            chunk,
            chunks,
            step,
            conv_act,
            gate_in,
            decay_log,
            skip_gain[None, :],
            b_wide,
            c_wide,
            state,
            ends,
        )
        ends = []
        gated.append(rows)
    gathered, projected, after, order = [], [], gated[-1:], gated[-1:]
    for rows in gated:
        parts = gather_parts(rows, 1, after)
        after = [part for mask, which, part in parts if which is not None and mask % 2 == 0]
        gathered.append(parts)
        partial = project(me, parts, out_proj, order)
        order = [partial]
        projected.append(
            lax.psum_scatter(partial, "exp", scatter_dimension=0, tiled=True)
        )
    last_seen = [part for mask, _, part in gathered[-1] if mask in (2, 4)]
    rest = send_columns([3, 5, 6, 7, 0, 1] + list(range(8, ctx_count)), last_seen)

    block_rows = residual.shape[0]
    owners = block_rows // tokens
    projected = jnp.stack(
        [piece.reshape(owners, tokens // chunks, width) for piece in projected], axis=1
    ).reshape(block_rows, width)
    mixer_out = (residual.astype(jnp.float32) + projected.astype(jnp.float32)).astype(
        jnp.bfloat16
    )
    mixer_wide = mixer_out.astype(jnp.float32)
    scaled = (mixer_wide * norm_gain[None, :]).astype(jnp.bfloat16)
    experts = expert_gate.shape[0] * exp_count
    capacity = 3 * block_rows * expert_ids.shape[1] // (2 * experts)
    spots = jnp.arange(capacity, dtype=jnp.int32)
    picks, gates = [], []
    for mask in range(exp_count):
        named = expert_ids == (exp_me ^ mask)
        here = jnp.any(named, axis=1)
        place = jnp.cumsum(here.astype(jnp.int32)) - 1
        picks.append(here[:, None] & (place[:, None] == spots[None, :]))
        gates.append(jnp.sum(jnp.where(named, route_gates, 0.0), axis=1, keepdims=True))
    picked = [pick.astype(jnp.bfloat16) for pick in picks]

    groups = [[0, 2], [1, 3]] if exp_count == 4 else [list(range(exp_count))]
    last = groups[-1][-1] if len(groups) > 1 else None
    masks = [mask for mask in range(exp_count) if mask != last][::-1]
    rows = dict(zip(masks, pick_rows([picked[mask] for mask in masks], scaled, rest[:3])))
    pieces = {mask: swap(rows[mask], "exp", mask) for mask in masks if mask != 0}
    pieces[0] = rows[0]
    if last is not None:
        (sent,) = pick_rows([picked[last]], scaled, (pieces[groups[0][-1]],))
        pieces[last] = swap(sent, "exp", last)
    hiddens, after = [], rest[3:]
    for group in groups:
        parts = gather_parts(join([pieces[mask] for mask in group], after), 0)
        after = tuple(part for mask, _, part in parts if mask in (2, 4))
        hiddens.append(hidden_units(me, parts, one_over_gain, expert_gate[0], expert_up[0]))
    parts = {mask: part for mask, _, part in gather_parts(join(hiddens))}
    answer = down(
        [parts[mask] for mask in range(ctx_count)],
        [down_parts[mask] for mask in range(ctx_count)],
    )
    answers = {}
    for place, mask in enumerate(mask for group in groups for mask in group):
        piece = lax.slice_in_dim(answer, place * capacity, (place + 1) * capacity, axis=0)
        answers[mask] = piece if mask == 0 else swap(piece, "exp", mask)
    block_out = combine(
        mixer_out,
        jnp.stack(picked),
        jnp.stack(gates),
        [answers[mask] for mask in range(exp_count)],
    )
    return (mixer_out, block_out)


def solution(mesh):
    placed = (
        P("ctx", "exp"),
        P("ctx", "exp"),
        P("ctx", "exp"),
        P(None, "ctx"),
        P(None, "ctx"),
        P(None, "exp"),
        P("exp"),
        P("exp"),
        P(None, "exp"),
        P("exp"),
        P(None, "exp"),
        P(None, "exp"),
        P("exp", "ctx"),
        P("exp", "ctx"),
        P("ctx"),
        P("exp", None, "ctx"),
        P("exp", None, "ctx"),
        P("exp", "ctx", None),
        P("exp", None),
        P("exp", None),
    )
    return jax.shard_map(
        shards,
        mesh=mesh,
        in_specs=placed,
        out_specs=(P("exp", "ctx"), P("exp", "ctx")),
        check_vma=False,
    )
```

```python
import functools

import jax
import jax.numpy as jnp
from jax import lax
from jax.experimental import pallas as pl
from jax.experimental.pallas import tpu as pltpu
from jax.sharding import PartitionSpec as P

D = 8192
LOG2E = 1.4426950408889634
LANES = 128
MIB = 1 << 20


def from_behind(array, axis, by):
    length = lax.axis_size(axis)
    pairs = [(i, i + by) for i in range(length) if 0 <= i + by < length]
    return lax.ppermute(array, axis, pairs)


def swap(array, axis, mask):
    return lax.ppermute(array, axis, [(i, i ^ mask) for i in range(lax.axis_size(axis))])


def halves_kernel(split_dim, first, second, low, high):
    half = low.shape[split_dim]
    if split_dim == 0:
        low[...] = first[0:half, :]
        high[...] = second[half:, :]
    else:
        low[...] = first[:, 0:half]
        high[...] = second[:, half:]


def halves(first, second, split_dim, after=()):
    shape = list(first.shape)
    shape[split_dim] //= 2
    whole = pl.BlockSpec(first.shape, lambda j: (0, 0))
    part = pl.BlockSpec(tuple(shape), lambda j: (0, 0))
    return launch(
        functools.partial(halves_kernel, split_dim),
        [],
        [first, second],
        [whole, whole],
        [part, part],
        [jax.ShapeDtypeStruct(tuple(shape), first.dtype)] * 2,
        after=after,
        limit=56,
        cost_estimate=cost(0, 6 * first.size),
        name="halves",
    )


def gather_parts(array, split_dim=None, after=()):
    count = lax.axis_size("ctx")
    if count != 8:
        return [(0, None, array)] + [(m, None, swap(array, "ctx", m)) for m in range(1, count)]
    over_a = swap(array, "ctx", 2)
    over_b = swap(array, "ctx", 4)
    if split_dim is None:
        crossed = [(6, None, swap(array, "ctx", 6))]
    else:
        low, high = halves(over_a, over_b, split_dim, after)
        crossed = [(6, 0, swap(low, "ctx", 4)), (6, 1, swap(high, "ctx", 2))]
    parts = []
    for mask, which, part in [(0, None, array), (2, None, over_a), (4, None, over_b)] + crossed:
        parts.append((mask, which, part))
        parts.append((mask + 1, which, swap(part, "ctx", 1)))
    return parts


def silu(value):
    return value / (1.0 + jnp.exp(-value))


def cost(flops, moved, transcendentals=0):
    return pl.CostEstimate(
        flops=int(flops), bytes_accessed=int(moved), transcendentals=int(transcendentals)
    )


ANY = pl.BlockSpec(memory_space=pl.ANY)


def launch(
    kernel, scalars, operands, in_specs, out_specs, out_shape, after=(), grid=(1,), scratch=(),
    limit=56, **rest
):
    taken = len(scalars) + len(operands)

    def body(*refs):
        kernel(*refs[:taken], *refs[taken + len(after) :])

    return pl.pallas_call(
        body,
        grid_spec=pltpu.PrefetchScalarGridSpec(
            num_scalar_prefetch=len(scalars),
            grid=grid,
            in_specs=list(in_specs) + [ANY] * len(after),
            out_specs=out_specs,
            scratch_shapes=list(scratch),
        ),
        out_shape=out_shape,
        compiler_params=pltpu.CompilerParams(vmem_limit_bytes=limit * MIB),
        **rest,
    )(*scalars, *operands, *after)


def cut_kernel(count, *refs):
    for source, out in zip(refs[-2 * count : -count], refs[-count:]):
        out[...] = source[...]


def cut_columns(me, rows, width, masks, after=()):
    step = rows.shape[0] // 3

    def block(mask):
        return pl.BlockSpec((step, width), lambda i, me: (i, me[0] ^ mask))

    return launch(
        functools.partial(cut_kernel, len(masks)),
        [me],
        [rows] * len(masks),
        [block(mask) for mask in masks],
        [pl.BlockSpec((step, width), lambda i, me: (i, 0))] * len(masks),
        [jax.ShapeDtypeStruct((rows.shape[0], width), rows.dtype)] * len(masks),
        after=after,
        grid=(3,),
        cost_estimate=cost(0, 4 * rows.shape[0] * width * len(masks)),
        name="cut_columns",
    )


def join_kernel(count, *refs):
    pieces, out, sems = refs[:count], refs[count], refs[count + 1]
    copies, row = [], 0
    for place, piece in enumerate(pieces):
        copies.append(
            pltpu.make_async_copy(piece, out.at[pl.ds(row, piece.shape[0]), :], sems.at[place])
        )
        row += piece.shape[0]
    for copy in copies:
        copy.start()
    for copy in copies:
        copy.wait()


def join(pieces, after=()):
    rows = sum(piece.shape[0] for piece in pieces)
    columns = pieces[0].shape[1]
    return launch(
        functools.partial(join_kernel, len(pieces)),
        [],
        list(pieces),
        [ANY] * len(pieces),
        pl.BlockSpec((rows, columns), lambda j: (0, 0)),
        jax.ShapeDtypeStruct((rows, columns), pieces[0].dtype),
        after=after,
        scratch=[pltpu.SemaphoreType.DMA((len(pieces),))],
        limit=56,
        cost_estimate=cost(0, 4 * rows * columns),
        name="join",
    )


BLOCK = 512


def by_blocks(kernel, split, *refs):
    width = next(ref for ref, cut in zip(refs, split) if cut).shape[1]

    def one(index, _):
        lanes = pl.ds(pl.multiple_of(index * BLOCK, BLOCK), BLOCK)
        kernel(*[ref.at[:, lanes] if cut else ref for ref, cut in zip(refs, split)])
        return 0

    lax.fori_loop(0, width // BLOCK, one, 0)


GROUP = 16
STATE_ROWS = 32


def state_kernel(
    mixer, rim, delta, kernel, bias, delta_bias, decay_log, extra, b_wide, step_out, conv_out,
    end_out, padded,
):
    tokens, width = mixer.shape
    blocks = width // LANES
    padded[0:8, :] = rim[...]
    padded[8:, :] = mixer[...].astype(jnp.float32)
    rate = [
        -jnp.exp(decay_log[:, k * LANES : (k + 1) * LANES]) * LOG2E for k in range(blocks)
    ]
    taps = kernel.shape[0]

    def group(index, carry):
        states, total = carry
        base = pl.multiple_of(index * GROUP, GROUP)
        window = padded[pl.ds(base, GROUP + 8), :]
        convolved = bias[...] + sum(
            kernel[k : k + 1, :] * window[9 - taps + k : 9 - taps + k + GROUP, :]
            for k in range(taps)
        )
        conv_act = silu(convolved)
        step = jnp.log(
            1.0 + jnp.exp(delta[pl.ds(base, GROUP), :].astype(jnp.float32) + delta_bias[...])
        )
        step_out[pl.ds(base, GROUP), :] = step
        conv_out[pl.ds(base, GROUP), :] = conv_act
        drive = step * conv_act
        states = list(states)
        for i in range(GROUP):
            b_tile = b_wide[pl.ds(pl.multiple_of((base + i) * 16, 16), 16), :]
            for k in range(blocks):
                lanes = slice(k * LANES, (k + 1) * LANES)
                states[k] = (
                    jnp.exp2(step[i : i + 1, lanes] * rate[k]) * states[k]
                    + b_tile * drive[i : i + 1, lanes]
                )
        return tuple(states), total + step[0:8, :] + step[8:16, :]

    start = tuple(jnp.zeros((16, LANES), jnp.float32) for _ in range(blocks))
    states, total = lax.fori_loop(
        0, tokens // GROUP, group, (start, jnp.zeros((8, width), jnp.float32))
    )
    for k in range(blocks):
        end_out[0:16, k * LANES : (k + 1) * LANES] = states[k].astype(end_out.dtype)
    total = jnp.sum(total, axis=0, keepdims=True)
    place = lax.broadcasted_iota(jnp.int32, (16, width), 0)
    pieces = jnp.where(place == 3, extra[...], 0.0)
    for row in range(3):
        piece = total.astype(jnp.bfloat16).astype(jnp.float32)
        pieces = jnp.where(place == row, piece, pieces)
        total = total - piece
    end_out[16:32, :] = pieces.astype(end_out.dtype)


def local_states(mixer_in, rim8, delta_in, kernel, bias, delta_bias, decay_log, extra, b_wide):
    tokens, channels = mixer_in.shape
    width = 1024
    rows = lambda n: pl.BlockSpec((n, width), lambda j: (0, j))
    return launch(
        functools.partial(by_blocks, state_kernel, [1] * 8 + [0] + [1] * 3 + [0]),
        [],
        [mixer_in, rim8, delta_in, kernel, bias, delta_bias, decay_log, extra, b_wide],
        [
            rows(tokens),
            rows(8),
            rows(tokens),
            rows(kernel.shape[0]),
            rows(1),
            rows(1),
            rows(16),
            rows(1),
            pl.BlockSpec((tokens * 16, LANES), lambda j: (0, 0)),
        ],
        [rows(tokens), rows(tokens), rows(STATE_ROWS)],
        [
            jax.ShapeDtypeStruct((tokens, channels), jnp.float32),
            jax.ShapeDtypeStruct((tokens, channels), jnp.float32),
            jax.ShapeDtypeStruct((STATE_ROWS, channels), jnp.bfloat16),
        ],
        grid=(channels // width,),
        scratch=[pltpu.VMEM((tokens + 8, BLOCK), jnp.float32)],
        cost_estimate=cost(
            tokens * channels * 16 * 5, tokens * channels * 12, tokens * channels * 18
        ),
        name="local_states",
    )


def gains_kernel(masks, me, *refs):
    parts, out = refs[: len(masks)], refs[-1]
    width = out.shape[2]
    for mask, part in zip(masks, parts):
        row = part[...].astype(jnp.float32)[3:4, :]
        gain = row[:, 0:width] + row[:, width : 2 * width] + row[:, 2 * width : 3 * width]
        out[me[0] ^ mask] = 1.0 / gain


def inverse_gains(me, ends, width):
    return launch(
        functools.partial(gains_kernel, [mask for mask, _, _ in ends]),
        [me],
        [end for _, _, end in ends],
        [pl.BlockSpec((16, 3 * width), lambda j, me: (1, 0))] * len(ends),
        pl.BlockSpec((len(ends), 1, width), lambda j, me: (0, 0, 0)),
        jax.ShapeDtypeStruct((len(ends), 1, width), jnp.float32),
        limit=56,
        name="inverse_gains",
    )


def fold_rows(tiles):
    place = lax.broadcasted_iota(jnp.int32, (8, LANES), 0)
    for shift in (1, 2, 4):
        first = (place & shift) == 0
        tiles = [
            jnp.where(first, a, b) + pltpu.roll(jnp.where(first, b, a), shift, 0)
            for a, b in zip(tiles[0::2], tiles[1::2])
        ]
    return tiles[0]


def readout_kernel(
    masks, me, step_in, conv_in, gate_in, decay_log, skip, b_wide, c_wide, entering, *refs
):
    ends = refs[: len(masks)]
    gated, leaving, scanned = refs[len(masks) : len(masks) + 3]
    tokens, width = step_in.shape
    blocks = width // LANES
    rate = [
        -jnp.exp(decay_log[:, k * LANES : (k + 1) * LANES]) * LOG2E for k in range(blocks)
    ]
    start = [entering[:, k * LANES : (k + 1) * LANES] for k in range(blocks)]
    if masks:
        held = refs[-1]
        for mask, end in zip(masks, ends):
            held[mask] = end[...].astype(jnp.float32)
        for owner in range(len(masks) - 1):
            end = held[me[0] ^ owner]
            total = end[16:17, :] + end[17:18, :] + end[18:19, :]
            for k in range(blocks):
                lanes = slice(k * LANES, (k + 1) * LANES)
                later = jnp.exp2(total[:, lanes] * rate[k]) * start[k] + end[0:16, lanes]
                start[k] = jnp.where(owner < me[0], later, start[k])

    def group(index, states):
        base = pl.multiple_of(index * GROUP, GROUP)
        step = step_in[pl.ds(base, GROUP), :]
        conv_act = conv_in[pl.ds(base, GROUP), :]
        drive = step * conv_act
        states = list(states)
        for half in range(GROUP // 8):
            tiles = [[] for _ in range(blocks)]
            for i in range(half * 8, half * 8 + 8):
                spot = pl.ds(pl.multiple_of((base + i) * 16, 16), 16)
                b_tile = b_wide[spot, :]
                c_tile = c_wide[spot, :]
                for k in range(blocks):
                    lanes = slice(k * LANES, (k + 1) * LANES)
                    states[k] = (
                        jnp.exp2(step[i : i + 1, lanes] * rate[k]) * states[k]
                        + b_tile * drive[i : i + 1, lanes]
                    )
                    read = c_tile * states[k]
                    tiles[k].append(read[0:8] + read[8:16])
            for k in range(blocks):
                scanned[
                    pl.ds(pl.multiple_of(base + half * 8, 8), 8), k * LANES : (k + 1) * LANES
                ] = fold_rows(tiles[k])
        gate = gate_in[pl.ds(base, GROUP), :].astype(jnp.float32)
        mixed = scanned[pl.ds(base, GROUP), :] + skip[...] * conv_act
        gated[pl.ds(base, GROUP), :] = (mixed * silu(gate)).astype(gated.dtype)
        return tuple(states)

    states = lax.fori_loop(0, tokens // GROUP, group, tuple(start))
    for k in range(blocks):
        leaving[:, k * LANES : (k + 1) * LANES] = states[k]


def read_out(
    me, chunk, chunks, step, conv_act, gate_in, decay_log, skip, b_wide, c_wide, entering, ends,
    after=(),
):
    tokens, channels = step.shape
    tokens = tokens // chunks
    width = 1024
    some = pl.BlockSpec((tokens, width), lambda j, me: (chunk, j))
    rows = lambda n: pl.BlockSpec((n, width), lambda j, me: (0, j))
    wide = pl.BlockSpec((tokens * 16, LANES), lambda j, me: (chunk, 0))
    masks = [mask for mask, _, _ in ends]
    scratch = [pltpu.VMEM((tokens, BLOCK), jnp.float32)]
    if ends:
        scratch.append(pltpu.VMEM((len(ends), STATE_ROWS, BLOCK), jnp.float32))
    split = [0] + [1] * 5 + [0, 0, 1] + [1] * len(ends) + [1, 1] + [0] * len(scratch)
    return launch(
        functools.partial(by_blocks, functools.partial(readout_kernel, masks), split),
        [me],
        [step, conv_act, gate_in, decay_log, skip, b_wide, c_wide, entering]
        + [end for _, _, end in ends],
        [some, some, some, rows(16), rows(1), wide, wide, rows(16)]
        + [rows(STATE_ROWS)] * len(ends),
        [rows(tokens), rows(16)],
        [
            jax.ShapeDtypeStruct((tokens, channels), jnp.bfloat16),
            jax.ShapeDtypeStruct((16, channels), jnp.float32),
        ],
        after=after,
        grid=(channels // width,),
        scratch=scratch,
        cost_estimate=cost(
            tokens * channels * 16 * 7, tokens * channels * 12, tokens * channels * 18
        ),
        name="read_out",
    )


def project_kernel(layout, me, weight, *refs):
    parts, (out, held, sems) = refs[: len(layout)], refs[len(layout) :]
    rows = held.shape[0] // (1 + max(mask for mask, _ in layout))

    @pl.when(pl.program_id(0) == 0)
    def _():
        copies = []
        for place, (mask, column) in enumerate(layout):
            part = parts[place]
            owner = me[0] ^ mask
            copies.append(
                pltpu.make_async_copy(
                    part,
                    held.at[
                        pl.ds(pl.multiple_of(owner * rows, rows), rows),
                        pl.ds(column, part.shape[1]),
                    ],
                    sems.at[place],
                )
            )
        for copy in copies:
            copy.start()
        for copy in copies:
            copy.wait()

    out[...] = jnp.dot(held[...], weight[...], preferred_element_type=jnp.float32).astype(
        out.dtype
    )


def project(me, parts, weight, after=()):
    depth, columns = weight.shape
    rows = parts[0][2].shape[0]
    total = rows * lax.axis_size("ctx")
    layout = [(mask, (which or 0) * depth // 2) for mask, which, _ in parts]
    tile = min(256, columns)
    return launch(
        functools.partial(project_kernel, layout),
        [me],
        [weight] + [part for _, _, part in parts],
        [pl.BlockSpec((depth, tile), lambda j, me: (0, j))] + [ANY] * len(parts),
        pl.BlockSpec((total, tile), lambda j, me: (0, j)),
        jax.ShapeDtypeStruct((total, columns), jnp.bfloat16),
        after=after,
        grid=(columns // tile,),
        scratch=[
            pltpu.VMEM((total, depth), jnp.bfloat16),
            pltpu.SemaphoreType.DMA((len(parts),)),
        ],
        limit=56,
        cost_estimate=cost(
            2 * total * depth * columns, 2 * (total * depth + depth * columns + total * columns)
        ),
        name="project",
    )


def hidden_kernel(layout, me, gain, gate_rows, up_rows, *refs):
    parts, (out, held, total, squares, sems) = refs[: len(layout)], refs[len(layout) :]
    turn = pl.program_id(0)

    def copy_of(place):
        mask, row = layout[place]
        part = parts[place]
        column = ((me[0] ^ mask) & 1) * part.shape[1]
        return pltpu.make_async_copy(
            part,
            held.at[
                mask // 2,
                pl.ds(row, part.shape[0]),
                pl.ds(pl.multiple_of(column, LANES), part.shape[1]),
            ],
            sems.at[place],
        )

    @pl.when(turn == 0)
    def _():
        for place in range(len(layout)):
            copy_of(place).start()
        total[...] = jnp.zeros_like(total)
        squares[...] = jnp.zeros_like(squares)

    for place, (mask, _) in enumerate(layout):

        @pl.when(turn == mask // 2)
        def _():
            copy_of(place).wait()

    width = out.shape[1]
    both = jnp.concatenate([gate_rows[...], up_rows[...]], axis=1)
    total[...] += jnp.dot(held[turn], both, preferred_element_type=jnp.float32)
    slots = out.shape[0]
    for row in range(0, slots, 64):
        mixer_square = squares[row : row + 64, :]
        for lane in range(0, held.shape[2], LANES):
            value = held[turn, row : row + 64, lane : lane + LANES].astype(jnp.float32)
            spot = lane % gain.shape[2]
            value = value * gain[lane // gain.shape[2], :, spot : spot + LANES]
            mixer_square += value * value
        squares[row : row + 64, :] = mixer_square

    @pl.when(turn == pl.num_programs(0) - 1)
    def _():
        def finish(index, _):
            spot = pl.ds(pl.multiple_of(index * 64, 64), 64)
            mean = jnp.sum(squares[spot, :], axis=1, keepdims=True) / D
            factor = lax.rsqrt(mean + 1e-05)
            gate_act = total[spot, 0:width] * factor
            up_act = total[spot, width:] * factor
            out[spot, :] = (silu(gate_act) * up_act).astype(out.dtype)
            return 0

        lax.fori_loop(0, out.shape[0] // 64, finish, 0)


def hidden_units(me, parts, one_over_gain, gate, up, after=()):
    slots, depth = parts[0][2].shape
    count = lax.axis_size("ctx")
    width = gate.shape[1]
    layout = [(mask, (which or 0) * slots // 2) for mask, which, _ in parts]
    block = pl.BlockSpec((2 * depth, width), lambda k, me: ((me[0] // 2) ^ k, 0))
    return launch(
        functools.partial(hidden_kernel, layout),
        [me],
        [one_over_gain, gate, up] + [part for _, _, part in parts],
        [
            pl.BlockSpec((2, 1, depth), lambda k, me: ((me[0] // 2) ^ k, 0, 0)),
            block,
            block,
        ] + [ANY] * len(parts),
        pl.BlockSpec((slots, width), lambda k, me: (0, 0)),
        jax.ShapeDtypeStruct((slots, width), jnp.bfloat16),
        after=after,
        grid=(count // 2,),
        scratch=[
            pltpu.VMEM((count // 2, slots, 2 * depth), jnp.bfloat16),
            pltpu.VMEM((slots, 2 * width), jnp.float32),
            pltpu.VMEM((slots, LANES), jnp.float32),
            pltpu.SemaphoreType.DMA((len(parts),)),
        ],
        limit=56,
        cost_estimate=cost(
            4 * slots * depth * count * width, 2 * count * depth * (slots + 2 * width)
        ),
        name="hidden_units",
    )


def down_kernel(layout, me, *refs):
    count = len(layout)
    units, weights, (out, held, sems) = refs[:count], refs[count:-3], refs[-3:]
    slots, width = held.shape[0], weights[0].shape[0]
    rows = slots * len(weights) // count

    @pl.when(pl.program_id(0) == 0)
    def _():
        copies = []
        for place, (mask, begin, row) in enumerate(layout):
            copies.append(
                pltpu.make_async_copy(
                    units[place].at[pl.ds(begin, rows), :],
                    held.at[pl.ds(row, rows), pl.ds(mask * width, width)],
                    sems.at[place],
                )
            )
        for copy in copies:
            copy.start()
        for copy in copies:
            copy.wait()

    tall = jnp.concatenate([weight[...] for weight in weights], axis=0)
    out[...] = jnp.dot(held[...], tall, preferred_element_type=jnp.float32).astype(out.dtype)


def down(me, segments, rows, weights, own, after=()):
    columns = weights[-1].shape[1]
    width = own.shape[0]
    depth = width * len(weights)
    slots = rows * len(segments)
    tile = min(256, columns)
    layout, units = [], []
    for place, (parts, begin) in enumerate(segments):
        for mask, part in enumerate(parts):
            layout.append((mask, begin, place * rows))
            units.append(part)
    steps = columns // tile
    return launch(
        functools.partial(down_kernel, layout),
        [me],
        units + [own] + list(weights[1:]),
        [ANY] * len(units)
        + [pl.BlockSpec((width, tile), lambda j, me: (0, me[0] * steps + j))]
        + [pl.BlockSpec((width, tile), lambda j, me: (0, j))] * (len(weights) - 1),
        pl.BlockSpec((slots, tile), lambda j, me: (0, j)),
        jax.ShapeDtypeStruct((slots, columns), jnp.bfloat16),
        after=after,
        grid=(steps,),
        scratch=[
            pltpu.VMEM((slots, depth), jnp.bfloat16),
            pltpu.SemaphoreType.DMA((len(units),)),
        ],
        limit=56,
        cost_estimate=cost(
            2 * slots * depth * columns, 2 * (slots * depth + depth * columns + slots * columns)
        ),
        name="down",
    )


def pick_kernel(count, rows, *refs):
    for picks, out in zip(refs[:count], refs[count:]):
        out[...] = lax.dot_general(
            picks[...], rows[...], (((0,), (0,)), ((), ())), preferred_element_type=jnp.float32
        ).astype(out.dtype)


def pick_rows(picks, rows, after=()):
    shape = (picks[0].shape[1], rows.shape[1])
    whole = lambda shape: pl.BlockSpec(shape, lambda j: (0, 0))
    return launch(
        functools.partial(pick_kernel, len(picks)),
        [],
        [rows] + list(picks),
        [whole(rows.shape)] + [whole(pick.shape) for pick in picks],
        [whole(shape)] * len(picks),
        [jax.ShapeDtypeStruct(shape, rows.dtype)] * len(picks),
        after=after,
        limit=56,
        cost_estimate=cost(2 * rows.size * shape[0] * len(picks), 4 * rows.size),
        name="pick_rows",
    )


def combine_kernel(me, mixer, ids, gates, *refs):
    out = refs[-1]
    count = len(refs) // 2
    total = mixer[...].astype(jnp.float32)
    for mask in range(count):
        named = ids[...] == (me[0] ^ mask)
        gate = jnp.sum(jnp.where(named, gates[...], 0.0), axis=1, keepdims=True)
        total += gate * jnp.dot(
            refs[mask][...], refs[count + mask][...], preferred_element_type=jnp.float32
        )
    out[...] = total.astype(out.dtype)


def combine(me, mixer_out, ids, gates, picks, answers):
    operands = [mixer_out, ids, gates] + list(picks) + list(answers)
    return launch(
        combine_kernel,
        [me],
        operands,
        [pl.BlockSpec(array.shape, lambda j, me: (0, 0)) for array in operands],
        pl.BlockSpec(mixer_out.shape, lambda j, me: (0, 0)),
        jax.ShapeDtypeStruct(mixer_out.shape, jnp.bfloat16),
        cost_estimate=cost(
            2 * mixer_out.size * answers[0].shape[0] * len(answers), 4 * mixer_out.size
        ),
        name="combine",
    )


def shards(
    mixer_in,
    gate_in,
    delta_in,
    b_proj,
    c_proj,
    conv_kernel,
    conv_bias,
    delta_bias,
    decay_log,
    skip_gain,
    prefix_state,
    prefix_tail,
    out_proj,
    residual,
    norm_gain,
    expert_gate,
    expert_up,
    expert_down,
    expert_ids,
    route_gates,
):
    tokens = mixer_in.shape[0]
    rim = prefix_tail.shape[0]
    ctx_count = lax.axis_size("ctx")
    exp_count = lax.axis_size("exp")
    ctx_me = lax.axis_index("ctx")
    exp_me = lax.axis_index("exp")
    me = ctx_me.astype(jnp.int32).reshape(1)

    rim_rows = from_behind(mixer_in[tokens - rim :], "ctx", 1)
    rim_rows = jnp.where(ctx_me == 0, prefix_tail, rim_rows).astype(jnp.float32)
    rim8 = jnp.pad(rim_rows, ((8 - rim, 0), (0, 0)))

    width = out_proj.shape[1]
    down_rows = expert_down[0]
    down_parts = {}

    def send_columns(masks, after=()):
        for mask, cut in zip(masks, cut_columns(me, down_rows, width, masks, after)):
            down_parts[mask] = cut if mask == 0 else swap(cut, "ctx", mask)
        return tuple(down_parts[mask] for mask in masks)

    early = send_columns([2, 4, 3, 5])

    extra, left = [], norm_gain
    for _ in range(3):
        extra.append(lax.reduce_precision(left, 8, 7))
        left = left - extra[-1]
    extra = jnp.concatenate(extra)
    extra = jnp.pad(extra, (0, mixer_in.shape[1] - extra.shape[0]))[None, :]

    wide = lambda proj: jnp.broadcast_to(proj.T[:, :, None], (tokens, 16, LANES)).reshape(
        tokens * 16, LANES
    )
    b_wide, c_wide = wide(b_proj), wide(c_proj)
    step, conv_act, end = local_states(
        mixer_in,
        rim8,
        delta_in,
        conv_kernel,
        conv_bias[None, :],
        delta_bias[None, :],
        decay_log,
        extra,
        b_wide,
    )
    chunks = 2
    state, ends = prefix_state, gather_parts(join([end], early[:2]))
    one_over_gain = inverse_gains(me, ends, width)
    gated = []
    for chunk in range(chunks):
        rows, state = read_out(
            me,
            chunk,
            chunks,
            step,
            conv_act,
            gate_in,
            decay_log,
            skip_gain[None, :],
            b_wide,
            c_wide,
            state,
            ends,
            early[2:],
        )
        ends = []
        gated.append(rows)
    near = lambda parts: [part for mask, _, part in parts if mask in (2, 4)]
    far = lambda parts: [part for mask, which, part in parts if which is not None][::2]
    scatter = lambda rows: lax.psum_scatter(rows, "exp", scatter_dimension=0, tiled=True)
    front = gather_parts(gated[0], 1, gated[1:])
    back = gather_parts(gated[1], 1, far(front))
    partial = project(me, front, out_proj, near(back))
    projected = [scatter(partial)]
    (middle,) = send_columns([6], far(front))
    partial = project(me, back, out_proj, [partial, middle])
    projected.append(scatter(partial))
    late = send_columns([7, 1] + list(range(8, ctx_count)), [partial])

    block_rows = residual.shape[0]
    owners = block_rows // tokens
    projected = jnp.stack(
        [piece.reshape(owners, tokens // chunks, width) for piece in projected], axis=1
    ).reshape(block_rows, width)
    mixer_out = (residual.astype(jnp.float32) + projected.astype(jnp.float32)).astype(
        jnp.bfloat16
    )
    mixer_wide = mixer_out.astype(jnp.float32)
    scaled = (mixer_wide * norm_gain[None, :]).astype(jnp.bfloat16)
    experts = expert_gate.shape[0] * exp_count
    capacity = 3 * block_rows * expert_ids.shape[1] // (2 * experts)
    spots = jnp.arange(capacity, dtype=jnp.int32)
    picked = []
    for mask in range(exp_count):
        here = jnp.any(expert_ids == (exp_me ^ mask), axis=1)
        place = jnp.cumsum(here.astype(jnp.int32)) - 1
        pick = here[:, None] & (place[:, None] == spots[None, :])
        picked.append(pick.astype(jnp.bfloat16))

    groups = [[0, 2], [1, 3]] if exp_count == 4 else [list(range(exp_count))]
    last = groups[-1][-1] if len(groups) > 1 else None
    masks = [mask for mask in range(exp_count) if mask != last][::-1]
    rows = dict(zip(masks, pick_rows([picked[mask] for mask in masks], scaled, late[:1])))
    pieces = {mask: swap(rows[mask], "exp", mask) for mask in masks if mask != 0}
    pieces[0] = rows[0]
    if last is not None:
        (sent,) = pick_rows([picked[last]], scaled, (pieces[groups[0][-1]],))
        pieces[last] = swap(sent, "exp", last)
    segments, after, order = {}, late[1:], ()
    for group in groups:
        parts = gather_parts(join([pieces[mask] for mask in group], after), 0, order)
        after = near(parts)
        hidden = hidden_units(me, parts, one_over_gain, expert_gate[0], expert_up[0])
        order = [hidden]
        units = {mask: part for mask, _, part in gather_parts(hidden)}
        for place, mask in enumerate(group):
            segments[mask] = ([units[m] for m in range(ctx_count)], place * capacity)
    answers = {}
    weights = [None] + [down_parts[mask] for mask in range(1, ctx_count)]
    order = ()
    for group in [list(range(1, exp_count))[::-1], [0]]:
        answer = down(
            me, [segments[mask] for mask in group], capacity, weights, down_rows, order
        )
        order = [answer]
        for place, mask in enumerate(group):
            piece = lax.slice_in_dim(answer, place * capacity, (place + 1) * capacity, axis=0)
            answers[mask] = piece if mask == 0 else swap(piece, "exp", mask)
    block_out = combine(
        exp_me.astype(jnp.int32).reshape(1),
        mixer_out,
        expert_ids,
        route_gates,
        picked,
        [answers[mask] for mask in range(exp_count)],
    )
    return (mixer_out, block_out)


def solution(mesh):
    placed = (
        P("ctx", "exp"),
        P("ctx", "exp"),
        P("ctx", "exp"),
        P(None, "ctx"),
        P(None, "ctx"),
        P(None, "exp"),
        P("exp"),
        P("exp"),
        P(None, "exp"),
        P("exp"),
        P(None, "exp"),
        P(None, "exp"),
        P("exp", "ctx"),
        P("exp", "ctx"),
        P("ctx"),
        P("exp", None, "ctx"),
        P("exp", None, "ctx"),
        P("exp", "ctx", None),
        P("exp", None),
        P("exp", None),
    )
    return jax.shard_map(
        shards,
        mesh=mesh,
        in_specs=placed,
        out_specs=(P("exp", "ctx"), P("exp", "ctx")),
        check_vma=False,
    )
```

```python
import functools

import jax
import jax.numpy as jnp
from jax import lax
from jax.experimental import pallas as pl
from jax.experimental.pallas import tpu as pltpu
from jax.sharding import PartitionSpec as P

D = 8192
LOG2E = 1.4426950408889634
LANES = 128
MIB = 1 << 20


def from_behind(array, axis, by):
    length = lax.axis_size(axis)
    pairs = [(i, i + by) for i in range(length) if 0 <= i + by < length]
    return lax.ppermute(array, axis, pairs)


def swap(array, axis, mask):
    return lax.ppermute(array, axis, [(i, i ^ mask) for i in range(lax.axis_size(axis))])


def halves_kernel(split_dim, first, second, low, high):
    half = low.shape[split_dim]
    if split_dim == 0:
        low[...] = first[0:half, :]
        high[...] = second[half:, :]
    else:
        low[...] = first[:, 0:half]
        high[...] = second[:, half:]


def halves(first, second, split_dim, after=()):
    shape = list(first.shape)
    shape[split_dim] //= 2
    whole = pl.BlockSpec(first.shape, lambda j: (0, 0))
    part = pl.BlockSpec(tuple(shape), lambda j: (0, 0))
    return launch(
        functools.partial(halves_kernel, split_dim),
        [],
        [first, second],
        [whole, whole],
        [part, part],
        [jax.ShapeDtypeStruct(tuple(shape), first.dtype)] * 2,
        after=after,
        limit=16,
        cost_estimate=cost(0, 6 * first.size),
        name="halves",
    )


def gather_parts(array, split_dim=None, after=()):
    count = lax.axis_size("ctx")
    if count != 8:
        return [(0, None, array)] + [(m, None, swap(array, "ctx", m)) for m in range(1, count)]
    over_a = swap(array, "ctx", 2)
    over_b = swap(array, "ctx", 4)
    if split_dim is None:
        crossed = [(6, None, swap(array, "ctx", 6))]
    else:
        low, high = halves(over_a, over_b, split_dim, after)
        crossed = [(6, 0, swap(low, "ctx", 4)), (6, 1, swap(high, "ctx", 2))]
    parts = []
    for mask, which, part in [(0, None, array), (2, None, over_a), (4, None, over_b)] + crossed:
        parts.append((mask, which, part))
        parts.append((mask + 1, which, swap(part, "ctx", 1)))
    return parts


def silu(value):
    return value / (1.0 + jnp.exp(-value))


def cost(flops, moved, transcendentals=0):
    return pl.CostEstimate(
        flops=int(flops), bytes_accessed=int(moved), transcendentals=int(transcendentals)
    )


ANY = pl.BlockSpec(memory_space=pl.ANY)


def launch(
    kernel, scalars, operands, in_specs, out_specs, out_shape, after=(), grid=(1,), scratch=(),
    limit=56, **rest
):
    taken = len(scalars) + len(operands)

    def body(*refs):
        kernel(*refs[:taken], *refs[taken + len(after) :])

    return pl.pallas_call(
        body,
        grid_spec=pltpu.PrefetchScalarGridSpec(
            num_scalar_prefetch=len(scalars),
            grid=grid,
            in_specs=list(in_specs) + [ANY] * len(after),
            out_specs=out_specs,
            scratch_shapes=list(scratch),
        ),
        out_shape=out_shape,
        compiler_params=pltpu.CompilerParams(vmem_limit_bytes=limit * MIB),
        **rest,
    )(*scalars, *operands, *after)


def cut_kernel(count, *refs):
    for source, out in zip(refs[-2 * count : -count], refs[-count:]):
        out[...] = source[...]


def cut_columns(me, rows, width, masks, after=()):
    step = rows.shape[0] // 3

    def block(mask):
        return pl.BlockSpec((step, width), lambda i, me: (i, me[0] ^ mask))

    return launch(
        functools.partial(cut_kernel, len(masks)),
        [me],
        [rows] * len(masks),
        [block(mask) for mask in masks],
        [pl.BlockSpec((step, width), lambda i, me: (i, 0))] * len(masks),
        [jax.ShapeDtypeStruct((rows.shape[0], width), rows.dtype)] * len(masks),
        after=after,
        grid=(3,),
        cost_estimate=cost(0, 4 * rows.shape[0] * width * len(masks)),
        name="cut_columns",
    )


def join_kernel(count, *refs):
    pieces, out, sems = refs[:count], refs[count], refs[count + 1]
    copies, row = [], 0
    for place, piece in enumerate(pieces):
        copies.append(
            pltpu.make_async_copy(piece, out.at[pl.ds(row, piece.shape[0]), :], sems.at[place])
        )
        row += piece.shape[0]
    for copy in copies:
        copy.start()
    for copy in copies:
        copy.wait()


def join(pieces, after=()):
    rows = sum(piece.shape[0] for piece in pieces)
    columns = pieces[0].shape[1]
    return launch(
        functools.partial(join_kernel, len(pieces)),
        [],
        list(pieces),
        [ANY] * len(pieces),
        pl.BlockSpec((rows, columns), lambda j: (0, 0)),
        jax.ShapeDtypeStruct((rows, columns), pieces[0].dtype),
        after=after,
        scratch=[pltpu.SemaphoreType.DMA((len(pieces),))],
        limit=16,
        cost_estimate=cost(0, 4 * rows * columns),
        name="join",
    )


BLOCK = 512


def by_blocks(kernel, split, *refs):
    width = next(ref for ref, cut in zip(refs, split) if cut).shape[1]

    def one(index, _):
        lanes = pl.ds(pl.multiple_of(index * BLOCK, BLOCK), BLOCK)
        kernel(*[ref.at[:, lanes] if cut else ref for ref, cut in zip(refs, split)])
        return 0

    lax.fori_loop(0, width // BLOCK, one, 0)


GROUP = 16
STATE_ROWS = 32


def state_kernel(
    mixer, rim, delta, kernel, bias, delta_bias, decay_log, extra, b_wide, step_out, conv_out,
    end_out, padded,
):
    tokens, width = mixer.shape
    blocks = width // LANES
    padded[0:8, :] = rim[...]
    padded[8:, :] = mixer[...].astype(jnp.float32)
    rate = [
        -jnp.exp(decay_log[:, k * LANES : (k + 1) * LANES]) * LOG2E for k in range(blocks)
    ]
    taps = kernel.shape[0]

    def group(index, carry):
        states, total = carry
        base = pl.multiple_of(index * GROUP, GROUP)
        window = padded[pl.ds(base, GROUP + 8), :]
        convolved = bias[...] + sum(
            kernel[k : k + 1, :] * window[9 - taps + k : 9 - taps + k + GROUP, :]
            for k in range(taps)
        )
        conv_act = silu(convolved)
        step = jnp.log(
            1.0 + jnp.exp(delta[pl.ds(base, GROUP), :].astype(jnp.float32) + delta_bias[...])
        )
        step_out[pl.ds(base, GROUP), :] = step
        conv_out[pl.ds(base, GROUP), :] = conv_act
        drive = step * conv_act
        states = list(states)
        for i in range(GROUP):
            b_tile = b_wide[pl.ds(pl.multiple_of((base + i) * 16, 16), 16), :]
            for k in range(blocks):
                lanes = slice(k * LANES, (k + 1) * LANES)
                states[k] = (
                    jnp.exp2(step[i : i + 1, lanes] * rate[k]) * states[k]
                    + b_tile * drive[i : i + 1, lanes]
                )
        return tuple(states), total + step[0:8, :] + step[8:16, :]

    start = tuple(jnp.zeros((16, LANES), jnp.float32) for _ in range(blocks))
    states, total = lax.fori_loop(
        0, tokens // GROUP, group, (start, jnp.zeros((8, width), jnp.float32))
    )
    for k in range(blocks):
        end_out[0:16, k * LANES : (k + 1) * LANES] = states[k].astype(end_out.dtype)
    total = jnp.sum(total, axis=0, keepdims=True)
    place = lax.broadcasted_iota(jnp.int32, (16, width), 0)
    pieces = jnp.where(place == 3, extra[...], 0.0)
    for row in range(3):
        piece = total.astype(jnp.bfloat16).astype(jnp.float32)
        pieces = jnp.where(place == row, piece, pieces)
        total = total - piece
    end_out[16:32, :] = pieces.astype(end_out.dtype)


def local_states(mixer_in, rim8, delta_in, kernel, bias, delta_bias, decay_log, extra, b_wide):
    tokens, channels = mixer_in.shape
    width = 1024
    rows = lambda n: pl.BlockSpec((n, width), lambda j: (0, j))
    return launch(
        functools.partial(by_blocks, state_kernel, [1] * 8 + [0] + [1] * 3 + [0]),
        [],
        [mixer_in, rim8, delta_in, kernel, bias, delta_bias, decay_log, extra, b_wide],
        [
            rows(tokens),
            rows(8),
            rows(tokens),
            rows(kernel.shape[0]),
            rows(1),
            rows(1),
            rows(16),
            rows(1),
            pl.BlockSpec((tokens * 16, LANES), lambda j: (0, 0)),
        ],
        [rows(tokens), rows(tokens), rows(STATE_ROWS)],
        [
            jax.ShapeDtypeStruct((tokens, channels), jnp.float32),
            jax.ShapeDtypeStruct((tokens, channels), jnp.float32),
            jax.ShapeDtypeStruct((STATE_ROWS, channels), jnp.bfloat16),
        ],
        grid=(channels // width,),
        scratch=[pltpu.VMEM((tokens + 8, BLOCK), jnp.float32)],
        cost_estimate=cost(
            tokens * channels * 16 * 5, tokens * channels * 12, tokens * channels * 18
        ),
        name="local_states",
    )


def gains_kernel(masks, me, *refs):
    parts, out = refs[: len(masks)], refs[-1]
    width = out.shape[2]
    for mask, part in zip(masks, parts):
        row = part[...].astype(jnp.float32)[3:4, :]
        gain = row[:, 0:width] + row[:, width : 2 * width] + row[:, 2 * width : 3 * width]
        out[me[0] ^ mask] = 1.0 / gain


def inverse_gains(me, ends, width):
    return launch(
        functools.partial(gains_kernel, [mask for mask, _, _ in ends]),
        [me],
        [end for _, _, end in ends],
        [pl.BlockSpec((16, 3 * width), lambda j, me: (1, 0))] * len(ends),
        pl.BlockSpec((len(ends), 1, width), lambda j, me: (0, 0, 0)),
        jax.ShapeDtypeStruct((len(ends), 1, width), jnp.float32),
        limit=16,
        name="inverse_gains",
    )


def fold_rows(tiles):
    place = lax.broadcasted_iota(jnp.int32, (8, LANES), 0)
    for shift in (1, 2, 4):
        first = (place & shift) == 0
        tiles = [
            jnp.where(first, a, b) + pltpu.roll(jnp.where(first, b, a), shift, 0)
            for a, b in zip(tiles[0::2], tiles[1::2])
        ]
    return tiles[0]


def readout_kernel(
    masks, me, step_in, conv_in, gate_in, decay_log, skip, b_wide, c_wide, entering, *refs
):
    ends = refs[: len(masks)]
    gated, leaving, scanned = refs[len(masks) : len(masks) + 3]
    tokens, width = step_in.shape
    blocks = width // LANES
    rate = [
        -jnp.exp(decay_log[:, k * LANES : (k + 1) * LANES]) * LOG2E for k in range(blocks)
    ]
    start = [entering[:, k * LANES : (k + 1) * LANES] for k in range(blocks)]
    if masks:
        held = refs[-1]
        for mask, end in zip(masks, ends):
            held[mask] = end[...].astype(jnp.float32)
        for owner in range(len(masks) - 1):
            end = held[me[0] ^ owner]
            total = end[16:17, :] + end[17:18, :] + end[18:19, :]
            for k in range(blocks):
                lanes = slice(k * LANES, (k + 1) * LANES)
                later = jnp.exp2(total[:, lanes] * rate[k]) * start[k] + end[0:16, lanes]
                start[k] = jnp.where(owner < me[0], later, start[k])

    def group(index, states):
        base = pl.multiple_of(index * GROUP, GROUP)
        step = step_in[pl.ds(base, GROUP), :]
        conv_act = conv_in[pl.ds(base, GROUP), :]
        drive = step * conv_act
        states = list(states)
        for half in range(GROUP // 8):
            tiles = [[] for _ in range(blocks)]
            for i in range(half * 8, half * 8 + 8):
                spot = pl.ds(pl.multiple_of((base + i) * 16, 16), 16)
                b_tile = b_wide[spot, :]
                c_tile = c_wide[spot, :]
                for k in range(blocks):
                    lanes = slice(k * LANES, (k + 1) * LANES)
                    states[k] = (
                        jnp.exp2(step[i : i + 1, lanes] * rate[k]) * states[k]
                        + b_tile * drive[i : i + 1, lanes]
                    )
                    read = c_tile * states[k]
                    tiles[k].append(read[0:8] + read[8:16])
            for k in range(blocks):
                scanned[
                    pl.ds(pl.multiple_of(base + half * 8, 8), 8), k * LANES : (k + 1) * LANES
                ] = fold_rows(tiles[k])
        gate = gate_in[pl.ds(base, GROUP), :].astype(jnp.float32)
        mixed = scanned[pl.ds(base, GROUP), :] + skip[...] * conv_act
        gated[pl.ds(base, GROUP), :] = (mixed * silu(gate)).astype(gated.dtype)
        return tuple(states)

    states = lax.fori_loop(0, tokens // GROUP, group, tuple(start))
    for k in range(blocks):
        leaving[:, k * LANES : (k + 1) * LANES] = states[k]


def read_out(
    me, chunk, chunks, step, conv_act, gate_in, decay_log, skip, b_wide, c_wide, entering, ends,
    after=(),
):
    tokens, channels = step.shape
    tokens = tokens // chunks
    width = 1024
    some = pl.BlockSpec((tokens, width), lambda j, me: (chunk, j))
    rows = lambda n: pl.BlockSpec((n, width), lambda j, me: (0, j))
    wide = pl.BlockSpec((tokens * 16, LANES), lambda j, me: (chunk, 0))
    masks = [mask for mask, _, _ in ends]
    scratch = [pltpu.VMEM((tokens, BLOCK), jnp.float32)]
    if ends:
        scratch.append(pltpu.VMEM((len(ends), STATE_ROWS, BLOCK), jnp.float32))
    split = [0] + [1] * 5 + [0, 0, 1] + [1] * len(ends) + [1, 1] + [0] * len(scratch)
    return launch(
        functools.partial(by_blocks, functools.partial(readout_kernel, masks), split),
        [me],
        [step, conv_act, gate_in, decay_log, skip, b_wide, c_wide, entering]
        + [end for _, _, end in ends],
        [some, some, some, rows(16), rows(1), wide, wide, rows(16)]
        + [rows(STATE_ROWS)] * len(ends),
        [rows(tokens), rows(16)],
        [
            jax.ShapeDtypeStruct((tokens, channels), jnp.bfloat16),
            jax.ShapeDtypeStruct((16, channels), jnp.float32),
        ],
        after=after,
        grid=(channels // width,),
        scratch=scratch,
        cost_estimate=cost(
            tokens * channels * 16 * 7, tokens * channels * 12, tokens * channels * 18
        ),
        name="read_out",
    )


def project_kernel(layout, me, weight, *refs):
    parts, (out, held, sems) = refs[: len(layout)], refs[len(layout) :]
    rows = held.shape[0] // (1 + max(mask for mask, _ in layout))

    @pl.when(pl.program_id(0) == 0)
    def _():
        copies = []
        for place, (mask, column) in enumerate(layout):
            part = parts[place]
            owner = me[0] ^ mask
            copies.append(
                pltpu.make_async_copy(
                    part,
                    held.at[
                        pl.ds(pl.multiple_of(owner * rows, rows), rows),
                        pl.ds(column, part.shape[1]),
                    ],
                    sems.at[place],
                )
            )
        for copy in copies:
            copy.start()
        for copy in copies:
            copy.wait()

    out[...] = jnp.dot(held[...], weight[...], preferred_element_type=jnp.float32).astype(
        out.dtype
    )


def project(me, parts, weight, after=()):
    depth, columns = weight.shape
    rows = parts[0][2].shape[0]
    total = rows * lax.axis_size("ctx")
    layout = [(mask, (which or 0) * depth // 2) for mask, which, _ in parts]
    tile = min(256, columns)
    return launch(
        functools.partial(project_kernel, layout),
        [me],
        [weight] + [part for _, _, part in parts],
        [pl.BlockSpec((depth, tile), lambda j, me: (0, j))] + [ANY] * len(parts),
        pl.BlockSpec((total, tile), lambda j, me: (0, j)),
        jax.ShapeDtypeStruct((total, columns), jnp.bfloat16),
        after=after,
        grid=(columns // tile,),
        scratch=[
            pltpu.VMEM((total, depth), jnp.bfloat16),
            pltpu.SemaphoreType.DMA((len(parts),)),
        ],
        limit=40,
        cost_estimate=cost(
            2 * total * depth * columns, 2 * (total * depth + depth * columns + total * columns)
        ),
        name="project",
    )


def hidden_kernel(layout, me, gain, gate_rows, up_rows, *refs):
    parts, (out, held, total, squares, sems) = refs[: len(layout)], refs[len(layout) :]
    turn = pl.program_id(0)

    def copy_of(place):
        mask, row = layout[place]
        part = parts[place]
        column = ((me[0] ^ mask) & 1) * part.shape[1]
        return pltpu.make_async_copy(
            part,
            held.at[
                mask // 2,
                pl.ds(row, part.shape[0]),
                pl.ds(pl.multiple_of(column, LANES), part.shape[1]),
            ],
            sems.at[place],
        )

    @pl.when(turn == 0)
    def _():
        for place in range(len(layout)):
            copy_of(place).start()
        total[...] = jnp.zeros_like(total)
        squares[...] = jnp.zeros_like(squares)

    for place, (mask, _) in enumerate(layout):

        @pl.when(turn == mask // 2)
        def _():
            copy_of(place).wait()

    width = out.shape[1]
    both = jnp.concatenate([gate_rows[...], up_rows[...]], axis=1)
    total[...] += jnp.dot(held[turn], both, preferred_element_type=jnp.float32)
    slots = out.shape[0]
    for row in range(0, slots, 64):
        mixer_square = squares[row : row + 64, :]
        for lane in range(0, held.shape[2], LANES):
            value = held[turn, row : row + 64, lane : lane + LANES].astype(jnp.float32)
            spot = lane % gain.shape[2]
            value = value * gain[lane // gain.shape[2], :, spot : spot + LANES]
            mixer_square += value * value
        squares[row : row + 64, :] = mixer_square

    @pl.when(turn == pl.num_programs(0) - 1)
    def _():
        def finish(index, _):
            spot = pl.ds(pl.multiple_of(index * 64, 64), 64)
            mean = jnp.sum(squares[spot, :], axis=1, keepdims=True) / D
            factor = lax.rsqrt(mean + 1e-05)
            gate_act = total[spot, 0:width] * factor
            up_act = total[spot, width:] * factor
            out[spot, :] = (silu(gate_act) * up_act).astype(out.dtype)
            return 0

        lax.fori_loop(0, out.shape[0] // 64, finish, 0)


def hidden_units(me, groups, one_over_gain, gate, up, after=()):
    depth = groups[0][0][2].shape[1]
    count = lax.axis_size("ctx")
    width = gate.shape[1]
    layout, parts, slots = [], [], 0
    for group in groups:
        rows = group[0][2].shape[0]
        layout += [(mask, slots + (which or 0) * rows // 2) for mask, which, _ in group]
        parts += group
        slots += rows
    block = pl.BlockSpec((2 * depth, width), lambda k, me: ((me[0] // 2) ^ k, 0))
    return launch(
        functools.partial(hidden_kernel, layout),
        [me],
        [one_over_gain, gate, up] + [part for _, _, part in parts],
        [
            pl.BlockSpec((2, 1, depth), lambda k, me: ((me[0] // 2) ^ k, 0, 0)),
            block,
            block,
        ] + [ANY] * len(parts),
        pl.BlockSpec((slots, width), lambda k, me: (0, 0)),
        jax.ShapeDtypeStruct((slots, width), jnp.bfloat16),
        after=after,
        grid=(count // 2,),
        scratch=[
            pltpu.VMEM((count // 2, slots, 2 * depth), jnp.bfloat16),
            pltpu.VMEM((slots, 2 * width), jnp.float32),
            pltpu.VMEM((slots, LANES), jnp.float32),
            pltpu.SemaphoreType.DMA((len(parts),)),
        ],
        limit=40,
        cost_estimate=cost(
            4 * slots * depth * count * width, 2 * count * depth * (slots + 2 * width)
        ),
        name="hidden_units",
    )


def down_kernel(layout, me, *refs):
    count = len(layout)
    units, weights, (out, held, sems) = refs[:count], refs[count:-3], refs[-3:]
    slots, width = held.shape[0], weights[0].shape[0]
    rows = slots * len(weights) // count

    @pl.when(pl.program_id(0) == 0)
    def _():
        copies = []
        for place, (mask, begin, row) in enumerate(layout):
            copies.append(
                pltpu.make_async_copy(
                    units[place].at[pl.ds(begin, rows), :],
                    held.at[pl.ds(row, rows), pl.ds(mask * width, width)],
                    sems.at[place],
                )
            )
        for copy in copies:
            copy.start()
        for copy in copies:
            copy.wait()

    tall = jnp.concatenate([weight[...] for weight in weights], axis=0)
    out[...] = jnp.dot(held[...], tall, preferred_element_type=jnp.float32).astype(out.dtype)


def down(me, segments, rows, weights, own, after=()):
    columns = weights[-1].shape[1]
    width = own.shape[0]
    depth = width * len(weights)
    slots = rows * len(segments)
    tile = min(256, columns)
    layout, units = [], []
    for place, (parts, begin) in enumerate(segments):
        for mask, part in enumerate(parts):
            layout.append((mask, begin, place * rows))
            units.append(part)
    steps = columns // tile
    return launch(
        functools.partial(down_kernel, layout),
        [me],
        units + [own] + list(weights[1:]),
        [ANY] * len(units)
        + [pl.BlockSpec((width, tile), lambda j, me: (0, me[0] * steps + j))]
        + [pl.BlockSpec((width, tile), lambda j, me: (0, j))] * (len(weights) - 1),
        pl.BlockSpec((slots, tile), lambda j, me: (0, j)),
        jax.ShapeDtypeStruct((slots, columns), jnp.bfloat16),
        after=after,
        grid=(steps,),
        scratch=[
            pltpu.VMEM((slots, depth), jnp.bfloat16),
            pltpu.SemaphoreType.DMA((len(units),)),
        ],
        limit=40,
        cost_estimate=cost(
            2 * slots * depth * columns, 2 * (slots * depth + depth * columns + slots * columns)
        ),
        name="down",
    )


def pick_kernel(count, rows, *refs):
    for picks, out in zip(refs[:count], refs[count:]):
        out[...] = lax.dot_general(
            picks[...], rows[...], (((0,), (0,)), ((), ())), preferred_element_type=jnp.float32
        ).astype(out.dtype)


def pick_rows(picks, rows, after=()):
    shape = (picks[0].shape[1], rows.shape[1])
    whole = lambda shape: pl.BlockSpec(shape, lambda j: (0, 0))
    return launch(
        functools.partial(pick_kernel, len(picks)),
        [],
        [rows] + list(picks),
        [whole(rows.shape)] + [whole(pick.shape) for pick in picks],
        [whole(shape)] * len(picks),
        [jax.ShapeDtypeStruct(shape, rows.dtype)] * len(picks),
        after=after,
        limit=24,
        cost_estimate=cost(2 * rows.size * shape[0] * len(picks), 4 * rows.size),
        name="pick_rows",
    )


def combine_kernel(me, mixer, ids, gates, *refs):
    out = refs[-1]
    count = len(refs) // 2
    total = mixer[...].astype(jnp.float32)
    for mask in range(count):
        named = ids[...] == (me[0] ^ mask)
        gate = jnp.sum(jnp.where(named, gates[...], 0.0), axis=1, keepdims=True)
        total += gate * jnp.dot(
            refs[mask][...], refs[count + mask][...], preferred_element_type=jnp.float32
        )
    out[...] = total.astype(out.dtype)


def combine(me, mixer_out, ids, gates, picks, answers):
    operands = [mixer_out, ids, gates] + list(picks) + list(answers)
    return launch(
        combine_kernel,
        [me],
        operands,
        [pl.BlockSpec(array.shape, lambda j, me: (0, 0)) for array in operands],
        pl.BlockSpec(mixer_out.shape, lambda j, me: (0, 0)),
        jax.ShapeDtypeStruct(mixer_out.shape, jnp.bfloat16),
        cost_estimate=cost(
            2 * mixer_out.size * answers[0].shape[0] * len(answers), 4 * mixer_out.size
        ),
        limit=24,
        name="combine",
    )


def shards(
    mixer_in,
    gate_in,
    delta_in,
    b_proj,
    c_proj,
    conv_kernel,
    conv_bias,
    delta_bias,
    decay_log,
    skip_gain,
    prefix_state,
    prefix_tail,
    out_proj,
    residual,
    norm_gain,
    expert_gate,
    expert_up,
    expert_down,
    expert_ids,
    route_gates,
):
    tokens = mixer_in.shape[0]
    rim = prefix_tail.shape[0]
    ctx_count = lax.axis_size("ctx")
    exp_count = lax.axis_size("exp")
    ctx_me = lax.axis_index("ctx")
    exp_me = lax.axis_index("exp")
    me = ctx_me.astype(jnp.int32).reshape(1)

    rim_rows = from_behind(mixer_in[tokens - rim :], "ctx", 1)
    rim_rows = jnp.where(ctx_me == 0, prefix_tail, rim_rows).astype(jnp.float32)
    rim8 = jnp.pad(rim_rows, ((8 - rim, 0), (0, 0)))

    width = out_proj.shape[1]
    down_rows = expert_down[0]
    down_parts = {}

    def send_columns(masks, after=()):
        for mask, cut in zip(masks, cut_columns(me, down_rows, width, masks, after)):
            down_parts[mask] = swap(cut, "ctx", mask)
        return tuple(down_parts[mask] for mask in masks)

    early = send_columns([2, 4])

    extra, left = [], norm_gain
    for _ in range(3):
        extra.append(lax.reduce_precision(left, 8, 7))
        left = left - extra[-1]
    extra = jnp.concatenate(extra)
    extra = jnp.pad(extra, (0, mixer_in.shape[1] - extra.shape[0]))[None, :]

    wide = lambda proj: jnp.broadcast_to(proj.T[:, :, None], (tokens, 16, LANES)).reshape(
        tokens * 16, LANES
    )
    b_wide, c_wide = wide(b_proj), wide(c_proj)
    step, conv_act, end = local_states(
        mixer_in,
        rim8,
        delta_in,
        conv_kernel,
        conv_bias[None, :],
        delta_bias[None, :],
        decay_log,
        extra,
        b_wide,
    )
    chunks = 2
    state, ends = prefix_state, gather_parts(join([end], early))
    one_over_gain = inverse_gains(me, ends, width)
    gated = []
    for chunk in range(chunks):
        rows, state = read_out(
            me,
            chunk,
            chunks,
            step,
            conv_act,
            gate_in,
            decay_log,
            skip_gain[None, :],
            b_wide,
            c_wide,
            state,
            ends,
        )
        ends = []
        gated.append(rows)
    near = lambda parts: [part for mask, _, part in parts if mask in (2, 4)]
    far = lambda parts: [part for mask, which, part in parts if which is not None][::2]
    scatter = lambda rows: lax.psum_scatter(rows, "exp", scatter_dimension=0, tiled=True)
    front = gather_parts(gated[0], 1, gated[1:])
    late = send_columns([3, 5, 6, 7, 1] + list(range(8, ctx_count)), near(front))
    back = gather_parts(gated[1], 1, far(front))
    partial = project(me, front, out_proj, gated[1:])
    projected = [scatter(partial)]
    partial = project(me, back, out_proj, [partial])
    projected.append(scatter(partial))

    block_rows = residual.shape[0]
    owners = block_rows // tokens
    projected = jnp.stack(
        [piece.reshape(owners, tokens // chunks, width) for piece in projected], axis=1
    ).reshape(block_rows, width)
    mixer_out = (residual.astype(jnp.float32) + projected.astype(jnp.float32)).astype(
        jnp.bfloat16
    )
    mixer_wide = mixer_out.astype(jnp.float32)
    scaled = (mixer_wide * norm_gain[None, :]).astype(jnp.bfloat16)
    experts = expert_gate.shape[0] * exp_count
    capacity = 3 * block_rows * expert_ids.shape[1] // (2 * experts)
    spots = jnp.arange(capacity, dtype=jnp.int32)
    picked = []
    for mask in range(exp_count):
        here = jnp.any(expert_ids == (exp_me ^ mask), axis=1)
        place = jnp.cumsum(here.astype(jnp.int32)) - 1
        pick = here[:, None] & (place[:, None] == spots[None, :])
        picked.append(pick.astype(jnp.bfloat16))

    groups = [[0, 2], [1, 3]] if exp_count == 4 else [list(range(exp_count))]
    last = groups[-1][-1] if len(groups) > 1 else None
    masks = [mask for mask in range(exp_count) if mask != last][::-1]
    rows = dict(zip(masks, pick_rows([picked[mask] for mask in masks], scaled)))
    pieces = {mask: swap(rows[mask], "exp", mask) for mask in masks if mask != 0}
    pieces[0] = rows[0]
    if last is not None:
        (sent,) = pick_rows([picked[last]], scaled, (pieces[groups[0][-1]],))
        pieces[last] = swap(sent, "exp", last)
    arrived, after = [], late
    for place, group in enumerate(groups):
        parts = gather_parts(join([pieces[mask] for mask in group], after), 0)
        after = near(parts)
        arrived.append(parts)
    hidden = hidden_units(me, arrived, one_over_gain, expert_gate[0], expert_up[0])
    units = {mask: part for mask, _, part in gather_parts(hidden)}
    units = [units[mask] for mask in range(ctx_count)]
    slots_of = [mask for group in groups for mask in group]
    segments = {mask: (units, place * capacity) for place, mask in enumerate(slots_of)}
    answers = {}
    weights = [None] + [down_parts[mask] for mask in range(1, ctx_count)]
    order = ()
    for group in [list(range(1, exp_count))[::-1], [0]]:
        answer = down(
            me, [segments[mask] for mask in group], capacity, weights, down_rows, order
        )
        order = [answer]
        for place, mask in enumerate(group):
            piece = lax.slice_in_dim(answer, place * capacity, (place + 1) * capacity, axis=0)
            answers[mask] = piece if mask == 0 else swap(piece, "exp", mask)
    block_out = combine(
        exp_me.astype(jnp.int32).reshape(1),
        mixer_out,
        expert_ids,
        route_gates,
        picked,
        [answers[mask] for mask in range(exp_count)],
    )
    return (mixer_out, block_out)


def solution(mesh):
    placed = (
        P("ctx", "exp"),
        P("ctx", "exp"),
        P("ctx", "exp"),
        P(None, "ctx"),
        P(None, "ctx"),
        P(None, "exp"),
        P("exp"),
        P("exp"),
        P(None, "exp"),
        P("exp"),
        P(None, "exp"),
        P(None, "exp"),
        P("exp", "ctx"),
        P("exp", "ctx"),
        P("ctx"),
        P("exp", None, "ctx"),
        P("exp", None, "ctx"),
        P("exp", "ctx", None),
        P("exp", None),
        P("exp", None),
    )
    return jax.shard_map(
        shards,
        mesh=mesh,
        in_specs=placed,
        out_specs=(P("exp", "ctx"), P("exp", "ctx")),
        check_vma=False,
    )
```

```python
import functools

import jax
import jax.numpy as jnp
from jax import lax
from jax.experimental import pallas as pl
from jax.experimental.pallas import tpu as pltpu
from jax.sharding import PartitionSpec as P

D = 8192
LOG2E = 1.4426950408889634
LANES = 128
MIB = 1 << 20


def from_behind(array, axis, by):
    length = lax.axis_size(axis)
    pairs = [(i, i + by) for i in range(length) if 0 <= i + by < length]
    return lax.ppermute(array, axis, pairs)


def swap(array, axis, mask):
    return lax.ppermute(array, axis, [(i, i ^ mask) for i in range(lax.axis_size(axis))])


def halves_kernel(split_dim, first, second, low, high):
    half = low.shape[split_dim]
    if split_dim == 0:
        low[...] = first[0:half, :]
        high[...] = second[half:, :]
    else:
        low[...] = first[:, 0:half]
        high[...] = second[:, half:]


def halves(first, second, split_dim, after=()):
    shape = list(first.shape)
    shape[split_dim] //= 2
    whole = pl.BlockSpec(first.shape, lambda j: (0, 0))
    part = pl.BlockSpec(tuple(shape), lambda j: (0, 0))
    return launch(
        functools.partial(halves_kernel, split_dim),
        [],
        [first, second],
        [whole, whole],
        [part, part],
        [jax.ShapeDtypeStruct(tuple(shape), first.dtype)] * 2,
        after=after,
        limit=16,
        cost_estimate=cost(0, 6 * first.size),
        name="halves",
    )


def gather_parts(array, split_dim=None, after=()):
    count = lax.axis_size("ctx")
    if count != 8:
        return [(0, None, array)] + [(m, None, swap(array, "ctx", m)) for m in range(1, count)]
    over_a = swap(array, "ctx", 2)
    over_b = swap(array, "ctx", 4)
    if split_dim is None:
        crossed = [(6, None, swap(array, "ctx", 6))]
    else:
        low, high = halves(over_a, over_b, split_dim, after)
        crossed = [(6, 0, swap(low, "ctx", 4)), (6, 1, swap(high, "ctx", 2))]
    parts = []
    for mask, which, part in [(0, None, array), (2, None, over_a), (4, None, over_b)] + crossed:
        parts.append((mask, which, part))
        parts.append((mask + 1, which, swap(part, "ctx", 1)))
    return parts


def silu(value):
    return value / (1.0 + jnp.exp(-value))


def cost(flops, moved, transcendentals=0):
    return pl.CostEstimate(
        flops=int(flops), bytes_accessed=int(moved), transcendentals=int(transcendentals)
    )


ANY = pl.BlockSpec(memory_space=pl.ANY)


def launch(
    kernel, scalars, operands, in_specs, out_specs, out_shape, after=(), grid=(1,), scratch=(),
    limit=56, **rest
):
    taken = len(scalars) + len(operands)

    def body(*refs):
        kernel(*refs[:taken], *refs[taken + len(after) :])

    return pl.pallas_call(
        body,
        grid_spec=pltpu.PrefetchScalarGridSpec(
            num_scalar_prefetch=len(scalars),
            grid=grid,
            in_specs=list(in_specs) + [ANY] * len(after),
            out_specs=out_specs,
            scratch_shapes=list(scratch),
        ),
        out_shape=out_shape,
        compiler_params=pltpu.CompilerParams(vmem_limit_bytes=limit * MIB),
        **rest,
    )(*scalars, *operands, *after)


def cut_kernel(count, *refs):
    for source, out in zip(refs[-2 * count : -count], refs[-count:]):
        out[...] = source[...]


def cut_columns(me, rows, width, masks, after=()):
    step = rows.shape[0] // 3

    def block(mask):
        return pl.BlockSpec((step, width), lambda i, me: (i, me[0] ^ mask))

    return launch(
        functools.partial(cut_kernel, len(masks)),
        [me],
        [rows] * len(masks),
        [block(mask) for mask in masks],
        [pl.BlockSpec((step, width), lambda i, me: (i, 0))] * len(masks),
        [jax.ShapeDtypeStruct((rows.shape[0], width), rows.dtype)] * len(masks),
        after=after,
        grid=(3,),
        cost_estimate=cost(0, 4 * rows.shape[0] * width * len(masks)),
        name="cut_columns",
    )


def join_kernel(count, *refs):
    pieces, out, sems = refs[:count], refs[count], refs[count + 1]
    copies, row = [], 0
    for place, piece in enumerate(pieces):
        copies.append(
            pltpu.make_async_copy(piece, out.at[pl.ds(row, piece.shape[0]), :], sems.at[place])
        )
        row += piece.shape[0]
    for copy in copies:
        copy.start()
    for copy in copies:
        copy.wait()


def join(pieces, after=()):
    rows = sum(piece.shape[0] for piece in pieces)
    columns = pieces[0].shape[1]
    return launch(
        functools.partial(join_kernel, len(pieces)),
        [],
        list(pieces),
        [ANY] * len(pieces),
        pl.BlockSpec((rows, columns), lambda j: (0, 0)),
        jax.ShapeDtypeStruct((rows, columns), pieces[0].dtype),
        after=after,
        scratch=[pltpu.SemaphoreType.DMA((len(pieces),))],
        limit=16,
        cost_estimate=cost(0, 4 * rows * columns),
        name="join",
    )


BLOCK = 512


def by_blocks(kernel, split, *refs):
    width = next(ref for ref, cut in zip(refs, split) if cut).shape[1]

    def one(index, _):
        lanes = pl.ds(pl.multiple_of(index * BLOCK, BLOCK), BLOCK)
        kernel(*[ref.at[:, lanes] if cut else ref for ref, cut in zip(refs, split)])
        return 0

    lax.fori_loop(0, width // BLOCK, one, 0)


GROUP = 16
STATE_ROWS = 32


def state_kernel(
    mixer, rim, delta, kernel, bias, delta_bias, decay_log, extra, b_wide, step_out, conv_out,
    end_out, padded,
):
    tokens, width = mixer.shape
    blocks = width // LANES
    padded[0:8, :] = rim[...]
    padded[8:, :] = mixer[...].astype(jnp.float32)
    rate = [
        -jnp.exp(decay_log[:, k * LANES : (k + 1) * LANES]) * LOG2E for k in range(blocks)
    ]
    taps = kernel.shape[0]

    def group(index, carry):
        states, total = carry
        base = pl.multiple_of(index * GROUP, GROUP)
        window = padded[pl.ds(base, GROUP + 8), :]
        convolved = bias[...] + sum(
            kernel[k : k + 1, :] * window[9 - taps + k : 9 - taps + k + GROUP, :]
            for k in range(taps)
        )
        conv_act = silu(convolved)
        step = jnp.log(
            1.0 + jnp.exp(delta[pl.ds(base, GROUP), :].astype(jnp.float32) + delta_bias[...])
        )
        step_out[pl.ds(base, GROUP), :] = step
        conv_out[pl.ds(base, GROUP), :] = conv_act
        drive = step * conv_act
        states = list(states)
        for i in range(GROUP):
            b_tile = b_wide[pl.ds(pl.multiple_of((base + i) * 16, 16), 16), :]
            for k in range(blocks):
                lanes = slice(k * LANES, (k + 1) * LANES)
                states[k] = (
                    jnp.exp2(step[i : i + 1, lanes] * rate[k]) * states[k]
                    + b_tile * drive[i : i + 1, lanes]
                )
        return tuple(states), total + step[0:8, :] + step[8:16, :]

    start = tuple(jnp.zeros((16, LANES), jnp.float32) for _ in range(blocks))
    states, total = lax.fori_loop(
        0, tokens // GROUP, group, (start, jnp.zeros((8, width), jnp.float32))
    )
    for k in range(blocks):
        end_out[0:16, k * LANES : (k + 1) * LANES] = states[k].astype(end_out.dtype)
    total = jnp.sum(total, axis=0, keepdims=True)
    place = lax.broadcasted_iota(jnp.int32, (16, width), 0)
    pieces = jnp.where(place == 3, extra[...], 0.0)
    for row in range(3):
        piece = total.astype(jnp.bfloat16).astype(jnp.float32)
        pieces = jnp.where(place == row, piece, pieces)
        total = total - piece
    end_out[16:32, :] = pieces.astype(end_out.dtype)


def local_states(mixer_in, rim8, delta_in, kernel, bias, delta_bias, decay_log, extra, b_wide):
    tokens, channels = mixer_in.shape
    width = 1024
    rows = lambda n: pl.BlockSpec((n, width), lambda j: (0, j))
    return launch(
        functools.partial(by_blocks, state_kernel, [1] * 8 + [0] + [1] * 3 + [0]),
        [],
        [mixer_in, rim8, delta_in, kernel, bias, delta_bias, decay_log, extra, b_wide],
        [
            rows(tokens),
            rows(8),
            rows(tokens),
            rows(kernel.shape[0]),
            rows(1),
            rows(1),
            rows(16),
            rows(1),
            pl.BlockSpec((tokens * 16, LANES), lambda j: (0, 0)),
        ],
        [rows(tokens), rows(tokens), rows(STATE_ROWS)],
        [
            jax.ShapeDtypeStruct((tokens, channels), jnp.float32),
            jax.ShapeDtypeStruct((tokens, channels), jnp.float32),
            jax.ShapeDtypeStruct((STATE_ROWS, channels), jnp.bfloat16),
        ],
        grid=(channels // width,),
        scratch=[pltpu.VMEM((tokens + 8, BLOCK), jnp.float32)],
        cost_estimate=cost(
            tokens * channels * 16 * 5, tokens * channels * 12, tokens * channels * 18
        ),
        name="local_states",
    )


def gains_kernel(masks, me, *refs):
    parts, out = refs[: len(masks)], refs[-1]
    width = out.shape[2]
    for mask, part in zip(masks, parts):
        row = part[...].astype(jnp.float32)[3:4, :]
        gain = row[:, 0:width] + row[:, width : 2 * width] + row[:, 2 * width : 3 * width]
        out[me[0] ^ mask] = 1.0 / gain


def inverse_gains(me, ends, width):
    return launch(
        functools.partial(gains_kernel, [mask for mask, _, _ in ends]),
        [me],
        [end for _, _, end in ends],
        [pl.BlockSpec((16, 3 * width), lambda j, me: (1, 0))] * len(ends),
        pl.BlockSpec((len(ends), 1, width), lambda j, me: (0, 0, 0)),
        jax.ShapeDtypeStruct((len(ends), 1, width), jnp.float32),
        limit=16,
        name="inverse_gains",
    )


def fold_rows(tiles):
    place = lax.broadcasted_iota(jnp.int32, (8, LANES), 0)
    for shift in (1, 2, 4):
        first = (place & shift) == 0
        tiles = [
            jnp.where(first, a, b) + pltpu.roll(jnp.where(first, b, a), shift, 0)
            for a, b in zip(tiles[0::2], tiles[1::2])
        ]
    return tiles[0]


def readout_kernel(
    masks, me, step_in, conv_in, gate_in, decay_log, skip, b_wide, c_wide, entering, *refs
):
    ends = refs[: len(masks)]
    gated, leaving, scanned = refs[len(masks) : len(masks) + 3]
    tokens, width = step_in.shape
    blocks = width // LANES
    rate = [
        -jnp.exp(decay_log[:, k * LANES : (k + 1) * LANES]) * LOG2E for k in range(blocks)
    ]
    start = [entering[:, k * LANES : (k + 1) * LANES] for k in range(blocks)]
    if masks:
        held = refs[-1]
        for mask, end in zip(masks, ends):
            held[mask] = end[...].astype(jnp.float32)
        for owner in range(len(masks) - 1):
            end = held[me[0] ^ owner]
            total = end[16:17, :] + end[17:18, :] + end[18:19, :]
            for k in range(blocks):
                lanes = slice(k * LANES, (k + 1) * LANES)
                later = jnp.exp2(total[:, lanes] * rate[k]) * start[k] + end[0:16, lanes]
                start[k] = jnp.where(owner < me[0], later, start[k])

    def group(index, states):
        base = pl.multiple_of(index * GROUP, GROUP)
        step = step_in[pl.ds(base, GROUP), :]
        conv_act = conv_in[pl.ds(base, GROUP), :]
        drive = step * conv_act
        states = list(states)
        for half in range(GROUP // 8):
            tiles = [[] for _ in range(blocks)]
            for i in range(half * 8, half * 8 + 8):
                spot = pl.ds(pl.multiple_of((base + i) * 16, 16), 16)
                b_tile = b_wide[spot, :]
                c_tile = c_wide[spot, :]
                for k in range(blocks):
                    lanes = slice(k * LANES, (k + 1) * LANES)
                    states[k] = (
                        jnp.exp2(step[i : i + 1, lanes] * rate[k]) * states[k]
                        + b_tile * drive[i : i + 1, lanes]
                    )
                    read = c_tile * states[k]
                    tiles[k].append(read[0:8] + read[8:16])
            for k in range(blocks):
                scanned[
                    pl.ds(pl.multiple_of(base + half * 8, 8), 8), k * LANES : (k + 1) * LANES
                ] = fold_rows(tiles[k])
        gate = gate_in[pl.ds(base, GROUP), :].astype(jnp.float32)
        mixed = scanned[pl.ds(base, GROUP), :] + skip[...] * conv_act
        gated[pl.ds(base, GROUP), :] = (mixed * silu(gate)).astype(gated.dtype)
        return tuple(states)

    states = lax.fori_loop(0, tokens // GROUP, group, tuple(start))
    for k in range(blocks):
        leaving[:, k * LANES : (k + 1) * LANES] = states[k]


def read_out(
    me, chunk, chunks, step, conv_act, gate_in, decay_log, skip, b_wide, c_wide, entering, ends,
    after=(),
):
    tokens, channels = step.shape
    tokens = tokens // chunks
    width = 1024
    some = pl.BlockSpec((tokens, width), lambda j, me: (chunk, j))
    rows = lambda n: pl.BlockSpec((n, width), lambda j, me: (0, j))
    wide = pl.BlockSpec((tokens * 16, LANES), lambda j, me: (chunk, 0))
    masks = [mask for mask, _, _ in ends]
    scratch = [pltpu.VMEM((tokens, BLOCK), jnp.float32)]
    if ends:
        scratch.append(pltpu.VMEM((len(ends), STATE_ROWS, BLOCK), jnp.float32))
    split = [0] + [1] * 5 + [0, 0, 1] + [1] * len(ends) + [1, 1] + [0] * len(scratch)
    return launch(
        functools.partial(by_blocks, functools.partial(readout_kernel, masks), split),
        [me],
        [step, conv_act, gate_in, decay_log, skip, b_wide, c_wide, entering]
        + [end for _, _, end in ends],
        [some, some, some, rows(16), rows(1), wide, wide, rows(16)]
        + [rows(STATE_ROWS)] * len(ends),
        [rows(tokens), rows(16)],
        [
            jax.ShapeDtypeStruct((tokens, channels), jnp.bfloat16),
            jax.ShapeDtypeStruct((16, channels), jnp.float32),
        ],
        after=after,
        grid=(channels // width,),
        scratch=scratch,
        cost_estimate=cost(
            tokens * channels * 16 * 7, tokens * channels * 12, tokens * channels * 18
        ),
        name="read_out",
    )


def project_kernel(layout, me, weight, *refs):
    parts, (out, held, sems) = refs[: len(layout)], refs[len(layout) :]
    rows = held.shape[0] // (1 + max(mask for mask, _ in layout))

    @pl.when(pl.program_id(0) == 0)
    def _():
        copies = []
        for place, (mask, column) in enumerate(layout):
            part = parts[place]
            owner = me[0] ^ mask
            copies.append(
                pltpu.make_async_copy(
                    part,
                    held.at[
                        pl.ds(pl.multiple_of(owner * rows, rows), rows),
                        pl.ds(column, part.shape[1]),
                    ],
                    sems.at[place],
                )
            )
        for copy in copies:
            copy.start()
        for copy in copies:
            copy.wait()

    out[...] = jnp.dot(held[...], weight[...], preferred_element_type=jnp.float32).astype(
        out.dtype
    )


def project(me, parts, weight, after=()):
    depth, columns = weight.shape
    rows = parts[0][2].shape[0]
    total = rows * lax.axis_size("ctx")
    layout = [(mask, (which or 0) * depth // 2) for mask, which, _ in parts]
    tile = min(256, columns)
    return launch(
        functools.partial(project_kernel, layout),
        [me],
        [weight] + [part for _, _, part in parts],
        [pl.BlockSpec((depth, tile), lambda j, me: (0, j))] + [ANY] * len(parts),
        pl.BlockSpec((total, tile), lambda j, me: (0, j)),
        jax.ShapeDtypeStruct((total, columns), jnp.bfloat16),
        after=after,
        grid=(columns // tile,),
        scratch=[
            pltpu.VMEM((total, depth), jnp.bfloat16),
            pltpu.SemaphoreType.DMA((len(parts),)),
        ],
        limit=40,
        cost_estimate=cost(
            2 * total * depth * columns, 2 * (total * depth + depth * columns + total * columns)
        ),
        name="project",
    )


def hidden_kernel(layout, me, gain, gate_rows, up_rows, *refs):
    parts, (out, held, total, squares, sems) = refs[: len(layout)], refs[len(layout) :]
    turn = pl.program_id(0)

    def copy_of(place):
        mask, row = layout[place]
        part = parts[place]
        column = ((me[0] ^ mask) & 1) * part.shape[1]
        return pltpu.make_async_copy(
            part,
            held.at[
                mask // 2,
                pl.ds(row, part.shape[0]),
                pl.ds(pl.multiple_of(column, LANES), part.shape[1]),
            ],
            sems.at[place],
        )

    @pl.when(turn == 0)
    def _():
        for place in range(len(layout)):
            copy_of(place).start()
        total[...] = jnp.zeros_like(total)
        squares[...] = jnp.zeros_like(squares)

    for place, (mask, _) in enumerate(layout):

        @pl.when(turn == mask // 2)
        def _():
            copy_of(place).wait()

    width = out.shape[1]
    both = jnp.concatenate([gate_rows[...], up_rows[...]], axis=1)
    total[...] += jnp.dot(held[turn], both, preferred_element_type=jnp.float32)
    slots = out.shape[0]
    for row in range(0, slots, 64):
        mixer_square = squares[row : row + 64, :]
        for lane in range(0, held.shape[2], LANES):
            value = held[turn, row : row + 64, lane : lane + LANES].astype(jnp.float32)
            spot = lane % gain.shape[2]
            value = value * gain[lane // gain.shape[2], :, spot : spot + LANES]
            mixer_square += value * value
        squares[row : row + 64, :] = mixer_square

    @pl.when(turn == pl.num_programs(0) - 1)
    def _():
        def finish(index, _):
            spot = pl.ds(pl.multiple_of(index * 64, 64), 64)
            mean = jnp.sum(squares[spot, :], axis=1, keepdims=True) / D
            factor = lax.rsqrt(mean + 1e-05)
            gate_act = total[spot, 0:width] * factor
            up_act = total[spot, width:] * factor
            out[spot, :] = (silu(gate_act) * up_act).astype(out.dtype)
            return 0

        lax.fori_loop(0, out.shape[0] // 64, finish, 0)


def hidden_units(me, groups, one_over_gain, gate, up, after=()):
    depth = groups[0][0][2].shape[1]
    count = lax.axis_size("ctx")
    width = gate.shape[1]
    layout, parts, slots = [], [], 0
    for group in groups:
        rows = group[0][2].shape[0]
        layout += [(mask, slots + (which or 0) * rows // 2) for mask, which, _ in group]
        parts += group
        slots += rows
    block = pl.BlockSpec((2 * depth, width), lambda k, me: ((me[0] // 2) ^ k, 0))
    return launch(
        functools.partial(hidden_kernel, layout),
        [me],
        [one_over_gain, gate, up] + [part for _, _, part in parts],
        [
            pl.BlockSpec((2, 1, depth), lambda k, me: ((me[0] // 2) ^ k, 0, 0)),
            block,
            block,
        ] + [ANY] * len(parts),
        pl.BlockSpec((slots, width), lambda k, me: (0, 0)),
        jax.ShapeDtypeStruct((slots, width), jnp.bfloat16),
        after=after,
        grid=(count // 2,),
        scratch=[
            pltpu.VMEM((count // 2, slots, 2 * depth), jnp.bfloat16),
            pltpu.VMEM((slots, 2 * width), jnp.float32),
            pltpu.VMEM((slots, LANES), jnp.float32),
            pltpu.SemaphoreType.DMA((len(parts),)),
        ],
        limit=40,
        cost_estimate=cost(
            4 * slots * depth * count * width, 2 * count * depth * (slots + 2 * width)
        ),
        name="hidden_units",
    )


def down_kernel(layout, me, *refs):
    count = len(layout)
    units, weights, (out, held, sems) = refs[:count], refs[count:-3], refs[-3:]
    width = weights[0].shape[0]

    @pl.when(pl.program_id(0) == 0)
    def _():
        copies = []
        for place, (mask, row) in enumerate(layout):
            unit = units[place]
            copies.append(
                pltpu.make_async_copy(
                    unit,
                    held.at[pl.ds(row, unit.shape[0]), pl.ds(mask * width, width)],
                    sems.at[place],
                )
            )
        for copy in copies:
            copy.start()
        for copy in copies:
            copy.wait()

    tall = jnp.concatenate([weight[...] for weight in weights], axis=0)
    out[...] = jnp.dot(held[...], tall, preferred_element_type=jnp.float32).astype(out.dtype)


def down(me, parts, weights, own, after=()):
    columns = weights[-1].shape[1]
    width = own.shape[0]
    depth = width * len(weights)
    slots = parts[0][2].shape[0]
    tile = min(256, columns)
    layout = [(mask, (which or 0) * slots // 2) for mask, which, _ in parts]
    units = [part for _, _, part in parts]
    steps = columns // tile
    return launch(
        functools.partial(down_kernel, layout),
        [me],
        units + [own] + list(weights[1:]),
        [ANY] * len(units)
        + [pl.BlockSpec((width, tile), lambda j, me: (0, me[0] * steps + j))]
        + [pl.BlockSpec((width, tile), lambda j, me: (0, j))] * (len(weights) - 1),
        pl.BlockSpec((slots, tile), lambda j, me: (0, j)),
        jax.ShapeDtypeStruct((slots, columns), jnp.bfloat16),
        after=after,
        grid=(steps,),
        scratch=[
            pltpu.VMEM((slots, depth), jnp.bfloat16),
            pltpu.SemaphoreType.DMA((len(units),)),
        ],
        limit=40,
        cost_estimate=cost(
            2 * slots * depth * columns, 2 * (slots * depth + depth * columns + slots * columns)
        ),
        name="down",
    )


def pick_kernel(count, rows, *refs):
    for picks, out in zip(refs[:count], refs[count:]):
        out[...] = lax.dot_general(
            picks[...], rows[...], (((0,), (0,)), ((), ())), preferred_element_type=jnp.float32
        ).astype(out.dtype)


def pick_rows(picks, rows, after=()):
    shape = (picks[0].shape[1], rows.shape[1])
    whole = lambda shape: pl.BlockSpec(shape, lambda j: (0, 0))
    return launch(
        functools.partial(pick_kernel, len(picks)),
        [],
        [rows] + list(picks),
        [whole(rows.shape)] + [whole(pick.shape) for pick in picks],
        [whole(shape)] * len(picks),
        [jax.ShapeDtypeStruct(shape, rows.dtype)] * len(picks),
        after=after,
        limit=24,
        cost_estimate=cost(2 * rows.size * shape[0] * len(picks), 4 * rows.size),
        name="pick_rows",
    )


def combine_kernel(me, mixer, ids, gates, *refs):
    out = refs[-1]
    count = len(refs) // 2
    total = mixer[...].astype(jnp.float32)
    for mask in range(count):
        named = ids[...] == (me[0] ^ mask)
        gate = jnp.sum(jnp.where(named, gates[...], 0.0), axis=1, keepdims=True)
        total += gate * jnp.dot(
            refs[mask][...], refs[count + mask][...], preferred_element_type=jnp.float32
        )
    out[...] = total.astype(out.dtype)


def combine(me, mixer_out, ids, gates, picks, answers):
    operands = [mixer_out, ids, gates] + list(picks) + list(answers)
    return launch(
        combine_kernel,
        [me],
        operands,
        [pl.BlockSpec(array.shape, lambda j, me: (0, 0)) for array in operands],
        pl.BlockSpec(mixer_out.shape, lambda j, me: (0, 0)),
        jax.ShapeDtypeStruct(mixer_out.shape, jnp.bfloat16),
        cost_estimate=cost(
            2 * mixer_out.size * answers[0].shape[0] * len(answers), 4 * mixer_out.size
        ),
        limit=24,
        name="combine",
    )


def shards(
    mixer_in,
    gate_in,
    delta_in,
    b_proj,
    c_proj,
    conv_kernel,
    conv_bias,
    delta_bias,
    decay_log,
    skip_gain,
    prefix_state,
    prefix_tail,
    out_proj,
    residual,
    norm_gain,
    expert_gate,
    expert_up,
    expert_down,
    expert_ids,
    route_gates,
):
    tokens = mixer_in.shape[0]
    rim = prefix_tail.shape[0]
    ctx_count = lax.axis_size("ctx")
    exp_count = lax.axis_size("exp")
    ctx_me = lax.axis_index("ctx")
    exp_me = lax.axis_index("exp")
    me = ctx_me.astype(jnp.int32).reshape(1)

    rim_rows = from_behind(mixer_in[tokens - rim :], "ctx", 1)
    rim_rows = jnp.where(ctx_me == 0, prefix_tail, rim_rows).astype(jnp.float32)
    rim8 = jnp.pad(rim_rows, ((8 - rim, 0), (0, 0)))

    width = out_proj.shape[1]
    down_rows = expert_down[0]
    down_parts = {}

    def send_columns(masks, after=()):
        for mask, cut in zip(masks, cut_columns(me, down_rows, width, masks, after)):
            down_parts[mask] = swap(cut, "ctx", mask)
        return tuple(down_parts[mask] for mask in masks)

    early = send_columns([2, 4])

    extra, left = [], norm_gain
    for _ in range(3):
        extra.append(lax.reduce_precision(left, 8, 7))
        left = left - extra[-1]
    extra = jnp.concatenate(extra)
    extra = jnp.pad(extra, (0, mixer_in.shape[1] - extra.shape[0]))[None, :]

    wide = lambda proj: jnp.broadcast_to(proj.T[:, :, None], (tokens, 16, LANES)).reshape(
        tokens * 16, LANES
    )
    b_wide, c_wide = wide(b_proj), wide(c_proj)
    step, conv_act, end = local_states(
        mixer_in,
        rim8,
        delta_in,
        conv_kernel,
        conv_bias[None, :],
        delta_bias[None, :],
        decay_log,
        extra,
        b_wide,
    )
    chunks = 2
    state, ends = prefix_state, gather_parts(join([end], early))
    one_over_gain = inverse_gains(me, ends, width)
    gated = []
    for chunk in range(chunks):
        rows, state = read_out(
            me,
            chunk,
            chunks,
            step,
            conv_act,
            gate_in,
            decay_log,
            skip_gain[None, :],
            b_wide,
            c_wide,
            state,
            ends,
        )
        ends = []
        gated.append(rows)
    near = lambda parts: [part for mask, _, part in parts if mask in (2, 4)]
    far = lambda parts: [part for mask, which, part in parts if which is not None][::2]
    scatter = lambda rows: lax.psum_scatter(rows, "exp", scatter_dimension=0, tiled=True)
    front = gather_parts(gated[0], 1, gated[1:])
    late = send_columns([3, 5, 6, 7, 1] + list(range(8, ctx_count)), near(front))
    back = gather_parts(gated[1], 1, far(front))
    partial = project(me, front, out_proj, near(back))
    projected = [scatter(partial)]
    partial = project(me, back, out_proj, [partial])
    projected.append(scatter(partial))

    block_rows = residual.shape[0]
    owners = block_rows // tokens
    projected = jnp.stack(
        [piece.reshape(owners, tokens // chunks, width) for piece in projected], axis=1
    ).reshape(block_rows, width)
    mixer_out = (residual.astype(jnp.float32) + projected.astype(jnp.float32)).astype(
        jnp.bfloat16
    )
    mixer_wide = mixer_out.astype(jnp.float32)
    scaled = (mixer_wide * norm_gain[None, :]).astype(jnp.bfloat16)
    experts = expert_gate.shape[0] * exp_count
    capacity = 3 * block_rows * expert_ids.shape[1] // (2 * experts)
    spots = jnp.arange(capacity, dtype=jnp.int32)
    picked = []
    for mask in range(exp_count):
        here = jnp.any(expert_ids == (exp_me ^ mask), axis=1)
        place = jnp.cumsum(here.astype(jnp.int32)) - 1
        pick = here[:, None] & (place[:, None] == spots[None, :])
        picked.append(pick.astype(jnp.bfloat16))

    groups = [[0, 1], [2, 3]] if exp_count == 4 else [list(range(exp_count))]
    sent = pick_rows(picked, scaled)
    pieces = [rows if mask == 0 else swap(rows, "exp", mask) for mask, rows in enumerate(sent)]
    hiddens, after, order = [], late[:3], late[3:]
    for group in groups:
        parts = gather_parts(join([pieces[mask] for mask in group], after), 0, order)
        after = near(parts)
        hidden = hidden_units(me, [parts], one_over_gain, expert_gate[0], expert_up[0])
        order = [hidden]
        hiddens.append(hidden)
    answers, order = {}, []
    weights = [None] + [down_parts[mask] for mask in range(1, ctx_count)]
    for group, hidden in zip(groups, hiddens):
        last = group is groups[-1]
        units = join([hidden], far(parts)) if not last else hidden
        units = gather_parts(units, 0, hiddens[-1:] if not last else ())
        answer = down(me, units, weights, down_rows, order)
        order = [answer]
        for place, mask in enumerate(group):
            piece = lax.slice_in_dim(answer, place * capacity, (place + 1) * capacity, axis=0)
            answers[mask] = piece if mask == 0 else swap(piece, "exp", mask)
    block_out = combine(
        exp_me.astype(jnp.int32).reshape(1),
        mixer_out,
        expert_ids,
        route_gates,
        picked,
        [answers[mask] for mask in range(exp_count)],
    )
    return (mixer_out, block_out)


def solution(mesh):
    placed = (
        P("ctx", "exp"),
        P("ctx", "exp"),
        P("ctx", "exp"),
        P(None, "ctx"),
        P(None, "ctx"),
        P(None, "exp"),
        P("exp"),
        P("exp"),
        P(None, "exp"),
        P("exp"),
        P(None, "exp"),
        P(None, "exp"),
        P("exp", "ctx"),
        P("exp", "ctx"),
        P("ctx"),
        P("exp", None, "ctx"),
        P("exp", None, "ctx"),
        P("exp", "ctx", None),
        P("exp", None),
        P("exp", None),
    )
    return jax.shard_map(
        shards,
        mesh=mesh,
        in_specs=placed,
        out_specs=(P("exp", "ctx"), P("exp", "ctx")),
        check_vma=False,
    )
```

```python
import functools

import jax
import jax.numpy as jnp
from jax import lax
from jax.experimental import pallas as pl
from jax.experimental.pallas import tpu as pltpu
from jax.sharding import PartitionSpec as P

D = 8192
LOG2E = 1.4426950408889634
LANES = 128
MIB = 1 << 20


def from_behind(array, axis, by):
    length = lax.axis_size(axis)
    pairs = [(i, i + by) for i in range(length) if 0 <= i + by < length]
    return lax.ppermute(array, axis, pairs)


def swap(array, axis, mask):
    return lax.ppermute(array, axis, [(i, i ^ mask) for i in range(lax.axis_size(axis))])


def halves_kernel(split_dim, first, second, low, high):
    half = low.shape[split_dim]
    if split_dim == 0:
        low[...] = first[0:half, :]
        high[...] = second[half:, :]
    else:
        low[...] = first[:, 0:half]
        high[...] = second[:, half:]


def halves(first, second, split_dim, after=()):
    shape = list(first.shape)
    shape[split_dim] //= 2
    whole = pl.BlockSpec(first.shape, lambda j: (0, 0))
    part = pl.BlockSpec(tuple(shape), lambda j: (0, 0))
    return launch(
        functools.partial(halves_kernel, split_dim),
        [],
        [first, second],
        [whole, whole],
        [part, part],
        [jax.ShapeDtypeStruct(tuple(shape), first.dtype)] * 2,
        after=after,
        limit=16,
        cost_estimate=cost(0, 6 * first.size),
        name="halves",
    )


def gather_parts(array, split_dim=None, after=()):
    count = lax.axis_size("ctx")
    if count != 8:
        return [(0, None, array)] + [(m, None, swap(array, "ctx", m)) for m in range(1, count)]
    over_a = swap(array, "ctx", 2)
    over_b = swap(array, "ctx", 4)
    if split_dim is None:
        crossed = [(6, None, swap(array, "ctx", 6))]
    else:
        low, high = halves(over_a, over_b, split_dim, after)
        crossed = [(6, 0, swap(low, "ctx", 4)), (6, 1, swap(high, "ctx", 2))]
    parts = []
    for mask, which, part in [(0, None, array), (2, None, over_a), (4, None, over_b)] + crossed:
        parts.append((mask, which, part))
        parts.append((mask + 1, which, swap(part, "ctx", 1)))
    return parts


def silu(value):
    return value / (1.0 + jnp.exp(-value))


def cost(flops, moved, transcendentals=0):
    return pl.CostEstimate(
        flops=int(flops), bytes_accessed=int(moved), transcendentals=int(transcendentals)
    )


ANY = pl.BlockSpec(memory_space=pl.ANY)


def launch(
    kernel, scalars, operands, in_specs, out_specs, out_shape, after=(), grid=(1,), scratch=(),
    limit=56, **rest
):
    taken = len(scalars) + len(operands)

    def body(*refs):
        kernel(*refs[:taken], *refs[taken + len(after) :])

    return pl.pallas_call(
        body,
        grid_spec=pltpu.PrefetchScalarGridSpec(
            num_scalar_prefetch=len(scalars),
            grid=grid,
            in_specs=list(in_specs) + [ANY] * len(after),
            out_specs=out_specs,
            scratch_shapes=list(scratch),
        ),
        out_shape=out_shape,
        compiler_params=pltpu.CompilerParams(vmem_limit_bytes=limit * MIB),
        **rest,
    )(*scalars, *operands, *after)


def cut_kernel(layout, me, *refs):
    count = sum(len(pieces) for pieces in layout)
    sources, outs = iter(refs[:count]), refs[count:]
    for pieces, out in zip(layout, outs):
        width = out.shape[1] // len(pieces)
        for place in range(len(pieces)):
            out[:, place * width : (place + 1) * width] = next(sources)[...]


def cut_columns(me, rows, width, layout, after=()):
    step = rows.shape[0] // 3
    parts = rows.shape[1] // lax.axis_size("ctx") // width

    def block(mask, part):
        return pl.BlockSpec((step, width), lambda i, me: (i, (me[0] ^ mask) * parts + part))

    flat = [piece for pieces in layout for piece in pieces]
    widths = [width * len(pieces) for pieces in layout]
    return launch(
        functools.partial(cut_kernel, layout),
        [me],
        [rows] * len(flat),
        [block(*piece) for piece in flat],
        [pl.BlockSpec((step, wide), lambda i, me: (i, 0)) for wide in widths],
        [jax.ShapeDtypeStruct((rows.shape[0], wide), rows.dtype) for wide in widths],
        after=after,
        grid=(3,),
        cost_estimate=cost(0, 4 * rows.shape[0] * width * len(flat)),
        name="cut_columns",
    )


def join_kernel(count, *refs):
    pieces, out, sems = refs[:count], refs[count], refs[count + 1]
    copies, row = [], 0
    for place, piece in enumerate(pieces):
        copies.append(
            pltpu.make_async_copy(piece, out.at[pl.ds(row, piece.shape[0]), :], sems.at[place])
        )
        row += piece.shape[0]
    for copy in copies:
        copy.start()
    for copy in copies:
        copy.wait()


def join(pieces, after=()):
    rows = sum(piece.shape[0] for piece in pieces)
    columns = pieces[0].shape[1]
    return launch(
        functools.partial(join_kernel, len(pieces)),
        [],
        list(pieces),
        [ANY] * len(pieces),
        pl.BlockSpec((rows, columns), lambda j: (0, 0)),
        jax.ShapeDtypeStruct((rows, columns), pieces[0].dtype),
        after=after,
        scratch=[pltpu.SemaphoreType.DMA((len(pieces),))],
        limit=16,
        cost_estimate=cost(0, 4 * rows * columns),
        name="join",
    )


BLOCK = 512


def by_blocks(kernel, split, *refs):
    width = next(ref for ref, cut in zip(refs, split) if cut).shape[1]

    def one(index, _):
        lanes = pl.ds(pl.multiple_of(index * BLOCK, BLOCK), BLOCK)
        kernel(*[ref.at[:, lanes] if cut else ref for ref, cut in zip(refs, split)])
        return 0

    lax.fori_loop(0, width // BLOCK, one, 0)


GROUP = 16
STATE_ROWS = 32


def state_kernel(
    mixer, rim, delta, kernel, bias, delta_bias, decay_log, extra, b_wide, step_out, conv_out,
    end_out, padded,
):
    tokens, width = mixer.shape
    blocks = width // LANES
    padded[0:8, :] = rim[...]
    padded[8:, :] = mixer[...].astype(jnp.float32)
    rate = [
        -jnp.exp(decay_log[:, k * LANES : (k + 1) * LANES]) * LOG2E for k in range(blocks)
    ]
    taps = kernel.shape[0]

    def group(index, carry):
        states, total = carry
        base = pl.multiple_of(index * GROUP, GROUP)
        window = padded[pl.ds(base, GROUP + 8), :]
        convolved = bias[...] + sum(
            kernel[k : k + 1, :] * window[9 - taps + k : 9 - taps + k + GROUP, :]
            for k in range(taps)
        )
        conv_act = silu(convolved)
        step = jnp.log(
            1.0 + jnp.exp(delta[pl.ds(base, GROUP), :].astype(jnp.float32) + delta_bias[...])
        )
        step_out[pl.ds(base, GROUP), :] = step
        conv_out[pl.ds(base, GROUP), :] = conv_act
        drive = step * conv_act
        states = list(states)
        for i in range(GROUP):
            b_tile = b_wide[pl.ds(pl.multiple_of((base + i) * 16, 16), 16), :]
            for k in range(blocks):
                lanes = slice(k * LANES, (k + 1) * LANES)
                states[k] = (
                    jnp.exp2(step[i : i + 1, lanes] * rate[k]) * states[k]
                    + b_tile * drive[i : i + 1, lanes]
                )
        return tuple(states), total + step[0:8, :] + step[8:16, :]

    start = tuple(jnp.zeros((16, LANES), jnp.float32) for _ in range(blocks))
    states, total = lax.fori_loop(
        0, tokens // GROUP, group, (start, jnp.zeros((8, width), jnp.float32))
    )
    for k in range(blocks):
        end_out[0:16, k * LANES : (k + 1) * LANES] = states[k].astype(end_out.dtype)
    total = jnp.sum(total, axis=0, keepdims=True)
    place = lax.broadcasted_iota(jnp.int32, (16, width), 0)
    pieces = jnp.where(place == 3, extra[...], 0.0)
    for row in range(3):
        piece = total.astype(jnp.bfloat16).astype(jnp.float32)
        pieces = jnp.where(place == row, piece, pieces)
        total = total - piece
    end_out[16:32, :] = pieces.astype(end_out.dtype)


def local_states(mixer_in, rim8, delta_in, kernel, bias, delta_bias, decay_log, extra, b_wide):
    tokens, channels = mixer_in.shape
    width = 1024
    rows = lambda n: pl.BlockSpec((n, width), lambda j: (0, j))
    return launch(
        functools.partial(by_blocks, state_kernel, [1] * 8 + [0] + [1] * 3 + [0]),
        [],
        [mixer_in, rim8, delta_in, kernel, bias, delta_bias, decay_log, extra, b_wide],
        [
            rows(tokens),
            rows(8),
            rows(tokens),
            rows(kernel.shape[0]),
            rows(1),
            rows(1),
            rows(16),
            rows(1),
            pl.BlockSpec((tokens * 16, LANES), lambda j: (0, 0)),
        ],
        [rows(tokens), rows(tokens), rows(STATE_ROWS)],
        [
            jax.ShapeDtypeStruct((tokens, channels), jnp.float32),
            jax.ShapeDtypeStruct((tokens, channels), jnp.float32),
            jax.ShapeDtypeStruct((STATE_ROWS, channels), jnp.bfloat16),
        ],
        grid=(channels // width,),
        scratch=[pltpu.VMEM((tokens + 8, BLOCK), jnp.float32)],
        cost_estimate=cost(
            tokens * channels * 16 * 5, tokens * channels * 12, tokens * channels * 18
        ),
        name="local_states",
    )


def gains_kernel(masks, me, *refs):
    parts, out = refs[: len(masks)], refs[-1]
    width = out.shape[2]
    for mask, part in zip(masks, parts):
        row = part[...].astype(jnp.float32)[3:4, :]
        gain = row[:, 0:width] + row[:, width : 2 * width] + row[:, 2 * width : 3 * width]
        out[me[0] ^ mask] = 1.0 / gain


def inverse_gains(me, ends, width):
    return launch(
        functools.partial(gains_kernel, [mask for mask, _, _ in ends]),
        [me],
        [end for _, _, end in ends],
        [pl.BlockSpec((16, 3 * width), lambda j, me: (1, 0))] * len(ends),
        pl.BlockSpec((len(ends), 1, width), lambda j, me: (0, 0, 0)),
        jax.ShapeDtypeStruct((len(ends), 1, width), jnp.float32),
        limit=16,
        name="inverse_gains",
    )


def fold_rows(tiles):
    place = lax.broadcasted_iota(jnp.int32, (8, LANES), 0)
    for shift in (1, 2, 4):
        first = (place & shift) == 0
        tiles = [
            jnp.where(first, a, b) + pltpu.roll(jnp.where(first, b, a), shift, 0)
            for a, b in zip(tiles[0::2], tiles[1::2])
        ]
    return tiles[0]


def readout_kernel(
    masks, me, step_in, conv_in, gate_in, decay_log, skip, b_wide, c_wide, entering, *refs
):
    ends = refs[: len(masks)]
    gated, leaving, scanned = refs[len(masks) : len(masks) + 3]
    tokens, width = step_in.shape
    blocks = width // LANES
    rate = [
        -jnp.exp(decay_log[:, k * LANES : (k + 1) * LANES]) * LOG2E for k in range(blocks)
    ]
    start = [entering[:, k * LANES : (k + 1) * LANES] for k in range(blocks)]
    if masks:
        held = refs[-1]
        for mask, end in zip(masks, ends):
            held[mask] = end[...].astype(jnp.float32)
        for owner in range(len(masks) - 1):
            end = held[me[0] ^ owner]
            total = end[16:17, :] + end[17:18, :] + end[18:19, :]
            for k in range(blocks):
                lanes = slice(k * LANES, (k + 1) * LANES)
                later = jnp.exp2(total[:, lanes] * rate[k]) * start[k] + end[0:16, lanes]
                start[k] = jnp.where(owner < me[0], later, start[k])

    def group(index, states):
        base = pl.multiple_of(index * GROUP, GROUP)
        step = step_in[pl.ds(base, GROUP), :]
        conv_act = conv_in[pl.ds(base, GROUP), :]
        drive = step * conv_act
        states = list(states)
        for half in range(GROUP // 8):
            tiles = [[] for _ in range(blocks)]
            for i in range(half * 8, half * 8 + 8):
                spot = pl.ds(pl.multiple_of((base + i) * 16, 16), 16)
                b_tile = b_wide[spot, :]
                c_tile = c_wide[spot, :]
                for k in range(blocks):
                    lanes = slice(k * LANES, (k + 1) * LANES)
                    states[k] = (
                        jnp.exp2(step[i : i + 1, lanes] * rate[k]) * states[k]
                        + b_tile * drive[i : i + 1, lanes]
                    )
                    read = c_tile * states[k]
                    tiles[k].append(read[0:8] + read[8:16])
            for k in range(blocks):
                scanned[
                    pl.ds(pl.multiple_of(base + half * 8, 8), 8), k * LANES : (k + 1) * LANES
                ] = fold_rows(tiles[k])
        gate = gate_in[pl.ds(base, GROUP), :].astype(jnp.float32)
        mixed = scanned[pl.ds(base, GROUP), :] + skip[...] * conv_act
        gated[pl.ds(base, GROUP), :] = (mixed * silu(gate)).astype(gated.dtype)
        return tuple(states)

    states = lax.fori_loop(0, tokens // GROUP, group, tuple(start))
    for k in range(blocks):
        leaving[:, k * LANES : (k + 1) * LANES] = states[k]


def read_out(
    me, chunk, chunks, step, conv_act, gate_in, decay_log, skip, b_wide, c_wide, entering, ends,
    after=(),
):
    tokens, channels = step.shape
    tokens = tokens // chunks
    width = 1024
    some = pl.BlockSpec((tokens, width), lambda j, me: (chunk, j))
    rows = lambda n: pl.BlockSpec((n, width), lambda j, me: (0, j))
    wide = pl.BlockSpec((tokens * 16, LANES), lambda j, me: (chunk, 0))
    masks = [mask for mask, _, _ in ends]
    scratch = [pltpu.VMEM((tokens, BLOCK), jnp.float32)]
    if ends:
        scratch.append(pltpu.VMEM((len(ends), STATE_ROWS, BLOCK), jnp.float32))
    split = [0] + [1] * 5 + [0, 0, 1] + [1] * len(ends) + [1, 1] + [0] * len(scratch)
    return launch(
        functools.partial(by_blocks, functools.partial(readout_kernel, masks), split),
        [me],
        [step, conv_act, gate_in, decay_log, skip, b_wide, c_wide, entering]
        + [end for _, _, end in ends],
        [some, some, some, rows(16), rows(1), wide, wide, rows(16)]
        + [rows(STATE_ROWS)] * len(ends),
        [rows(tokens), rows(16)],
        [
            jax.ShapeDtypeStruct((tokens, channels), jnp.bfloat16),
            jax.ShapeDtypeStruct((16, channels), jnp.float32),
        ],
        after=after,
        grid=(channels // width,),
        scratch=scratch,
        cost_estimate=cost(
            tokens * channels * 16 * 7, tokens * channels * 12, tokens * channels * 18
        ),
        name="read_out",
    )


def project_kernel(layout, me, weight, *refs):
    parts, (out, held, sems) = refs[: len(layout)], refs[len(layout) :]
    rows = held.shape[0] // (1 + max(mask for mask, _ in layout))

    @pl.when(pl.program_id(0) == 0)
    def _():
        copies = []
        for place, (mask, column) in enumerate(layout):
            part = parts[place]
            owner = me[0] ^ mask
            copies.append(
                pltpu.make_async_copy(
                    part,
                    held.at[
                        pl.ds(pl.multiple_of(owner * rows, rows), rows),
                        pl.ds(column, part.shape[1]),
                    ],
                    sems.at[place],
                )
            )
        for copy in copies:
            copy.start()
        for copy in copies:
            copy.wait()

    out[...] = jnp.dot(held[...], weight[...], preferred_element_type=jnp.float32).astype(
        out.dtype
    )


def project(me, parts, weight, after=()):
    depth, columns = weight.shape
    rows = parts[0][2].shape[0]
    total = rows * lax.axis_size("ctx")
    layout = [(mask, (which or 0) * depth // 2) for mask, which, _ in parts]
    tile = min(256, columns)
    return launch(
        functools.partial(project_kernel, layout),
        [me],
        [weight] + [part for _, _, part in parts],
        [pl.BlockSpec((depth, tile), lambda j, me: (0, j))] + [ANY] * len(parts),
        pl.BlockSpec((total, tile), lambda j, me: (0, j)),
        jax.ShapeDtypeStruct((total, columns), jnp.bfloat16),
        after=after,
        grid=(columns // tile,),
        scratch=[
            pltpu.VMEM((total, depth), jnp.bfloat16),
            pltpu.SemaphoreType.DMA((len(parts),)),
        ],
        limit=40,
        cost_estimate=cost(
            2 * total * depth * columns, 2 * (total * depth + depth * columns + total * columns)
        ),
        name="project",
    )


def hidden_kernel(layout, me, gain, gate_rows, up_rows, *refs):
    parts, (out, held, total, squares, sems) = refs[: len(layout)], refs[len(layout) :]
    turn = pl.program_id(0)

    def copy_of(place):
        mask, row = layout[place]
        part = parts[place]
        column = ((me[0] ^ mask) & 1) * part.shape[1]
        return pltpu.make_async_copy(
            part,
            held.at[
                mask // 2,
                pl.ds(row, part.shape[0]),
                pl.ds(pl.multiple_of(column, LANES), part.shape[1]),
            ],
            sems.at[place],
        )

    @pl.when(turn == 0)
    def _():
        for place in range(len(layout)):
            copy_of(place).start()
        total[...] = jnp.zeros_like(total)
        squares[...] = jnp.zeros_like(squares)

    for place, (mask, _) in enumerate(layout):

        @pl.when(turn == mask // 2)
        def _():
            copy_of(place).wait()

    width = out.shape[1]
    both = jnp.concatenate([gate_rows[...], up_rows[...]], axis=1)
    total[...] += jnp.dot(held[turn], both, preferred_element_type=jnp.float32)
    slots = out.shape[0]
    for row in range(0, slots, 64):
        mixer_square = squares[row : row + 64, :]
        for lane in range(0, held.shape[2], LANES):
            value = held[turn, row : row + 64, lane : lane + LANES].astype(jnp.float32)
            spot = lane % gain.shape[2]
            value = value * gain[lane // gain.shape[2], :, spot : spot + LANES]
            mixer_square += value * value
        squares[row : row + 64, :] = mixer_square

    @pl.when(turn == pl.num_programs(0) - 1)
    def _():
        def finish(index, _):
            spot = pl.ds(pl.multiple_of(index * 64, 64), 64)
            mean = jnp.sum(squares[spot, :], axis=1, keepdims=True) / D
            factor = lax.rsqrt(mean + 1e-05)
            gate_act = total[spot, 0:width] * factor
            up_act = total[spot, width:] * factor
            out[spot, :] = (silu(gate_act) * up_act).astype(out.dtype)
            return 0

        lax.fori_loop(0, out.shape[0] // 64, finish, 0)


def hidden_units(me, groups, one_over_gain, gate, up, after=()):
    depth = groups[0][0][2].shape[1]
    count = lax.axis_size("ctx")
    width = gate.shape[1]
    layout, parts, slots = [], [], 0
    for group in groups:
        rows = group[0][2].shape[0]
        layout += [(mask, slots + (which or 0) * rows // 2) for mask, which, _ in group]
        parts += group
        slots += rows
    block = pl.BlockSpec((2 * depth, width), lambda k, me: ((me[0] // 2) ^ k, 0))
    return launch(
        functools.partial(hidden_kernel, layout),
        [me],
        [one_over_gain, gate, up] + [part for _, _, part in parts],
        [
            pl.BlockSpec((2, 1, depth), lambda k, me: ((me[0] // 2) ^ k, 0, 0)),
            block,
            block,
        ] + [ANY] * len(parts),
        pl.BlockSpec((slots, width), lambda k, me: (0, 0)),
        jax.ShapeDtypeStruct((slots, width), jnp.bfloat16),
        after=after,
        grid=(count // 2,),
        scratch=[
            pltpu.VMEM((count // 2, slots, 2 * depth), jnp.bfloat16),
            pltpu.VMEM((slots, 2 * width), jnp.float32),
            pltpu.VMEM((slots, LANES), jnp.float32),
            pltpu.SemaphoreType.DMA((len(parts),)),
        ],
        limit=40,
        cost_estimate=cost(
            4 * slots * depth * count * width, 2 * count * depth * (slots + 2 * width)
        ),
        name="hidden_units",
    )


def down_kernel(layout, me, *refs):
    count = len(layout)
    units, weights, (out, held, sems) = refs[:count], refs[count:-3], refs[-3:]
    width = weights[0].shape[0]

    @pl.when(pl.program_id(0) == 0)
    def _():
        copies = []
        for place, (mask, row) in enumerate(layout):
            unit = units[place]
            copies.append(
                pltpu.make_async_copy(
                    unit,
                    held.at[pl.ds(row, unit.shape[0]), pl.ds(mask * width, width)],
                    sems.at[place],
                )
            )
        for copy in copies:
            copy.start()
        for copy in copies:
            copy.wait()

    tall = jnp.concatenate([weight[...] for weight in weights], axis=0)
    out[...] = jnp.dot(held[...], tall, preferred_element_type=jnp.float32).astype(out.dtype)


def down(me, parts, weights, own, after=()):
    columns = weights[-1].shape[1]
    width = own.shape[0]
    depth = width * len(weights)
    slots = parts[0][2].shape[0]
    tile = min(256, columns)
    layout = [(mask, (which or 0) * slots // 2) for mask, which, _ in parts]
    units = [part for _, _, part in parts]
    steps = columns // tile
    return launch(
        functools.partial(down_kernel, layout),
        [me],
        units + [own] + list(weights[1:]),
        [ANY] * len(units)
        + [pl.BlockSpec((width, tile), lambda j, me: (0, me[0] * steps + j))]
        + [pl.BlockSpec((width, tile), lambda j, me: (0, j))] * (len(weights) - 1),
        pl.BlockSpec((slots, tile), lambda j, me: (0, j)),
        jax.ShapeDtypeStruct((slots, columns), jnp.bfloat16),
        after=after,
        grid=(steps,),
        scratch=[
            pltpu.VMEM((slots, depth), jnp.bfloat16),
            pltpu.SemaphoreType.DMA((len(units),)),
        ],
        limit=40,
        cost_estimate=cost(
            2 * slots * depth * columns, 2 * (slots * depth + depth * columns + slots * columns)
        ),
        name="down",
    )


def cross_kernel(me, *refs):
    units, (own, *sent), refs = refs[:6], refs[6:12], refs[12:]
    keep, give_a, give_b, held, sems = refs
    width = own.shape[0]
    turn = pl.program_id(0)

    @pl.when(turn == 0)
    def _():
        copies = []
        for mask, unit in enumerate(units):
            column = (2, 3, 0, 1, 4, 5)[mask] * width
            copies.append(
                pltpu.make_async_copy(unit, held.at[:, pl.ds(column, width)], sems.at[mask])
            )
        for copy in copies:
            copy.start()
        for copy in copies:
            copy.wait()

    def summed(first, weights):
        tall = jnp.concatenate([weight[...] for weight in weights], axis=0)
        rows = held[:, first * width : (first + 4) * width]
        return jnp.dot(rows, tall, preferred_element_type=jnp.float32).astype(keep.dtype)

    for step, out in enumerate((keep, give_a, keep, give_b)):

        @pl.when(turn == step)
        def _():
            if step < 2:
                out[...] = summed(0, [sent[1], sent[2], own, sent[0]])
            else:
                out[...] = summed(2, [own, sent[0], sent[3], sent[4]])


def cross_down(me, units, weights, own, after=()):
    width = own.shape[0]
    half = weights[2].shape[1] // 2
    slots = units[0].shape[0]

    def mine(j, me):
        return (0, (me[0] ^ (jnp.where(j == 1, 4, 0) + jnp.where(j == 3, 2, 0))) * 2 + j // 2)

    front = pl.BlockSpec((width, half), lambda j, me: (0, jnp.minimum(j, 1)))
    back = pl.BlockSpec((width, half), lambda j, me: (0, jnp.maximum(j - 2, 0)))
    given = pl.BlockSpec((slots, half), lambda j, me: (0, 0))
    return launch(
        cross_kernel,
        [me],
        [units[mask] for mask in range(6)] + [own] + [weights[mask] for mask in range(1, 6)],
        [ANY] * 6
        + [
            pl.BlockSpec((width, half), mine),
            pl.BlockSpec((width, half), lambda j, me: (0, j)),
            front,
            front,
            back,
            back,
        ],
        [pl.BlockSpec((slots, half), lambda j, me: (0, j // 2)), given, given],
        [
            jax.ShapeDtypeStruct((slots, 2 * half), jnp.bfloat16),
            jax.ShapeDtypeStruct((slots, half), jnp.bfloat16),
            jax.ShapeDtypeStruct((slots, half), jnp.bfloat16),
        ],
        after=after,
        grid=(4,),
        scratch=[
            pltpu.VMEM((slots, 6 * width), jnp.bfloat16),
            pltpu.SemaphoreType.DMA((6,)),
        ],
        limit=40,
        cost_estimate=cost(16 * slots * 4 * width * half, 24 * width * half * 2),
        name="cross_down",
    )


def settle_kernel(keep, first, second, *outs):
    half = first.shape[1]
    rows = outs[0].shape[0]
    for place, out in enumerate(outs):
        spot = slice(place * rows, (place + 1) * rows)
        for column, other in ((0, first), (half, second)):
            total = keep[spot, column : column + half].astype(jnp.float32)
            out[:, column : column + half] = (
                total + other[spot, :].astype(jnp.float32)
            ).astype(out.dtype)


def settle(keep, first, second, count, after=()):
    slots, columns = keep.shape
    whole = lambda array: pl.BlockSpec(array.shape, lambda j: (0, 0))
    shape = (slots // count, columns)
    return launch(
        settle_kernel,
        [],
        [keep, first, second],
        [whole(keep), whole(first), whole(second)],
        [pl.BlockSpec(shape, lambda j: (0, 0))] * count,
        [jax.ShapeDtypeStruct(shape, keep.dtype)] * count,
        after=after,
        limit=24,
        cost_estimate=cost(2 * keep.size, 6 * keep.size),
        name="settle",
    )


def pick_kernel(count, rows, *refs):
    for picks, out in zip(refs[:count], refs[count:]):
        out[...] = lax.dot_general(
            picks[...], rows[...], (((0,), (0,)), ((), ())), preferred_element_type=jnp.float32
        ).astype(out.dtype)


def pick_rows(picks, rows, after=()):
    shape = (picks[0].shape[1], rows.shape[1])
    whole = lambda shape: pl.BlockSpec(shape, lambda j: (0, 0))
    return launch(
        functools.partial(pick_kernel, len(picks)),
        [],
        [rows] + list(picks),
        [whole(rows.shape)] + [whole(pick.shape) for pick in picks],
        [whole(shape)] * len(picks),
        [jax.ShapeDtypeStruct(shape, rows.dtype)] * len(picks),
        after=after,
        limit=24,
        cost_estimate=cost(2 * rows.size * shape[0] * len(picks), 4 * rows.size),
        name="pick_rows",
    )


def combine_kernel(me, mixer, ids, gates, *refs):
    out = refs[-1]
    count = len(refs) // 2
    total = mixer[...].astype(jnp.float32)
    for mask in range(count):
        named = ids[...] == (me[0] ^ mask)
        gate = jnp.sum(jnp.where(named, gates[...], 0.0), axis=1, keepdims=True)
        total += gate * jnp.dot(
            refs[mask][...], refs[count + mask][...], preferred_element_type=jnp.float32
        )
    out[...] = total.astype(out.dtype)


def combine(me, mixer_out, ids, gates, picks, answers):
    operands = [mixer_out, ids, gates] + list(picks) + list(answers)
    return launch(
        combine_kernel,
        [me],
        operands,
        [pl.BlockSpec(array.shape, lambda j, me: (0, 0)) for array in operands],
        pl.BlockSpec(mixer_out.shape, lambda j, me: (0, 0)),
        jax.ShapeDtypeStruct(mixer_out.shape, jnp.bfloat16),
        cost_estimate=cost(
            2 * mixer_out.size * answers[0].shape[0] * len(answers), 4 * mixer_out.size
        ),
        limit=24,
        name="combine",
    )


def shards(
    mixer_in,
    gate_in,
    delta_in,
    b_proj,
    c_proj,
    conv_kernel,
    conv_bias,
    delta_bias,
    decay_log,
    skip_gain,
    prefix_state,
    prefix_tail,
    out_proj,
    residual,
    norm_gain,
    expert_gate,
    expert_up,
    expert_down,
    expert_ids,
    route_gates,
):
    tokens = mixer_in.shape[0]
    rim = prefix_tail.shape[0]
    ctx_count = lax.axis_size("ctx")
    exp_count = lax.axis_size("exp")
    ctx_me = lax.axis_index("ctx")
    exp_me = lax.axis_index("exp")
    me = ctx_me.astype(jnp.int32).reshape(1)

    rim_rows = from_behind(mixer_in[tokens - rim :], "ctx", 1)
    rim_rows = jnp.where(ctx_me == 0, prefix_tail, rim_rows).astype(jnp.float32)
    rim8 = jnp.pad(rim_rows, ((8 - rim, 0), (0, 0)))

    width = out_proj.shape[1]
    down_rows = expert_down[0]
    down_parts = {}
    crossing = ctx_count == 8

    def send_columns(masks, after=()):
        if crossing:
            layouts = {1: [(1, 0), (5, 0), (1, 1), (3, 1)]}
            layouts.update({mask: [(mask, 0), (mask ^ 4, 0)] for mask in (2, 3)})
            layouts.update({mask: [(mask, 1), (mask ^ 2, 1)] for mask in (4, 5)})
            cuts = cut_columns(me, down_rows, width // 2, [layouts[m] for m in masks], after)
        else:
            cuts = cut_columns(me, down_rows, width, [[(m, 0)] for m in masks], after)
        for mask, cut in zip(masks, cuts):
            down_parts[mask] = swap(cut, "ctx", mask)
        return tuple(down_parts[mask] for mask in masks)

    early = send_columns([2, 4])

    extra, left = [], norm_gain
    for _ in range(3):
        extra.append(lax.reduce_precision(left, 8, 7))
        left = left - extra[-1]
    extra = jnp.concatenate(extra)
    extra = jnp.pad(extra, (0, mixer_in.shape[1] - extra.shape[0]))[None, :]

    wide = lambda proj: jnp.broadcast_to(proj.T[:, :, None], (tokens, 16, LANES)).reshape(
        tokens * 16, LANES
    )
    b_wide, c_wide = wide(b_proj), wide(c_proj)
    step, conv_act, end = local_states(
        mixer_in,
        rim8,
        delta_in,
        conv_kernel,
        conv_bias[None, :],
        delta_bias[None, :],
        decay_log,
        extra,
        b_wide,
    )
    chunks = 2
    state, ends = prefix_state, gather_parts(join([end], early))
    one_over_gain = inverse_gains(me, ends, width)
    gated = []
    for chunk in range(chunks):
        rows, state = read_out(
            me,
            chunk,
            chunks,
            step,
            conv_act,
            gate_in,
            decay_log,
            skip_gain[None, :],
            b_wide,
            c_wide,
            state,
            ends,
        )
        ends = []
        gated.append(rows)
    near = lambda parts: [part for mask, _, part in parts if mask in (2, 4)]
    far = lambda parts: [part for mask, which, part in parts if which is not None][::2]
    scatter = lambda rows: lax.psum_scatter(rows, "exp", scatter_dimension=0, tiled=True)
    front = gather_parts(gated[0], 1, gated[1:])
    late_masks = [3, 5, 1] if crossing else [1, 3] + list(range(5, ctx_count))
    late = send_columns(late_masks, near(front))
    back = gather_parts(gated[1], 1, far(front))
    partial = project(me, front, out_proj, near(back))
    projected = [scatter(partial)]
    partial = project(me, back, out_proj, [partial])
    projected.append(scatter(partial))

    block_rows = residual.shape[0]
    owners = block_rows // tokens
    projected = jnp.stack(
        [piece.reshape(owners, tokens // chunks, width) for piece in projected], axis=1
    ).reshape(block_rows, width)
    mixer_out = (residual.astype(jnp.float32) + projected.astype(jnp.float32)).astype(
        jnp.bfloat16
    )
    mixer_wide = mixer_out.astype(jnp.float32)
    scaled = (mixer_wide * norm_gain[None, :]).astype(jnp.bfloat16)
    experts = expert_gate.shape[0] * exp_count
    capacity = 3 * block_rows * expert_ids.shape[1] // (2 * experts)
    spots = jnp.arange(capacity, dtype=jnp.int32)
    picked = []
    for mask in range(exp_count):
        here = jnp.any(expert_ids == (exp_me ^ mask), axis=1)
        place = jnp.cumsum(here.astype(jnp.int32)) - 1
        pick = here[:, None] & (place[:, None] == spots[None, :])
        picked.append(pick.astype(jnp.bfloat16))

    groups = [[0, 1], [2, 3]] if exp_count == 4 else [list(range(exp_count))]
    sent = pick_rows(picked, scaled, late)
    pieces = [rows if mask == 0 else swap(rows, "exp", mask) for mask, rows in enumerate(sent)]
    hiddens, after, order = [], (), ()
    for group in groups:
        parts = gather_parts(join([pieces[mask] for mask in group], after), 0, order)
        after = near(parts)
        hidden = hidden_units(me, [parts], one_over_gain, expert_gate[0], expert_up[0])
        order = [hidden]
        hiddens.append(hidden)
    answers, order = {}, []
    weights = [None] + [down_parts[mask] for mask in sorted(down_parts)]
    settled = []
    for group, hidden in zip(groups, hiddens):
        rows = hidden if group is groups[-1] else join([hidden], far(parts))
        if crossing:
            units = {0: rows, 2: swap(rows, "ctx", 2), 4: swap(rows, "ctx", 4)}
            units.update({mask + 1: swap(units[mask], "ctx", 1) for mask in (0, 2, 4)})
            keep, first, second = cross_down(me, units, weights, down_rows, order)
            order = [keep]
            settled.append((keep, swap(first, "ctx", 4), swap(second, "ctx", 2)))
        else:
            answer = down(me, gather_parts(rows), weights, down_rows, order)
            order = [answer]
            settled.append([answer])
    for group, sums in zip(groups, settled):
        if crossing:
            pieces = settle(*sums, len(group), order)
        else:
            pieces = jnp.split(sums[0], len(group))
        for mask, piece in zip(group, pieces):
            answers[mask] = piece if mask == 0 else swap(piece, "exp", mask)
    block_out = combine(
        exp_me.astype(jnp.int32).reshape(1),
        mixer_out,
        expert_ids,
        route_gates,
        picked,
        [answers[mask] for mask in range(exp_count)],
    )
    return (mixer_out, block_out)


def solution(mesh):
    placed = (
        P("ctx", "exp"),
        P("ctx", "exp"),
        P("ctx", "exp"),
        P(None, "ctx"),
        P(None, "ctx"),
        P(None, "exp"),
        P("exp"),
        P("exp"),
        P(None, "exp"),
        P("exp"),
        P(None, "exp"),
        P(None, "exp"),
        P("exp", "ctx"),
        P("exp", "ctx"),
        P("ctx"),
        P("exp", None, "ctx"),
        P("exp", None, "ctx"),
        P("exp", "ctx", None),
        P("exp", None),
        P("exp", None),
    )
    return jax.shard_map(
        shards,
        mesh=mesh,
        in_specs=placed,
        out_specs=(P("exp", "ctx"), P("exp", "ctx")),
        check_vma=False,
    )
```

```python
import functools

import jax
import jax.numpy as jnp
from jax import lax
from jax.experimental import pallas as pl
from jax.experimental.pallas import tpu as pltpu
from jax.sharding import PartitionSpec as P

D = 8192
LOG2E = 1.4426950408889634
LANES = 128
MIB = 1 << 20


def from_behind(array, axis, by):
    length = lax.axis_size(axis)
    pairs = [(i, i + by) for i in range(length) if 0 <= i + by < length]
    return lax.ppermute(array, axis, pairs)


def swap(array, axis, mask):
    return lax.ppermute(array, axis, [(i, i ^ mask) for i in range(lax.axis_size(axis))])


def halves_kernel(split_dim, first, second, low, high):
    half = low.shape[split_dim]
    if split_dim == 0:
        low[...] = first[0:half, :]
        high[...] = second[half:, :]
    else:
        low[...] = first[:, 0:half]
        high[...] = second[:, half:]


def halves(first, second, split_dim, after=()):
    shape = list(first.shape)
    shape[split_dim] //= 2
    whole = pl.BlockSpec(first.shape, lambda j: (0, 0))
    part = pl.BlockSpec(tuple(shape), lambda j: (0, 0))
    return launch(
        functools.partial(halves_kernel, split_dim),
        [],
        [first, second],
        [whole, whole],
        [part, part],
        [jax.ShapeDtypeStruct(tuple(shape), first.dtype)] * 2,
        after=after,
        limit=16,
        cost_estimate=cost(0, 6 * first.size),
        name="halves",
    )


def gather_parts(array, split_dim=None, after=()):
    count = lax.axis_size("ctx")
    if count != 8:
        return [(0, None, array)] + [(m, None, swap(array, "ctx", m)) for m in range(1, count)]
    over_a = swap(array, "ctx", 2)
    over_b = swap(array, "ctx", 4)
    if split_dim is None:
        crossed = [(6, None, swap(array, "ctx", 6))]
    else:
        low, high = halves(over_a, over_b, split_dim, after)
        crossed = [(6, 0, swap(low, "ctx", 4)), (6, 1, swap(high, "ctx", 2))]
    parts = []
    for mask, which, part in [(0, None, array), (2, None, over_a), (4, None, over_b)] + crossed:
        parts.append((mask, which, part))
        parts.append((mask + 1, which, swap(part, "ctx", 1)))
    return parts


def silu(value):
    return value / (1.0 + jnp.exp(-value))


def cost(flops, moved, transcendentals=0):
    return pl.CostEstimate(
        flops=int(flops), bytes_accessed=int(moved), transcendentals=int(transcendentals)
    )


ANY = pl.BlockSpec(memory_space=pl.ANY)


def launch(
    kernel, scalars, operands, in_specs, out_specs, out_shape, after=(), grid=(1,), scratch=(),
    limit=56, **rest
):
    taken = len(scalars) + len(operands)

    def body(*refs):
        kernel(*refs[:taken], *refs[taken + len(after) :])

    return pl.pallas_call(
        body,
        grid_spec=pltpu.PrefetchScalarGridSpec(
            num_scalar_prefetch=len(scalars),
            grid=grid,
            in_specs=list(in_specs) + [ANY] * len(after),
            out_specs=out_specs,
            scratch_shapes=list(scratch),
        ),
        out_shape=out_shape,
        compiler_params=pltpu.CompilerParams(vmem_limit_bytes=limit * MIB),
        **rest,
    )(*scalars, *operands, *after)


def cut_kernel(layout, me, *refs):
    count = sum(len(pieces) for pieces in layout)
    sources, outs = iter(refs[:count]), refs[count:]
    for pieces, out in zip(layout, outs):
        width = out.shape[1] // len(pieces)
        for place in range(len(pieces)):
            out[:, place * width : (place + 1) * width] = next(sources)[...]


def cut_columns(me, rows, width, layout, after=()):
    step = rows.shape[0] // 3
    parts = rows.shape[1] // lax.axis_size("ctx") // width

    def block(mask, part):
        return pl.BlockSpec((step, width), lambda i, me: (i, (me[0] ^ mask) * parts + part))

    flat = [piece for pieces in layout for piece in pieces]
    widths = [width * len(pieces) for pieces in layout]
    return launch(
        functools.partial(cut_kernel, layout),
        [me],
        [rows] * len(flat),
        [block(*piece) for piece in flat],
        [pl.BlockSpec((step, wide), lambda i, me: (i, 0)) for wide in widths],
        [jax.ShapeDtypeStruct((rows.shape[0], wide), rows.dtype) for wide in widths],
        after=after,
        grid=(3,),
        cost_estimate=cost(0, 4 * rows.shape[0] * width * len(flat)),
        name="cut_columns",
    )


def join_kernel(count, *refs):
    pieces, out, sems = refs[:count], refs[count], refs[count + 1]
    copies, row = [], 0
    for place, piece in enumerate(pieces):
        copies.append(
            pltpu.make_async_copy(piece, out.at[pl.ds(row, piece.shape[0]), :], sems.at[place])
        )
        row += piece.shape[0]
    for copy in copies:
        copy.start()
    for copy in copies:
        copy.wait()


def join(pieces, after=()):
    rows = sum(piece.shape[0] for piece in pieces)
    columns = pieces[0].shape[1]
    return launch(
        functools.partial(join_kernel, len(pieces)),
        [],
        list(pieces),
        [ANY] * len(pieces),
        pl.BlockSpec((rows, columns), lambda j: (0, 0)),
        jax.ShapeDtypeStruct((rows, columns), pieces[0].dtype),
        after=after,
        scratch=[pltpu.SemaphoreType.DMA((len(pieces),))],
        limit=16,
        cost_estimate=cost(0, 4 * rows * columns),
        name="join",
    )


BLOCK = 512


def by_blocks(kernel, split, *refs):
    width = next(ref for ref, cut in zip(refs, split) if cut).shape[1]

    def one(index, _):
        lanes = pl.ds(pl.multiple_of(index * BLOCK, BLOCK), BLOCK)
        kernel(*[ref.at[:, lanes] if cut else ref for ref, cut in zip(refs, split)])
        return 0

    lax.fori_loop(0, width // BLOCK, one, 0)


GROUP = 16
STATE_ROWS = 32


def state_kernel(
    mixer, rim, delta, kernel, bias, delta_bias, decay_log, extra, b_wide, step_out, conv_out,
    end_out, padded,
):
    tokens, width = mixer.shape
    blocks = width // LANES
    padded[0:8, :] = rim[...]
    padded[8:, :] = mixer[...].astype(jnp.float32)
    rate = [
        -jnp.exp(decay_log[:, k * LANES : (k + 1) * LANES]) * LOG2E for k in range(blocks)
    ]
    taps = kernel.shape[0]

    def group(index, carry):
        states, total = carry
        base = pl.multiple_of(index * GROUP, GROUP)
        window = padded[pl.ds(base, GROUP + 8), :]
        convolved = bias[...] + sum(
            kernel[k : k + 1, :] * window[9 - taps + k : 9 - taps + k + GROUP, :]
            for k in range(taps)
        )
        conv_act = silu(convolved)
        step = jnp.log(
            1.0 + jnp.exp(delta[pl.ds(base, GROUP), :].astype(jnp.float32) + delta_bias[...])
        )
        step_out[pl.ds(base, GROUP), :] = step
        conv_out[pl.ds(base, GROUP), :] = conv_act
        drive = step * conv_act
        states = list(states)
        for i in range(GROUP):
            b_tile = b_wide[pl.ds(pl.multiple_of((base + i) * 16, 16), 16), :]
            for k in range(blocks):
                lanes = slice(k * LANES, (k + 1) * LANES)
                states[k] = (
                    jnp.exp2(step[i : i + 1, lanes] * rate[k]) * states[k]
                    + b_tile * drive[i : i + 1, lanes]
                )
        return tuple(states), total + step[0:8, :] + step[8:16, :]

    start = tuple(jnp.zeros((16, LANES), jnp.float32) for _ in range(blocks))
    states, total = lax.fori_loop(
        0, tokens // GROUP, group, (start, jnp.zeros((8, width), jnp.float32))
    )
    for k in range(blocks):
        end_out[0:16, k * LANES : (k + 1) * LANES] = states[k].astype(end_out.dtype)
    total = jnp.sum(total, axis=0, keepdims=True)
    place = lax.broadcasted_iota(jnp.int32, (16, width), 0)
    pieces = jnp.where(place == 3, extra[...], 0.0)
    for row in range(3):
        piece = total.astype(jnp.bfloat16).astype(jnp.float32)
        pieces = jnp.where(place == row, piece, pieces)
        total = total - piece
    end_out[16:32, :] = pieces.astype(end_out.dtype)


def local_states(mixer_in, rim8, delta_in, kernel, bias, delta_bias, decay_log, extra, b_wide):
    tokens, channels = mixer_in.shape
    width = 1024
    rows = lambda n: pl.BlockSpec((n, width), lambda j: (0, j))
    return launch(
        functools.partial(by_blocks, state_kernel, [1] * 8 + [0] + [1] * 3 + [0]),
        [],
        [mixer_in, rim8, delta_in, kernel, bias, delta_bias, decay_log, extra, b_wide],
        [
            rows(tokens),
            rows(8),
            rows(tokens),
            rows(kernel.shape[0]),
            rows(1),
            rows(1),
            rows(16),
            rows(1),
            pl.BlockSpec((tokens * 16, LANES), lambda j: (0, 0)),
        ],
        [rows(tokens), rows(tokens), rows(STATE_ROWS)],
        [
            jax.ShapeDtypeStruct((tokens, channels), jnp.float32),
            jax.ShapeDtypeStruct((tokens, channels), jnp.float32),
            jax.ShapeDtypeStruct((STATE_ROWS, channels), jnp.bfloat16),
        ],
        grid=(channels // width,),
        scratch=[pltpu.VMEM((tokens + 8, BLOCK), jnp.float32)],
        cost_estimate=cost(
            tokens * channels * 16 * 5, tokens * channels * 12, tokens * channels * 18
        ),
        name="local_states",
    )


def gains_kernel(masks, me, *refs):
    parts, out = refs[: len(masks)], refs[-1]
    width = out.shape[2]
    for mask, part in zip(masks, parts):
        row = part[...].astype(jnp.float32)[3:4, :]
        gain = row[:, 0:width] + row[:, width : 2 * width] + row[:, 2 * width : 3 * width]
        out[me[0] ^ mask] = 1.0 / gain


def inverse_gains(me, ends, width):
    return launch(
        functools.partial(gains_kernel, [mask for mask, _, _ in ends]),
        [me],
        [end for _, _, end in ends],
        [pl.BlockSpec((16, 3 * width), lambda j, me: (1, 0))] * len(ends),
        pl.BlockSpec((len(ends), 1, width), lambda j, me: (0, 0, 0)),
        jax.ShapeDtypeStruct((len(ends), 1, width), jnp.float32),
        limit=16,
        name="inverse_gains",
    )


def fold_rows(tiles):
    place = lax.broadcasted_iota(jnp.int32, (8, LANES), 0)
    for shift in (1, 2, 4):
        first = (place & shift) == 0
        tiles = [
            jnp.where(first, a, b) + pltpu.roll(jnp.where(first, b, a), shift, 0)
            for a, b in zip(tiles[0::2], tiles[1::2])
        ]
    return tiles[0]


def readout_kernel(
    masks, me, step_in, conv_in, gate_in, decay_log, skip, b_wide, c_wide, entering, *refs
):
    ends = refs[: len(masks)]
    gated, leaving, scanned = refs[len(masks) : len(masks) + 3]
    tokens, width = step_in.shape
    blocks = width // LANES
    rate = [
        -jnp.exp(decay_log[:, k * LANES : (k + 1) * LANES]) * LOG2E for k in range(blocks)
    ]
    start = [entering[:, k * LANES : (k + 1) * LANES] for k in range(blocks)]
    if masks:
        held = refs[-1]
        for mask, end in zip(masks, ends):
            held[mask] = end[...].astype(jnp.float32)
        for owner in range(len(masks) - 1):
            end = held[me[0] ^ owner]
            total = end[16:17, :] + end[17:18, :] + end[18:19, :]
            for k in range(blocks):
                lanes = slice(k * LANES, (k + 1) * LANES)
                later = jnp.exp2(total[:, lanes] * rate[k]) * start[k] + end[0:16, lanes]
                start[k] = jnp.where(owner < me[0], later, start[k])

    def group(index, states):
        base = pl.multiple_of(index * GROUP, GROUP)
        step = step_in[pl.ds(base, GROUP), :]
        conv_act = conv_in[pl.ds(base, GROUP), :]
        drive = step * conv_act
        states = list(states)
        for half in range(GROUP // 8):
            tiles = [[] for _ in range(blocks)]
            for i in range(half * 8, half * 8 + 8):
                spot = pl.ds(pl.multiple_of((base + i) * 16, 16), 16)
                b_tile = b_wide[spot, :]
                c_tile = c_wide[spot, :]
                for k in range(blocks):
                    lanes = slice(k * LANES, (k + 1) * LANES)
                    states[k] = (
                        jnp.exp2(step[i : i + 1, lanes] * rate[k]) * states[k]
                        + b_tile * drive[i : i + 1, lanes]
                    )
                    read = c_tile * states[k]
                    tiles[k].append(read[0:8] + read[8:16])
            for k in range(blocks):
                scanned[
                    pl.ds(pl.multiple_of(base + half * 8, 8), 8), k * LANES : (k + 1) * LANES
                ] = fold_rows(tiles[k])
        gate = gate_in[pl.ds(base, GROUP), :].astype(jnp.float32)
        mixed = scanned[pl.ds(base, GROUP), :] + skip[...] * conv_act
        gated[pl.ds(base, GROUP), :] = (mixed * silu(gate)).astype(gated.dtype)
        return tuple(states)

    states = lax.fori_loop(0, tokens // GROUP, group, tuple(start))
    for k in range(blocks):
        leaving[:, k * LANES : (k + 1) * LANES] = states[k]


def read_out(
    me, chunk, chunks, step, conv_act, gate_in, decay_log, skip, b_wide, c_wide, entering, ends,
    after=(),
):
    tokens, channels = step.shape
    tokens = tokens // chunks
    width = 1024
    some = pl.BlockSpec((tokens, width), lambda j, me: (chunk, j))
    rows = lambda n: pl.BlockSpec((n, width), lambda j, me: (0, j))
    wide = pl.BlockSpec((tokens * 16, LANES), lambda j, me: (chunk, 0))
    masks = [mask for mask, _, _ in ends]
    scratch = [pltpu.VMEM((tokens, BLOCK), jnp.float32)]
    if ends:
        scratch.append(pltpu.VMEM((len(ends), STATE_ROWS, BLOCK), jnp.float32))
    split = [0] + [1] * 5 + [0, 0, 1] + [1] * len(ends) + [1, 1] + [0] * len(scratch)
    return launch(
        functools.partial(by_blocks, functools.partial(readout_kernel, masks), split),
        [me],
        [step, conv_act, gate_in, decay_log, skip, b_wide, c_wide, entering]
        + [end for _, _, end in ends],
        [some, some, some, rows(16), rows(1), wide, wide, rows(16)]
        + [rows(STATE_ROWS)] * len(ends),
        [rows(tokens), rows(16)],
        [
            jax.ShapeDtypeStruct((tokens, channels), jnp.bfloat16),
            jax.ShapeDtypeStruct((16, channels), jnp.float32),
        ],
        after=after,
        grid=(channels // width,),
        scratch=scratch,
        cost_estimate=cost(
            tokens * channels * 16 * 7, tokens * channels * 12, tokens * channels * 18
        ),
        name="read_out",
    )


def project_kernel(layout, me, weight, *refs):
    parts, (out, held, sems) = refs[: len(layout)], refs[len(layout) :]
    rows = held.shape[0] // (1 + max(mask for mask, _ in layout))

    @pl.when(pl.program_id(0) == 0)
    def _():
        copies = []
        for place, (mask, column) in enumerate(layout):
            part = parts[place]
            owner = me[0] ^ mask
            copies.append(
                pltpu.make_async_copy(
                    part,
                    held.at[
                        pl.ds(pl.multiple_of(owner * rows, rows), rows),
                        pl.ds(column, part.shape[1]),
                    ],
                    sems.at[place],
                )
            )
        for copy in copies:
            copy.start()
        for copy in copies:
            copy.wait()

    out[...] = jnp.dot(held[...], weight[...], preferred_element_type=jnp.float32).astype(
        out.dtype
    )


def project(me, parts, weight, after=()):
    depth, columns = weight.shape
    rows = parts[0][2].shape[0]
    total = rows * lax.axis_size("ctx")
    layout = [(mask, (which or 0) * depth // 2) for mask, which, _ in parts]
    tile = min(256, columns)
    return launch(
        functools.partial(project_kernel, layout),
        [me],
        [weight] + [part for _, _, part in parts],
        [pl.BlockSpec((depth, tile), lambda j, me: (0, j))] + [ANY] * len(parts),
        pl.BlockSpec((total, tile), lambda j, me: (0, j)),
        jax.ShapeDtypeStruct((total, columns), jnp.bfloat16),
        after=after,
        grid=(columns // tile,),
        scratch=[
            pltpu.VMEM((total, depth), jnp.bfloat16),
            pltpu.SemaphoreType.DMA((len(parts),)),
        ],
        limit=40,
        cost_estimate=cost(
            2 * total * depth * columns, 2 * (total * depth + depth * columns + total * columns)
        ),
        name="project",
    )


def hidden_kernel(layout, me, gain, gate_rows, up_rows, *refs):
    parts, (out, held, total, squares, sems) = refs[: len(layout)], refs[len(layout) :]
    turn = pl.program_id(0)

    def copy_of(place):
        mask, row = layout[place]
        part = parts[place]
        column = ((me[0] ^ mask) & 1) * part.shape[1]
        return pltpu.make_async_copy(
            part,
            held.at[
                mask // 2,
                pl.ds(row, part.shape[0]),
                pl.ds(pl.multiple_of(column, LANES), part.shape[1]),
            ],
            sems.at[place],
        )

    @pl.when(turn == 0)
    def _():
        for place in range(len(layout)):
            copy_of(place).start()
        total[...] = jnp.zeros_like(total)
        squares[...] = jnp.zeros_like(squares)

    for place, (mask, _) in enumerate(layout):

        @pl.when(turn == mask // 2)
        def _():
            copy_of(place).wait()

    width = out.shape[1]
    both = jnp.concatenate([gate_rows[...], up_rows[...]], axis=1)
    total[...] += jnp.dot(held[turn], both, preferred_element_type=jnp.float32)
    slots = out.shape[0]
    for row in range(0, slots, 64):
        mixer_square = squares[row : row + 64, :]
        for lane in range(0, held.shape[2], LANES):
            value = held[turn, row : row + 64, lane : lane + LANES].astype(jnp.float32)
            spot = lane % gain.shape[2]
            value = value * gain[lane // gain.shape[2], :, spot : spot + LANES]
            mixer_square += value * value
        squares[row : row + 64, :] = mixer_square

    @pl.when(turn == pl.num_programs(0) - 1)
    def _():
        def finish(index, _):
            spot = pl.ds(pl.multiple_of(index * 64, 64), 64)
            mean = jnp.sum(squares[spot, :], axis=1, keepdims=True) / D
            factor = lax.rsqrt(mean + 1e-05)
            gate_act = total[spot, 0:width] * factor
            up_act = total[spot, width:] * factor
            out[spot, :] = (silu(gate_act) * up_act).astype(out.dtype)
            return 0

        lax.fori_loop(0, out.shape[0] // 64, finish, 0)


def hidden_units(me, groups, one_over_gain, gate, up, after=()):
    depth = groups[0][0][2].shape[1]
    count = lax.axis_size("ctx")
    width = gate.shape[1]
    layout, parts, slots = [], [], 0
    for group in groups:
        rows = group[0][2].shape[0]
        layout += [(mask, slots + (which or 0) * rows // 2) for mask, which, _ in group]
        parts += group
        slots += rows
    block = pl.BlockSpec((2 * depth, width), lambda k, me: ((me[0] // 2) ^ k, 0))
    return launch(
        functools.partial(hidden_kernel, layout),
        [me],
        [one_over_gain, gate, up] + [part for _, _, part in parts],
        [
            pl.BlockSpec((2, 1, depth), lambda k, me: ((me[0] // 2) ^ k, 0, 0)),
            block,
            block,
        ] + [ANY] * len(parts),
        pl.BlockSpec((slots, width), lambda k, me: (0, 0)),
        jax.ShapeDtypeStruct((slots, width), jnp.bfloat16),
        after=after,
        grid=(count // 2,),
        scratch=[
            pltpu.VMEM((count // 2, slots, 2 * depth), jnp.bfloat16),
            pltpu.VMEM((slots, 2 * width), jnp.float32),
            pltpu.VMEM((slots, LANES), jnp.float32),
            pltpu.SemaphoreType.DMA((len(parts),)),
        ],
        limit=40,
        cost_estimate=cost(
            4 * slots * depth * count * width, 2 * count * depth * (slots + 2 * width)
        ),
        name="hidden_units",
    )


def down_kernel(layout, me, *refs):
    count = len(layout)
    units, weights, (out, held, sems) = refs[:count], refs[count:-3], refs[-3:]
    width = weights[0].shape[0]

    @pl.when(pl.program_id(0) == 0)
    def _():
        copies = []
        for place, (mask, row) in enumerate(layout):
            unit = units[place]
            copies.append(
                pltpu.make_async_copy(
                    unit,
                    held.at[pl.ds(row, unit.shape[0]), pl.ds(mask * width, width)],
                    sems.at[place],
                )
            )
        for copy in copies:
            copy.start()
        for copy in copies:
            copy.wait()

    tall = jnp.concatenate([weight[...] for weight in weights], axis=0)
    out[...] = jnp.dot(held[...], tall, preferred_element_type=jnp.float32).astype(out.dtype)


def down(me, parts, weights, own, after=()):
    columns = weights[-1].shape[1]
    width = own.shape[0]
    depth = width * len(weights)
    slots = parts[0][2].shape[0]
    tile = min(256, columns)
    layout = [(mask, (which or 0) * slots // 2) for mask, which, _ in parts]
    units = [part for _, _, part in parts]
    steps = columns // tile
    return launch(
        functools.partial(down_kernel, layout),
        [me],
        units + [own] + list(weights[1:]),
        [ANY] * len(units)
        + [pl.BlockSpec((width, tile), lambda j, me: (0, me[0] * steps + j))]
        + [pl.BlockSpec((width, tile), lambda j, me: (0, j))] * (len(weights) - 1),
        pl.BlockSpec((slots, tile), lambda j, me: (0, j)),
        jax.ShapeDtypeStruct((slots, columns), jnp.bfloat16),
        after=after,
        grid=(steps,),
        scratch=[
            pltpu.VMEM((slots, depth), jnp.bfloat16),
            pltpu.SemaphoreType.DMA((len(units),)),
        ],
        limit=40,
        cost_estimate=cost(
            2 * slots * depth * columns, 2 * (slots * depth + depth * columns + slots * columns)
        ),
        name="down",
    )


def cross_kernel(me, *refs):
    units, (own, *sent), refs = refs[:6], refs[6:12], refs[12:]
    keep, give_a, give_b, held, sems = refs
    width = own.shape[0]
    turn = pl.program_id(0)

    @pl.when(turn == 0)
    def _():
        copies = []
        for mask, unit in enumerate(units):
            column = (2, 3, 0, 1, 4, 5)[mask] * width
            copies.append(
                pltpu.make_async_copy(unit, held.at[:, pl.ds(column, width)], sems.at[mask])
            )
        for copy in copies:
            copy.start()
        for copy in copies:
            copy.wait()

    def summed(first, weights):
        tall = jnp.concatenate([weight[...] for weight in weights], axis=0)
        rows = held[:, first * width : (first + 4) * width]
        return jnp.dot(rows, tall, preferred_element_type=jnp.float32).astype(keep.dtype)

    for step, out in enumerate((keep, give_a, keep, give_b)):

        @pl.when(turn == step)
        def _():
            if step < 2:
                out[...] = summed(0, [sent[1], sent[2], own, sent[0]])
            else:
                out[...] = summed(2, [own, sent[0], sent[3], sent[4]])


def cross_down(me, units, weights, own, after=()):
    width = own.shape[0]
    half = weights[2].shape[1] // 2
    slots = units[0].shape[0]

    def mine(j, me):
        return (0, (me[0] ^ (jnp.where(j == 1, 4, 0) + jnp.where(j == 3, 2, 0))) * 2 + j // 2)

    front = pl.BlockSpec((width, half), lambda j, me: (0, jnp.minimum(j, 1)))
    back = pl.BlockSpec((width, half), lambda j, me: (0, jnp.maximum(j - 2, 0)))
    given = pl.BlockSpec((slots, half), lambda j, me: (0, 0))
    return launch(
        cross_kernel,
        [me],
        [units[mask] for mask in range(6)] + [own] + [weights[mask] for mask in range(1, 6)],
        [ANY] * 6
        + [
            pl.BlockSpec((width, half), mine),
            pl.BlockSpec((width, half), lambda j, me: (0, j)),
            front,
            front,
            back,
            back,
        ],
        [pl.BlockSpec((slots, half), lambda j, me: (0, j // 2)), given, given],
        [
            jax.ShapeDtypeStruct((slots, 2 * half), jnp.bfloat16),
            jax.ShapeDtypeStruct((slots, half), jnp.bfloat16),
            jax.ShapeDtypeStruct((slots, half), jnp.bfloat16),
        ],
        after=after,
        grid=(4,),
        scratch=[
            pltpu.VMEM((slots, 6 * width), jnp.bfloat16),
            pltpu.SemaphoreType.DMA((6,)),
        ],
        limit=40,
        cost_estimate=cost(16 * slots * 4 * width * half, 24 * width * half * 2),
        name="cross_down",
    )


def settle_kernel(keep, first, second, *outs):
    half = first.shape[1]
    rows = outs[0].shape[0]
    for place, out in enumerate(outs):
        spot = slice(place * rows, (place + 1) * rows)
        for column, other in ((0, first), (half, second)):
            total = keep[spot, column : column + half].astype(jnp.float32)
            out[:, column : column + half] = (
                total + other[spot, :].astype(jnp.float32)
            ).astype(out.dtype)


def settle(keep, first, second, count, after=()):
    slots, columns = keep.shape
    whole = lambda array: pl.BlockSpec(array.shape, lambda j: (0, 0))
    shape = (slots // count, columns)
    return launch(
        settle_kernel,
        [],
        [keep, first, second],
        [whole(keep), whole(first), whole(second)],
        [pl.BlockSpec(shape, lambda j: (0, 0))] * count,
        [jax.ShapeDtypeStruct(shape, keep.dtype)] * count,
        after=after,
        limit=24,
        cost_estimate=cost(2 * keep.size, 6 * keep.size),
        name="settle",
    )


def pick_kernel(count, rows, *refs):
    for picks, out in zip(refs[:count], refs[count:]):
        out[...] = lax.dot_general(
            picks[...], rows[...], (((0,), (0,)), ((), ())), preferred_element_type=jnp.float32
        ).astype(out.dtype)


def pick_rows(picks, rows, after=()):
    shape = (picks[0].shape[1], rows.shape[1])
    whole = lambda shape: pl.BlockSpec(shape, lambda j: (0, 0))
    return launch(
        functools.partial(pick_kernel, len(picks)),
        [],
        [rows] + list(picks),
        [whole(rows.shape)] + [whole(pick.shape) for pick in picks],
        [whole(shape)] * len(picks),
        [jax.ShapeDtypeStruct(shape, rows.dtype)] * len(picks),
        after=after,
        limit=24,
        cost_estimate=cost(2 * rows.size * shape[0] * len(picks), 4 * rows.size),
        name="pick_rows",
    )


def combine_kernel(me, mixer, ids, gates, *refs):
    out = refs[-1]
    count = len(refs) // 2
    total = mixer[...].astype(jnp.float32)
    for mask in range(count):
        named = ids[...] == (me[0] ^ mask)
        gate = jnp.sum(jnp.where(named, gates[...], 0.0), axis=1, keepdims=True)
        total += gate * jnp.dot(
            refs[mask][...], refs[count + mask][...], preferred_element_type=jnp.float32
        )
    out[...] = total.astype(out.dtype)


def combine(me, mixer_out, ids, gates, picks, answers):
    operands = [mixer_out, ids, gates] + list(picks) + list(answers)
    return launch(
        combine_kernel,
        [me],
        operands,
        [pl.BlockSpec(array.shape, lambda j, me: (0, 0)) for array in operands],
        pl.BlockSpec(mixer_out.shape, lambda j, me: (0, 0)),
        jax.ShapeDtypeStruct(mixer_out.shape, jnp.bfloat16),
        cost_estimate=cost(
            2 * mixer_out.size * answers[0].shape[0] * len(answers), 4 * mixer_out.size
        ),
        limit=24,
        name="combine",
    )


def shards(
    mixer_in,
    gate_in,
    delta_in,
    b_proj,
    c_proj,
    conv_kernel,
    conv_bias,
    delta_bias,
    decay_log,
    skip_gain,
    prefix_state,
    prefix_tail,
    out_proj,
    residual,
    norm_gain,
    expert_gate,
    expert_up,
    expert_down,
    expert_ids,
    route_gates,
):
    tokens = mixer_in.shape[0]
    rim = prefix_tail.shape[0]
    ctx_count = lax.axis_size("ctx")
    exp_count = lax.axis_size("exp")
    ctx_me = lax.axis_index("ctx")
    exp_me = lax.axis_index("exp")
    me = ctx_me.astype(jnp.int32).reshape(1)

    rim_rows = from_behind(mixer_in[tokens - rim :], "ctx", 1)
    rim_rows = jnp.where(ctx_me == 0, prefix_tail, rim_rows).astype(jnp.float32)
    rim8 = jnp.pad(rim_rows, ((8 - rim, 0), (0, 0)))

    width = out_proj.shape[1]
    down_rows = expert_down[0]
    down_parts = {}
    crossing = ctx_count == 8

    def send_columns(masks, after=()):
        if crossing:
            layouts = {1: [(1, 0), (5, 0), (1, 1), (3, 1)]}
            layouts.update({mask: [(mask, 0), (mask ^ 4, 0)] for mask in (2, 3)})
            layouts.update({mask: [(mask, 1), (mask ^ 2, 1)] for mask in (4, 5)})
            cuts = cut_columns(me, down_rows, width // 2, [layouts[m] for m in masks], after)
        else:
            cuts = cut_columns(me, down_rows, width, [[(m, 0)] for m in masks], after)
        for mask, cut in zip(masks, cuts):
            down_parts[mask] = swap(cut, "ctx", mask)
        return tuple(down_parts[mask] for mask in masks)

    early = send_columns([2, 4])

    extra, left = [], norm_gain
    for _ in range(3):
        extra.append(lax.reduce_precision(left, 8, 7))
        left = left - extra[-1]
    extra = jnp.concatenate(extra)
    extra = jnp.pad(extra, (0, mixer_in.shape[1] - extra.shape[0]))[None, :]

    wide = lambda proj: jnp.broadcast_to(proj.T[:, :, None], (tokens, 16, LANES)).reshape(
        tokens * 16, LANES
    )
    b_wide, c_wide = wide(b_proj), wide(c_proj)
    step, conv_act, end = local_states(
        mixer_in,
        rim8,
        delta_in,
        conv_kernel,
        conv_bias[None, :],
        delta_bias[None, :],
        decay_log,
        extra,
        b_wide,
    )
    chunks = 2
    state, ends = prefix_state, gather_parts(join([end], early))
    one_over_gain = inverse_gains(me, ends, width)
    gated = []
    for chunk in range(chunks):
        rows, state = read_out(
            me,
            chunk,
            chunks,
            step,
            conv_act,
            gate_in,
            decay_log,
            skip_gain[None, :],
            b_wide,
            c_wide,
            state,
            ends,
        )
        ends = []
        gated.append(rows)
    near = lambda parts: [part for mask, _, part in parts if mask in (2, 4)]
    far = lambda parts: [part for mask, which, part in parts if which is not None][::2]
    scatter = lambda rows: lax.psum_scatter(rows, "exp", scatter_dimension=0, tiled=True)
    front = gather_parts(gated[0], 1, gated[1:])
    late_masks = [3, 5, 1] if crossing else [1, 3] + list(range(5, ctx_count))
    late = send_columns(late_masks, near(front))
    back = gather_parts(gated[1], 1, far(front))
    partial = project(me, front, out_proj, near(back))
    projected = [scatter(partial)]
    partial = project(me, back, out_proj, [partial])
    projected.append(scatter(partial))

    block_rows = residual.shape[0]
    owners = block_rows // tokens
    projected = jnp.stack(
        [piece.reshape(owners, tokens // chunks, width) for piece in projected], axis=1
    ).reshape(block_rows, width)
    mixer_out = (residual.astype(jnp.float32) + projected.astype(jnp.float32)).astype(
        jnp.bfloat16
    )
    mixer_wide = mixer_out.astype(jnp.float32)
    scaled = (mixer_wide * norm_gain[None, :]).astype(jnp.bfloat16)
    experts = expert_gate.shape[0] * exp_count
    capacity = 3 * block_rows * expert_ids.shape[1] // (2 * experts)
    spots = jnp.arange(capacity, dtype=jnp.int32)
    picked = []
    for mask in range(exp_count):
        here = jnp.any(expert_ids == (exp_me ^ mask), axis=1)
        place = jnp.cumsum(here.astype(jnp.int32)) - 1
        pick = here[:, None] & (place[:, None] == spots[None, :])
        picked.append(pick.astype(jnp.bfloat16))

    groups = [[0], list(range(1, exp_count))]
    sent = pick_rows(picked, scaled, late)
    pieces = [rows if mask == 0 else swap(rows, "exp", mask) for mask, rows in enumerate(sent)]
    weights = [None] + [down_parts[mask] for mask in sorted(down_parts)]
    settled, arrived, order = [], (), ()
    for group in groups:
        rows = [pieces[mask] for mask in group]
        rows = join(rows, arrived) if len(group) > 1 else rows[0]
        parts = gather_parts(rows, 0, order)
        arrived = far(parts)
        hidden = hidden_units(me, [parts], one_over_gain, expert_gate[0], expert_up[0])
        if crossing:
            units = {0: hidden, 2: swap(hidden, "ctx", 2), 4: swap(hidden, "ctx", 4)}
            units.update({mask + 1: swap(units[mask], "ctx", 1) for mask in (0, 2, 4)})
            keep, first, second = cross_down(me, units, weights, down_rows)
            order = [keep]
            settled.append((keep, swap(first, "ctx", 4), swap(second, "ctx", 2)))
        else:
            answer = down(me, gather_parts(hidden), weights, down_rows)
            order = [answer]
            settled.append([answer])
    answers = {}
    for group, sums in zip(groups, settled):
        if crossing:
            pieces = settle(*sums, len(group), order)
        else:
            pieces = jnp.split(sums[0], len(group))
        for mask, piece in zip(group, pieces):
            answers[mask] = piece if mask == 0 else swap(piece, "exp", mask)
    block_out = combine(
        exp_me.astype(jnp.int32).reshape(1),
        mixer_out,
        expert_ids,
        route_gates,
        picked,
        [answers[mask] for mask in range(exp_count)],
    )
    return (mixer_out, block_out)


def solution(mesh):
    placed = (
        P("ctx", "exp"),
        P("ctx", "exp"),
        P("ctx", "exp"),
        P(None, "ctx"),
        P(None, "ctx"),
        P(None, "exp"),
        P("exp"),
        P("exp"),
        P(None, "exp"),
        P("exp"),
        P(None, "exp"),
        P(None, "exp"),
        P("exp", "ctx"),
        P("exp", "ctx"),
        P("ctx"),
        P("exp", None, "ctx"),
        P("exp", None, "ctx"),
        P("exp", "ctx", None),
        P("exp", None),
        P("exp", None),
    )
    return jax.shard_map(
        shards,
        mesh=mesh,
        in_specs=placed,
        out_specs=(P("exp", "ctx"), P("exp", "ctx")),
        check_vma=False,
    )
```

```python
import functools

import jax
import jax.numpy as jnp
from jax import lax
from jax.experimental import pallas as pl
from jax.experimental.pallas import tpu as pltpu
from jax.sharding import PartitionSpec as P

D = 8192
LOG2E = 1.4426950408889634
LANES = 128
MIB = 1 << 20


def from_behind(array, axis, by):
    length = lax.axis_size(axis)
    pairs = [(i, i + by) for i in range(length) if 0 <= i + by < length]
    return lax.ppermute(array, axis, pairs)


def swap(array, axis, mask):
    return lax.ppermute(array, axis, [(i, i ^ mask) for i in range(lax.axis_size(axis))])


def halves_kernel(split_dim, first, second, low, high):
    half = low.shape[split_dim]
    if split_dim == 0:
        low[...] = first[0:half, :]
        high[...] = second[half:, :]
    else:
        low[...] = first[:, 0:half]
        high[...] = second[:, half:]


def halves(first, second, split_dim, after=()):
    shape = list(first.shape)
    shape[split_dim] //= 2
    whole = pl.BlockSpec(first.shape, lambda j: (0, 0))
    part = pl.BlockSpec(tuple(shape), lambda j: (0, 0))
    return launch(
        functools.partial(halves_kernel, split_dim),
        [],
        [first, second],
        [whole, whole],
        [part, part],
        [jax.ShapeDtypeStruct(tuple(shape), first.dtype)] * 2,
        after=after,
        limit=16,
        cost_estimate=cost(0, 6 * first.size),
        name="halves",
    )


def gather_parts(array, split_dim=None, after=()):
    count = lax.axis_size("ctx")
    if count != 8:
        return [(0, None, array)] + [(m, None, swap(array, "ctx", m)) for m in range(1, count)]
    over_a = swap(array, "ctx", 2)
    over_b = swap(array, "ctx", 4)
    if split_dim is None:
        crossed = [(6, None, swap(array, "ctx", 6))]
    else:
        low, high = halves(over_a, over_b, split_dim, after)
        crossed = [(6, 0, swap(low, "ctx", 4)), (6, 1, swap(high, "ctx", 2))]
    parts = []
    for mask, which, part in [(0, None, array), (2, None, over_a), (4, None, over_b)] + crossed:
        parts.append((mask, which, part))
        parts.append((mask + 1, which, swap(part, "ctx", 1)))
    return parts


def silu(value):
    return value / (1.0 + jnp.exp(-value))


def cost(flops, moved, transcendentals=0):
    return pl.CostEstimate(
        flops=int(flops), bytes_accessed=int(moved), transcendentals=int(transcendentals)
    )


ANY = pl.BlockSpec(memory_space=pl.ANY)


def launch(
    kernel, scalars, operands, in_specs, out_specs, out_shape, after=(), grid=(1,), scratch=(),
    limit=56, **rest
):
    taken = len(scalars) + len(operands)

    def body(*refs):
        kernel(*refs[:taken], *refs[taken + len(after) :])

    return pl.pallas_call(
        body,
        grid_spec=pltpu.PrefetchScalarGridSpec(
            num_scalar_prefetch=len(scalars),
            grid=grid,
            in_specs=list(in_specs) + [ANY] * len(after),
            out_specs=out_specs,
            scratch_shapes=list(scratch),
        ),
        out_shape=out_shape,
        compiler_params=pltpu.CompilerParams(vmem_limit_bytes=limit * MIB),
        **rest,
    )(*scalars, *operands, *after)


def cut_kernel(layout, me, *refs):
    count = sum(len(pieces) for pieces in layout)
    sources, outs = iter(refs[:count]), refs[count:]
    for pieces, out in zip(layout, outs):
        width = out.shape[1] // len(pieces)
        for place in range(len(pieces)):
            out[:, place * width : (place + 1) * width] = next(sources)[...]


def cut_columns(me, rows, width, layout, after=()):
    step = rows.shape[0] // 3
    parts = rows.shape[1] // lax.axis_size("ctx") // width

    def block(mask, part):
        return pl.BlockSpec((step, width), lambda i, me: (i, (me[0] ^ mask) * parts + part))

    flat = [piece for pieces in layout for piece in pieces]
    widths = [width * len(pieces) for pieces in layout]
    return launch(
        functools.partial(cut_kernel, layout),
        [me],
        [rows] * len(flat),
        [block(*piece) for piece in flat],
        [pl.BlockSpec((step, wide), lambda i, me: (i, 0)) for wide in widths],
        [jax.ShapeDtypeStruct((rows.shape[0], wide), rows.dtype) for wide in widths],
        after=after,
        grid=(3,),
        cost_estimate=cost(0, 4 * rows.shape[0] * width * len(flat)),
        name="cut_columns",
    )


def join_kernel(count, *refs):
    pieces, out, sems = refs[:count], refs[count], refs[count + 1]
    copies, row = [], 0
    for place, piece in enumerate(pieces):
        copies.append(
            pltpu.make_async_copy(piece, out.at[pl.ds(row, piece.shape[0]), :], sems.at[place])
        )
        row += piece.shape[0]
    for copy in copies:
        copy.start()
    for copy in copies:
        copy.wait()


def join(pieces, after=()):
    rows = sum(piece.shape[0] for piece in pieces)
    columns = pieces[0].shape[1]
    return launch(
        functools.partial(join_kernel, len(pieces)),
        [],
        list(pieces),
        [ANY] * len(pieces),
        pl.BlockSpec((rows, columns), lambda j: (0, 0)),
        jax.ShapeDtypeStruct((rows, columns), pieces[0].dtype),
        after=after,
        scratch=[pltpu.SemaphoreType.DMA((len(pieces),))],
        limit=16,
        cost_estimate=cost(0, 4 * rows * columns),
        name="join",
    )


BLOCK = 512


def by_blocks(kernel, split, *refs):
    width = next(ref for ref, cut in zip(refs, split) if cut).shape[1]

    def one(index, _):
        lanes = pl.ds(pl.multiple_of(index * BLOCK, BLOCK), BLOCK)
        kernel(*[ref.at[:, lanes] if cut else ref for ref, cut in zip(refs, split)])
        return 0

    lax.fori_loop(0, width // BLOCK, one, 0)


GROUP = 16
STATE_ROWS = 32


def state_kernel(
    mixer, rim, delta, kernel, bias, delta_bias, decay_log, extra, b_wide, step_out, conv_out,
    end_out, padded,
):
    tokens, width = mixer.shape
    blocks = width // LANES
    padded[0:8, :] = rim[...]
    padded[8:, :] = mixer[...].astype(jnp.float32)
    rate = [
        -jnp.exp(decay_log[:, k * LANES : (k + 1) * LANES]) * LOG2E for k in range(blocks)
    ]
    taps = kernel.shape[0]

    def group(index, carry):
        states, total = carry
        base = pl.multiple_of(index * GROUP, GROUP)
        window = padded[pl.ds(base, GROUP + 8), :]
        convolved = bias[...] + sum(
            kernel[k : k + 1, :] * window[9 - taps + k : 9 - taps + k + GROUP, :]
            for k in range(taps)
        )
        conv_act = silu(convolved)
        step = jnp.log(
            1.0 + jnp.exp(delta[pl.ds(base, GROUP), :].astype(jnp.float32) + delta_bias[...])
        )
        step_out[pl.ds(base, GROUP), :] = step
        conv_out[pl.ds(base, GROUP), :] = conv_act
        drive = step * conv_act
        states = list(states)
        for i in range(GROUP):
            b_tile = b_wide[pl.ds(pl.multiple_of((base + i) * 16, 16), 16), :]
            for k in range(blocks):
                lanes = slice(k * LANES, (k + 1) * LANES)
                states[k] = (
                    jnp.exp2(step[i : i + 1, lanes] * rate[k]) * states[k]
                    + b_tile * drive[i : i + 1, lanes]
                )
        return tuple(states), total + step[0:8, :] + step[8:16, :]

    start = tuple(jnp.zeros((16, LANES), jnp.float32) for _ in range(blocks))
    states, total = lax.fori_loop(
        0, tokens // GROUP, group, (start, jnp.zeros((8, width), jnp.float32))
    )
    for k in range(blocks):
        end_out[0:16, k * LANES : (k + 1) * LANES] = states[k].astype(end_out.dtype)
    total = jnp.sum(total, axis=0, keepdims=True)
    place = lax.broadcasted_iota(jnp.int32, (16, width), 0)
    pieces = jnp.where(place == 3, extra[...], 0.0)
    for row in range(3):
        piece = total.astype(jnp.bfloat16).astype(jnp.float32)
        pieces = jnp.where(place == row, piece, pieces)
        total = total - piece
    end_out[16:32, :] = pieces.astype(end_out.dtype)


def local_states(mixer_in, rim8, delta_in, kernel, bias, delta_bias, decay_log, extra, b_wide):
    tokens, channels = mixer_in.shape
    width = 1024
    rows = lambda n: pl.BlockSpec((n, width), lambda j: (0, j))
    return launch(
        functools.partial(by_blocks, state_kernel, [1] * 8 + [0] + [1] * 3 + [0]),
        [],
        [mixer_in, rim8, delta_in, kernel, bias, delta_bias, decay_log, extra, b_wide],
        [
            rows(tokens),
            rows(8),
            rows(tokens),
            rows(kernel.shape[0]),
            rows(1),
            rows(1),
            rows(16),
            rows(1),
            pl.BlockSpec((tokens * 16, LANES), lambda j: (0, 0)),
        ],
        [rows(tokens), rows(tokens), rows(STATE_ROWS)],
        [
            jax.ShapeDtypeStruct((tokens, channels), jnp.float32),
            jax.ShapeDtypeStruct((tokens, channels), jnp.float32),
            jax.ShapeDtypeStruct((STATE_ROWS, channels), jnp.bfloat16),
        ],
        grid=(channels // width,),
        scratch=[pltpu.VMEM((tokens + 8, BLOCK), jnp.float32)],
        cost_estimate=cost(
            tokens * channels * 16 * 5, tokens * channels * 12, tokens * channels * 18
        ),
        name="local_states",
    )


def gains_kernel(masks, me, *refs):
    parts, out = refs[: len(masks)], refs[-1]
    width = out.shape[2]
    for mask, part in zip(masks, parts):
        row = part[...].astype(jnp.float32)[3:4, :]
        gain = row[:, 0:width] + row[:, width : 2 * width] + row[:, 2 * width : 3 * width]
        out[me[0] ^ mask] = 1.0 / gain


def inverse_gains(me, ends, width):
    return launch(
        functools.partial(gains_kernel, [mask for mask, _, _ in ends]),
        [me],
        [end for _, _, end in ends],
        [pl.BlockSpec((16, 3 * width), lambda j, me: (1, 0))] * len(ends),
        pl.BlockSpec((len(ends), 1, width), lambda j, me: (0, 0, 0)),
        jax.ShapeDtypeStruct((len(ends), 1, width), jnp.float32),
        limit=16,
        name="inverse_gains",
    )


def fold_rows(tiles):
    place = lax.broadcasted_iota(jnp.int32, (8, LANES), 0)
    for shift in (1, 2, 4):
        first = (place & shift) == 0
        tiles = [
            jnp.where(first, a, b) + pltpu.roll(jnp.where(first, b, a), shift, 0)
            for a, b in zip(tiles[0::2], tiles[1::2])
        ]
    return tiles[0]


def readout_kernel(
    masks, me, step_in, conv_in, gate_in, decay_log, skip, b_wide, c_wide, entering, *refs
):
    ends = refs[: len(masks)]
    gated, leaving, scanned = refs[len(masks) : len(masks) + 3]
    tokens, width = step_in.shape
    blocks = width // LANES
    rate = [
        -jnp.exp(decay_log[:, k * LANES : (k + 1) * LANES]) * LOG2E for k in range(blocks)
    ]
    start = [entering[:, k * LANES : (k + 1) * LANES] for k in range(blocks)]
    if masks:
        held = refs[-1]
        for mask, end in zip(masks, ends):
            held[mask] = end[...].astype(jnp.float32)
        for owner in range(len(masks) - 1):
            end = held[me[0] ^ owner]
            total = end[16:17, :] + end[17:18, :] + end[18:19, :]
            for k in range(blocks):
                lanes = slice(k * LANES, (k + 1) * LANES)
                later = jnp.exp2(total[:, lanes] * rate[k]) * start[k] + end[0:16, lanes]
                start[k] = jnp.where(owner < me[0], later, start[k])

    def group(index, states):
        base = pl.multiple_of(index * GROUP, GROUP)
        step = step_in[pl.ds(base, GROUP), :]
        conv_act = conv_in[pl.ds(base, GROUP), :]
        drive = step * conv_act
        states = list(states)
        for half in range(GROUP // 8):
            tiles = [[] for _ in range(blocks)]
            for i in range(half * 8, half * 8 + 8):
                spot = pl.ds(pl.multiple_of((base + i) * 16, 16), 16)
                b_tile = b_wide[spot, :]
                c_tile = c_wide[spot, :]
                for k in range(blocks):
                    lanes = slice(k * LANES, (k + 1) * LANES)
                    states[k] = (
                        jnp.exp2(step[i : i + 1, lanes] * rate[k]) * states[k]
                        + b_tile * drive[i : i + 1, lanes]
                    )
                    read = c_tile * states[k]
                    tiles[k].append(read[0:8] + read[8:16])
            for k in range(blocks):
                scanned[
                    pl.ds(pl.multiple_of(base + half * 8, 8), 8), k * LANES : (k + 1) * LANES
                ] = fold_rows(tiles[k])
        gate = gate_in[pl.ds(base, GROUP), :].astype(jnp.float32)
        mixed = scanned[pl.ds(base, GROUP), :] + skip[...] * conv_act
        gated[pl.ds(base, GROUP), :] = (mixed * silu(gate)).astype(gated.dtype)
        return tuple(states)

    states = lax.fori_loop(0, tokens // GROUP, group, tuple(start))
    for k in range(blocks):
        leaving[:, k * LANES : (k + 1) * LANES] = states[k]


def read_out(
    me, chunk, chunks, step, conv_act, gate_in, decay_log, skip, b_wide, c_wide, entering, ends,
    after=(),
):
    tokens, channels = step.shape
    tokens = tokens // chunks
    width = 1024
    some = pl.BlockSpec((tokens, width), lambda j, me: (chunk, j))
    rows = lambda n: pl.BlockSpec((n, width), lambda j, me: (0, j))
    wide = pl.BlockSpec((tokens * 16, LANES), lambda j, me: (chunk, 0))
    masks = [mask for mask, _, _ in ends]
    scratch = [pltpu.VMEM((tokens, BLOCK), jnp.float32)]
    if ends:
        scratch.append(pltpu.VMEM((len(ends), STATE_ROWS, BLOCK), jnp.float32))
    split = [0] + [1] * 5 + [0, 0, 1] + [1] * len(ends) + [1, 1] + [0] * len(scratch)
    return launch(
        functools.partial(by_blocks, functools.partial(readout_kernel, masks), split),
        [me],
        [step, conv_act, gate_in, decay_log, skip, b_wide, c_wide, entering]
        + [end for _, _, end in ends],
        [some, some, some, rows(16), rows(1), wide, wide, rows(16)]
        + [rows(STATE_ROWS)] * len(ends),
        [rows(tokens), rows(16)],
        [
            jax.ShapeDtypeStruct((tokens, channels), jnp.bfloat16),
            jax.ShapeDtypeStruct((16, channels), jnp.float32),
        ],
        after=after,
        grid=(channels // width,),
        scratch=scratch,
        cost_estimate=cost(
            tokens * channels * 16 * 7, tokens * channels * 12, tokens * channels * 18
        ),
        name="read_out",
    )


def project_kernel(layout, me, weight, *refs):
    parts, (out, held, sems) = refs[: len(layout)], refs[len(layout) :]
    rows = held.shape[0] // (1 + max(mask for mask, _ in layout))

    @pl.when(pl.program_id(0) == 0)
    def _():
        copies = []
        for place, (mask, column) in enumerate(layout):
            part = parts[place]
            owner = me[0] ^ mask
            copies.append(
                pltpu.make_async_copy(
                    part,
                    held.at[
                        pl.ds(pl.multiple_of(owner * rows, rows), rows),
                        pl.ds(column, part.shape[1]),
                    ],
                    sems.at[place],
                )
            )
        for copy in copies:
            copy.start()
        for copy in copies:
            copy.wait()

    out[...] = jnp.dot(held[...], weight[...], preferred_element_type=jnp.float32).astype(
        out.dtype
    )


def project(me, parts, weight, after=()):
    depth, columns = weight.shape
    rows = parts[0][2].shape[0]
    total = rows * lax.axis_size("ctx")
    layout = [(mask, (which or 0) * depth // 2) for mask, which, _ in parts]
    tile = min(256, columns)
    return launch(
        functools.partial(project_kernel, layout),
        [me],
        [weight] + [part for _, _, part in parts],
        [pl.BlockSpec((depth, tile), lambda j, me: (0, j))] + [ANY] * len(parts),
        pl.BlockSpec((total, tile), lambda j, me: (0, j)),
        jax.ShapeDtypeStruct((total, columns), jnp.bfloat16),
        after=after,
        grid=(columns // tile,),
        scratch=[
            pltpu.VMEM((total, depth), jnp.bfloat16),
            pltpu.SemaphoreType.DMA((len(parts),)),
        ],
        limit=40,
        cost_estimate=cost(
            2 * total * depth * columns, 2 * (total * depth + depth * columns + total * columns)
        ),
        name="project",
    )


def hidden_kernel(layout, me, gain, gate_rows, up_rows, *refs):
    parts, (out, held, total, squares, sems) = refs[: len(layout)], refs[len(layout) :]
    turn = pl.program_id(0)

    def copy_of(place):
        mask, row = layout[place]
        part = parts[place]
        column = ((me[0] ^ mask) & 1) * part.shape[1]
        return pltpu.make_async_copy(
            part,
            held.at[
                mask // 2,
                pl.ds(row, part.shape[0]),
                pl.ds(pl.multiple_of(column, LANES), part.shape[1]),
            ],
            sems.at[place],
        )

    @pl.when(turn == 0)
    def _():
        for place in range(len(layout)):
            copy_of(place).start()
        total[...] = jnp.zeros_like(total)
        squares[...] = jnp.zeros_like(squares)

    for place, (mask, _) in enumerate(layout):

        @pl.when(turn == mask // 2)
        def _():
            copy_of(place).wait()

    width = out.shape[1]
    both = jnp.concatenate([gate_rows[...], up_rows[...]], axis=1)
    total[...] += jnp.dot(held[turn], both, preferred_element_type=jnp.float32)
    slots = out.shape[0]
    for row in range(0, slots, 64):
        mixer_square = squares[row : row + 64, :]
        for lane in range(0, held.shape[2], LANES):
            value = held[turn, row : row + 64, lane : lane + LANES].astype(jnp.float32)
            spot = lane % gain.shape[2]
            value = value * gain[lane // gain.shape[2], :, spot : spot + LANES]
            mixer_square += value * value
        squares[row : row + 64, :] = mixer_square

    @pl.when(turn == pl.num_programs(0) - 1)
    def _():
        def finish(index, _):
            spot = pl.ds(pl.multiple_of(index * 64, 64), 64)
            mean = jnp.sum(squares[spot, :], axis=1, keepdims=True) / D
            factor = lax.rsqrt(mean + 1e-05)
            gate_act = total[spot, 0:width] * factor
            up_act = total[spot, width:] * factor
            out[spot, :] = (silu(gate_act) * up_act).astype(out.dtype)
            return 0

        lax.fori_loop(0, out.shape[0] // 64, finish, 0)


def hidden_units(me, groups, one_over_gain, gate, up, after=()):
    depth = groups[0][0][2].shape[1]
    count = lax.axis_size("ctx")
    width = gate.shape[1]
    layout, parts, slots = [], [], 0
    for group in groups:
        rows = group[0][2].shape[0]
        layout += [(mask, slots + (which or 0) * rows // 2) for mask, which, _ in group]
        parts += group
        slots += rows
    block = pl.BlockSpec((2 * depth, width), lambda k, me: ((me[0] // 2) ^ k, 0))
    return launch(
        functools.partial(hidden_kernel, layout),
        [me],
        [one_over_gain, gate, up] + [part for _, _, part in parts],
        [
            pl.BlockSpec((2, 1, depth), lambda k, me: ((me[0] // 2) ^ k, 0, 0)),
            block,
            block,
        ] + [ANY] * len(parts),
        pl.BlockSpec((slots, width), lambda k, me: (0, 0)),
        jax.ShapeDtypeStruct((slots, width), jnp.bfloat16),
        after=after,
        grid=(count // 2,),
        scratch=[
            pltpu.VMEM((count // 2, slots, 2 * depth), jnp.bfloat16),
            pltpu.VMEM((slots, 2 * width), jnp.float32),
            pltpu.VMEM((slots, LANES), jnp.float32),
            pltpu.SemaphoreType.DMA((len(parts),)),
        ],
        limit=40,
        cost_estimate=cost(
            4 * slots * depth * count * width, 2 * count * depth * (slots + 2 * width)
        ),
        name="hidden_units",
    )


def down_kernel(layout, me, *refs):
    count = len(layout)
    units, weights, (out, held, sems) = refs[:count], refs[count:-3], refs[-3:]
    width = weights[0].shape[0]

    @pl.when(pl.program_id(0) == 0)
    def _():
        copies = []
        for place, (mask, row) in enumerate(layout):
            unit = units[place]
            copies.append(
                pltpu.make_async_copy(
                    unit,
                    held.at[pl.ds(row, unit.shape[0]), pl.ds(mask * width, width)],
                    sems.at[place],
                )
            )
        for copy in copies:
            copy.start()
        for copy in copies:
            copy.wait()

    tall = jnp.concatenate([weight[...] for weight in weights], axis=0)
    out[...] = jnp.dot(held[...], tall, preferred_element_type=jnp.float32).astype(out.dtype)


def down(me, parts, weights, own, after=()):
    columns = weights[-1].shape[1]
    width = own.shape[0]
    depth = width * len(weights)
    slots = parts[0][2].shape[0]
    tile = min(256, columns)
    layout = [(mask, (which or 0) * slots // 2) for mask, which, _ in parts]
    units = [part for _, _, part in parts]
    steps = columns // tile
    return launch(
        functools.partial(down_kernel, layout),
        [me],
        units + [own] + list(weights[1:]),
        [ANY] * len(units)
        + [pl.BlockSpec((width, tile), lambda j, me: (0, me[0] * steps + j))]
        + [pl.BlockSpec((width, tile), lambda j, me: (0, j))] * (len(weights) - 1),
        pl.BlockSpec((slots, tile), lambda j, me: (0, j)),
        jax.ShapeDtypeStruct((slots, columns), jnp.bfloat16),
        after=after,
        grid=(steps,),
        scratch=[
            pltpu.VMEM((slots, depth), jnp.bfloat16),
            pltpu.SemaphoreType.DMA((len(units),)),
        ],
        limit=40,
        cost_estimate=cost(
            2 * slots * depth * columns, 2 * (slots * depth + depth * columns + slots * columns)
        ),
        name="down",
    )


def cross_kernel(me, *refs):
    units, (own, *sent), refs = refs[:6], refs[6:12], refs[12:]
    keep, give_a, give_b, held, sems = refs
    width = own.shape[0]
    turn = pl.program_id(0)

    @pl.when(turn == 0)
    def _():
        copies = []
        for mask, unit in enumerate(units):
            column = (2, 3, 0, 1, 4, 5)[mask] * width
            copies.append(
                pltpu.make_async_copy(unit, held.at[:, pl.ds(column, width)], sems.at[mask])
            )
        for copy in copies:
            copy.start()
        for copy in copies:
            copy.wait()

    def summed(first, weights):
        tall = jnp.concatenate([weight[...] for weight in weights], axis=0)
        rows = held[:, first * width : (first + 4) * width]
        return jnp.dot(rows, tall, preferred_element_type=jnp.float32).astype(keep.dtype)

    for step, out in enumerate((keep, give_a, keep, give_b)):

        @pl.when(turn == step)
        def _():
            if step < 2:
                out[...] = summed(0, [sent[1], sent[2], own, sent[0]])
            else:
                out[...] = summed(2, [own, sent[0], sent[3], sent[4]])


def cross_down(me, units, weights, own, after=()):
    width = own.shape[0]
    half = weights[2].shape[1] // 2
    slots = units[0].shape[0]

    def mine(j, me):
        return (0, (me[0] ^ (jnp.where(j == 1, 4, 0) + jnp.where(j == 3, 2, 0))) * 2 + j // 2)

    front = pl.BlockSpec((width, half), lambda j, me: (0, jnp.minimum(j, 1)))
    back = pl.BlockSpec((width, half), lambda j, me: (0, jnp.maximum(j - 2, 0)))
    given = pl.BlockSpec((slots, half), lambda j, me: (0, 0))
    return launch(
        cross_kernel,
        [me],
        [units[mask] for mask in range(6)] + [own] + [weights[mask] for mask in range(1, 6)],
        [ANY] * 6
        + [
            pl.BlockSpec((width, half), mine),
            pl.BlockSpec((width, half), lambda j, me: (0, j)),
            front,
            front,
            back,
            back,
        ],
        [pl.BlockSpec((slots, half), lambda j, me: (0, j // 2)), given, given],
        [
            jax.ShapeDtypeStruct((slots, 2 * half), jnp.bfloat16),
            jax.ShapeDtypeStruct((slots, half), jnp.bfloat16),
            jax.ShapeDtypeStruct((slots, half), jnp.bfloat16),
        ],
        after=after,
        grid=(4,),
        scratch=[
            pltpu.VMEM((slots, 6 * width), jnp.bfloat16),
            pltpu.SemaphoreType.DMA((6,)),
        ],
        limit=40,
        cost_estimate=cost(16 * slots * 4 * width * half, 24 * width * half * 2),
        name="cross_down",
    )


def settle_kernel(keep, first, second, *outs):
    half = first.shape[1]
    rows = outs[0].shape[0]
    for place, out in enumerate(outs):
        spot = slice(place * rows, (place + 1) * rows)
        for column, other in ((0, first), (half, second)):
            total = keep[spot, column : column + half].astype(jnp.float32)
            out[:, column : column + half] = (
                total + other[spot, :].astype(jnp.float32)
            ).astype(out.dtype)


def settle(keep, first, second, count, after=()):
    slots, columns = keep.shape
    whole = lambda array: pl.BlockSpec(array.shape, lambda j: (0, 0))
    shape = (slots // count, columns)
    return launch(
        settle_kernel,
        [],
        [keep, first, second],
        [whole(keep), whole(first), whole(second)],
        [pl.BlockSpec(shape, lambda j: (0, 0))] * count,
        [jax.ShapeDtypeStruct(shape, keep.dtype)] * count,
        after=after,
        limit=24,
        cost_estimate=cost(2 * keep.size, 6 * keep.size),
        name="settle",
    )


def pick_kernel(count, rows, *refs):
    for picks, out in zip(refs[:count], refs[count:]):
        out[...] = lax.dot_general(
            picks[...], rows[...], (((0,), (0,)), ((), ())), preferred_element_type=jnp.float32
        ).astype(out.dtype)


def pick_rows(picks, rows, after=()):
    shape = (picks[0].shape[1], rows.shape[1])
    whole = lambda shape: pl.BlockSpec(shape, lambda j: (0, 0))
    return launch(
        functools.partial(pick_kernel, len(picks)),
        [],
        [rows] + list(picks),
        [whole(rows.shape)] + [whole(pick.shape) for pick in picks],
        [whole(shape)] * len(picks),
        [jax.ShapeDtypeStruct(shape, rows.dtype)] * len(picks),
        after=after,
        limit=24,
        cost_estimate=cost(2 * rows.size * shape[0] * len(picks), 4 * rows.size),
        name="pick_rows",
    )


def combine_kernel(me, mixer, ids, gates, *refs):
    out = refs[-1]
    count = len(refs) // 2
    total = mixer[...].astype(jnp.float32)
    for mask in range(count):
        named = ids[...] == (me[0] ^ mask)
        gate = jnp.sum(jnp.where(named, gates[...], 0.0), axis=1, keepdims=True)
        total += gate * jnp.dot(
            refs[mask][...], refs[count + mask][...], preferred_element_type=jnp.float32
        )
    out[...] = total.astype(out.dtype)


def combine(me, mixer_out, ids, gates, picks, answers):
    operands = [mixer_out, ids, gates] + list(picks) + list(answers)
    return launch(
        combine_kernel,
        [me],
        operands,
        [pl.BlockSpec(array.shape, lambda j, me: (0, 0)) for array in operands],
        pl.BlockSpec(mixer_out.shape, lambda j, me: (0, 0)),
        jax.ShapeDtypeStruct(mixer_out.shape, jnp.bfloat16),
        cost_estimate=cost(
            2 * mixer_out.size * answers[0].shape[0] * len(answers), 4 * mixer_out.size
        ),
        limit=24,
        name="combine",
    )


def shards(
    mixer_in,
    gate_in,
    delta_in,
    b_proj,
    c_proj,
    conv_kernel,
    conv_bias,
    delta_bias,
    decay_log,
    skip_gain,
    prefix_state,
    prefix_tail,
    out_proj,
    residual,
    norm_gain,
    expert_gate,
    expert_up,
    expert_down,
    expert_ids,
    route_gates,
):
    tokens = mixer_in.shape[0]
    rim = prefix_tail.shape[0]
    ctx_count = lax.axis_size("ctx")
    exp_count = lax.axis_size("exp")
    ctx_me = lax.axis_index("ctx")
    exp_me = lax.axis_index("exp")
    me = ctx_me.astype(jnp.int32).reshape(1)

    rim_rows = from_behind(mixer_in[tokens - rim :], "ctx", 1)
    rim_rows = jnp.where(ctx_me == 0, prefix_tail, rim_rows).astype(jnp.float32)
    rim8 = jnp.pad(rim_rows, ((8 - rim, 0), (0, 0)))

    width = out_proj.shape[1]
    down_rows = expert_down[0]
    down_parts = {}
    crossing = ctx_count == 8

    def send_columns(masks, after=()):
        if crossing:
            layouts = {1: [(1, 0), (5, 0), (1, 1), (3, 1)]}
            layouts.update({mask: [(mask, 0), (mask ^ 4, 0)] for mask in (2, 3)})
            layouts.update({mask: [(mask, 1), (mask ^ 2, 1)] for mask in (4, 5)})
            cuts = cut_columns(me, down_rows, width // 2, [layouts[m] for m in masks], after)
        else:
            cuts = cut_columns(me, down_rows, width, [[(m, 0)] for m in masks], after)
        for mask, cut in zip(masks, cuts):
            down_parts[mask] = swap(cut, "ctx", mask)
        return tuple(down_parts[mask] for mask in masks)

    early = send_columns([2, 4], [rim_rows])

    extra, left = [], norm_gain
    for _ in range(3):
        extra.append(lax.reduce_precision(left, 8, 7))
        left = left - extra[-1]
    extra = jnp.concatenate(extra)
    extra = jnp.pad(extra, (0, mixer_in.shape[1] - extra.shape[0]))[None, :]

    wide = lambda proj: jnp.broadcast_to(proj.T[:, :, None], (tokens, 16, LANES)).reshape(
        tokens * 16, LANES
    )
    b_wide, c_wide = wide(b_proj), wide(c_proj)
    step, conv_act, end = local_states(
        mixer_in,
        rim8,
        delta_in,
        conv_kernel,
        conv_bias[None, :],
        delta_bias[None, :],
        decay_log,
        extra,
        b_wide,
    )
    chunks = 2
    state, ends = prefix_state, gather_parts(join([end], early))
    one_over_gain = inverse_gains(me, ends, width)
    gated = []
    for chunk in range(chunks):
        rows, state = read_out(
            me,
            chunk,
            chunks,
            step,
            conv_act,
            gate_in,
            decay_log,
            skip_gain[None, :],
            b_wide,
            c_wide,
            state,
            ends,
        )
        ends = []
        gated.append(rows)
    near = lambda parts: [part for mask, _, part in parts if mask in (2, 4)]
    far = lambda parts: [part for mask, which, part in parts if which is not None][::2]
    scatter = lambda rows: lax.psum_scatter(rows, "exp", scatter_dimension=0, tiled=True)
    front = gather_parts(gated[0], 1, gated[1:])
    late_masks = [3, 5, 1] if crossing else [1, 3] + list(range(5, ctx_count))
    late = send_columns(late_masks, near(front))
    back = gather_parts(gated[1], 1, far(front))
    partial = project(me, front, out_proj, near(back))
    projected = [scatter(partial)]
    partial = project(me, back, out_proj, [partial])
    projected.append(scatter(partial))

    block_rows = residual.shape[0]
    owners = block_rows // tokens
    projected = jnp.stack(
        [piece.reshape(owners, tokens // chunks, width) for piece in projected], axis=1
    ).reshape(block_rows, width)
    mixer_out = (residual.astype(jnp.float32) + projected.astype(jnp.float32)).astype(
        jnp.bfloat16
    )
    mixer_wide = mixer_out.astype(jnp.float32)
    scaled = (mixer_wide * norm_gain[None, :]).astype(jnp.bfloat16)
    experts = expert_gate.shape[0] * exp_count
    capacity = 3 * block_rows * expert_ids.shape[1] // (2 * experts)
    spots = jnp.arange(capacity, dtype=jnp.int32)
    picked = []
    for mask in range(exp_count):
        here = jnp.any(expert_ids == (exp_me ^ mask), axis=1)
        place = jnp.cumsum(here.astype(jnp.int32)) - 1
        pick = here[:, None] & (place[:, None] == spots[None, :])
        picked.append(pick.astype(jnp.bfloat16))

    groups = [[0], list(range(1, exp_count))]
    sent = pick_rows(picked, scaled, late)
    pieces = [rows if mask == 0 else swap(rows, "exp", mask) for mask, rows in enumerate(sent)]
    weights = [None] + [down_parts[mask] for mask in sorted(down_parts)]
    settled, arrived, order, first_units, keeps = [], (), (), (), ()
    for group in groups:
        rows = [pieces[mask] for mask in group]
        rows = join(rows, arrived) if len(group) > 1 else rows[0]
        parts = gather_parts(rows, 0, order)
        arrived = far(parts)
        hidden = hidden_units(me, [parts], one_over_gain, expert_gate[0], expert_up[0], first_units)
        order = [hidden]
        if crossing:
            units = {0: hidden, 2: swap(hidden, "ctx", 2), 4: swap(hidden, "ctx", 4)}
            units.update({mask + 1: swap(units[mask], "ctx", 1) for mask in (0, 2, 4)})
            first_units = [units[2], units[4]]
            keep, first, second = cross_down(me, units, weights, down_rows, keeps)
            keeps = [keep]
            settled.append((keep, swap(first, "ctx", 4), swap(second, "ctx", 2)))
        else:
            answer = down(me, gather_parts(hidden), weights, down_rows, keeps)
            keeps = [answer]
            settled.append([answer])
    answers = {}
    for group, sums in zip(groups, settled):
        if crossing:
            pieces = settle(*sums, len(group), keeps)
        else:
            pieces = jnp.split(sums[0], len(group))
        for mask, piece in zip(group, pieces):
            answers[mask] = piece if mask == 0 else swap(piece, "exp", mask)
    block_out = combine(
        exp_me.astype(jnp.int32).reshape(1),
        mixer_out,
        expert_ids,
        route_gates,
        picked,
        [answers[mask] for mask in range(exp_count)],
    )
    return (mixer_out, block_out)


def solution(mesh):
    placed = (
        P("ctx", "exp"),
        P("ctx", "exp"),
        P("ctx", "exp"),
        P(None, "ctx"),
        P(None, "ctx"),
        P(None, "exp"),
        P("exp"),
        P("exp"),
        P(None, "exp"),
        P("exp"),
        P(None, "exp"),
        P(None, "exp"),
        P("exp", "ctx"),
        P("exp", "ctx"),
        P("ctx"),
        P("exp", None, "ctx"),
        P("exp", None, "ctx"),
        P("exp", "ctx", None),
        P("exp", None),
        P("exp", None),
    )
    return jax.shard_map(
        shards,
        mesh=mesh,
        in_specs=placed,
        out_specs=(P("exp", "ctx"), P("exp", "ctx")),
        check_vma=False,
    )
```

```python
import functools

import jax
import jax.numpy as jnp
from jax import lax
from jax.experimental import pallas as pl
from jax.experimental.pallas import tpu as pltpu
from jax.sharding import PartitionSpec as P

D = 8192
LOG2E = 1.4426950408889634
LANES = 128
MIB = 1 << 20


def from_behind(array, axis, by):
    length = lax.axis_size(axis)
    pairs = [(i, i + by) for i in range(length) if 0 <= i + by < length]
    return lax.ppermute(array, axis, pairs)


def swap(array, axis, mask):
    return lax.ppermute(array, axis, [(i, i ^ mask) for i in range(lax.axis_size(axis))])


def halves_kernel(split_dim, first, second, low, high):
    half = low.shape[split_dim]
    if split_dim == 0:
        low[...] = first[0:half, :]
        high[...] = second[half:, :]
    else:
        low[...] = first[:, 0:half]
        high[...] = second[:, half:]


def halves(first, second, split_dim, after=()):
    shape = list(first.shape)
    shape[split_dim] //= 2
    whole = pl.BlockSpec(first.shape, lambda j: (0, 0))
    part = pl.BlockSpec(tuple(shape), lambda j: (0, 0))
    return launch(
        functools.partial(halves_kernel, split_dim),
        [],
        [first, second],
        [whole, whole],
        [part, part],
        [jax.ShapeDtypeStruct(tuple(shape), first.dtype)] * 2,
        after=after,
        limit=16,
        cost_estimate=cost(0, 6 * first.size),
        name="halves",
    )


def gather_parts(array, split_dim=None, after=()):
    count = lax.axis_size("ctx")
    if count != 8:
        return [(0, None, array)] + [(m, None, swap(array, "ctx", m)) for m in range(1, count)]
    over_a = swap(array, "ctx", 2)
    over_b = swap(array, "ctx", 4)
    if split_dim is None:
        crossed = [(6, None, swap(array, "ctx", 6))]
    else:
        low, high = halves(over_a, over_b, split_dim, after)
        crossed = [(6, 0, swap(low, "ctx", 4)), (6, 1, swap(high, "ctx", 2))]
    parts = []
    for mask, which, part in [(0, None, array), (2, None, over_a), (4, None, over_b)] + crossed:
        parts.append((mask, which, part))
        parts.append((mask + 1, which, swap(part, "ctx", 1)))
    return parts


def silu(value):
    return value / (1.0 + jnp.exp(-value))


def cost(flops, moved, transcendentals=0):
    return pl.CostEstimate(
        flops=int(flops), bytes_accessed=int(moved), transcendentals=int(transcendentals)
    )


ANY = pl.BlockSpec(memory_space=pl.ANY)


def launch(
    kernel, scalars, operands, in_specs, out_specs, out_shape, after=(), grid=(1,), scratch=(),
    limit=56, **rest
):
    taken = len(scalars) + len(operands)

    def body(*refs):
        kernel(*refs[:taken], *refs[taken + len(after) :])

    return pl.pallas_call(
        body,
        grid_spec=pltpu.PrefetchScalarGridSpec(
            num_scalar_prefetch=len(scalars),
            grid=grid,
            in_specs=list(in_specs) + [ANY] * len(after),
            out_specs=out_specs,
            scratch_shapes=list(scratch),
        ),
        out_shape=out_shape,
        compiler_params=pltpu.CompilerParams(vmem_limit_bytes=limit * MIB),
        **rest,
    )(*scalars, *operands, *after)


def cut_kernel(layout, me, *refs):
    count = sum(len(pieces) for pieces in layout)
    sources, outs = iter(refs[:count]), refs[count:]
    for pieces, out in zip(layout, outs):
        width = out.shape[1] // len(pieces)
        for place in range(len(pieces)):
            out[:, place * width : (place + 1) * width] = next(sources)[...]


def cut_columns(me, rows, width, layout, after=()):
    step = rows.shape[0] // 3
    parts = rows.shape[1] // lax.axis_size("ctx") // width

    def block(mask, part):
        return pl.BlockSpec((step, width), lambda i, me: (i, (me[0] ^ mask) * parts + part))

    flat = [piece for pieces in layout for piece in pieces]
    widths = [width * len(pieces) for pieces in layout]
    return launch(
        functools.partial(cut_kernel, layout),
        [me],
        [rows] * len(flat),
        [block(*piece) for piece in flat],
        [pl.BlockSpec((step, wide), lambda i, me: (i, 0)) for wide in widths],
        [jax.ShapeDtypeStruct((rows.shape[0], wide), rows.dtype) for wide in widths],
        after=after,
        grid=(3,),
        cost_estimate=cost(0, 4 * rows.shape[0] * width * len(flat)),
        name="cut_columns",
    )


def join_kernel(count, *refs):
    pieces, out, sems = refs[:count], refs[count], refs[count + 1]
    copies, row = [], 0
    for place, piece in enumerate(pieces):
        copies.append(
            pltpu.make_async_copy(piece, out.at[pl.ds(row, piece.shape[0]), :], sems.at[place])
        )
        row += piece.shape[0]
    for copy in copies:
        copy.start()
    for copy in copies:
        copy.wait()


def join(pieces, after=()):
    rows = sum(piece.shape[0] for piece in pieces)
    columns = pieces[0].shape[1]
    return launch(
        functools.partial(join_kernel, len(pieces)),
        [],
        list(pieces),
        [ANY] * len(pieces),
        pl.BlockSpec((rows, columns), lambda j: (0, 0)),
        jax.ShapeDtypeStruct((rows, columns), pieces[0].dtype),
        after=after,
        scratch=[pltpu.SemaphoreType.DMA((len(pieces),))],
        limit=16,
        cost_estimate=cost(0, 4 * rows * columns),
        name="join",
    )


BLOCK = 512


def by_blocks(kernel, split, *refs):
    width = next(ref for ref, cut in zip(refs, split) if cut).shape[1]

    def one(index, _):
        lanes = pl.ds(pl.multiple_of(index * BLOCK, BLOCK), BLOCK)
        kernel(*[ref.at[:, lanes] if cut else ref for ref, cut in zip(refs, split)])
        return 0

    lax.fori_loop(0, width // BLOCK, one, 0)


GROUP = 16
STATE_ROWS = 32


def state_kernel(
    mixer, rim, delta, kernel, bias, delta_bias, decay_log, extra, b_wide, step_out, conv_out,
    end_out, padded,
):
    tokens, width = mixer.shape
    blocks = width // LANES
    padded[0:8, :] = rim[...]
    padded[8:, :] = mixer[...].astype(jnp.float32)
    rate = [
        -jnp.exp(decay_log[:, k * LANES : (k + 1) * LANES]) * LOG2E for k in range(blocks)
    ]
    taps = kernel.shape[0]

    def group(index, carry):
        states, total = carry
        base = pl.multiple_of(index * GROUP, GROUP)
        window = padded[pl.ds(base, GROUP + 8), :]
        convolved = bias[...] + sum(
            kernel[k : k + 1, :] * window[9 - taps + k : 9 - taps + k + GROUP, :]
            for k in range(taps)
        )
        conv_act = silu(convolved)
        step = jnp.log(
            1.0 + jnp.exp(delta[pl.ds(base, GROUP), :].astype(jnp.float32) + delta_bias[...])
        )
        step_out[pl.ds(base, GROUP), :] = step
        conv_out[pl.ds(base, GROUP), :] = conv_act
        drive = step * conv_act
        states = list(states)
        for i in range(GROUP):
            b_tile = b_wide[pl.ds(pl.multiple_of((base + i) * 16, 16), 16), :]
            for k in range(blocks):
                lanes = slice(k * LANES, (k + 1) * LANES)
                states[k] = (
                    jnp.exp2(step[i : i + 1, lanes] * rate[k]) * states[k]
                    + b_tile * drive[i : i + 1, lanes]
                )
        return tuple(states), total + step[0:8, :] + step[8:16, :]

    start = tuple(jnp.zeros((16, LANES), jnp.float32) for _ in range(blocks))
    states, total = lax.fori_loop(
        0, tokens // GROUP, group, (start, jnp.zeros((8, width), jnp.float32))
    )
    for k in range(blocks):
        end_out[0:16, k * LANES : (k + 1) * LANES] = states[k].astype(end_out.dtype)
    total = jnp.sum(total, axis=0, keepdims=True)
    place = lax.broadcasted_iota(jnp.int32, (16, width), 0)
    pieces = jnp.where(place == 3, extra[...], 0.0)
    for row in range(3):
        piece = total.astype(jnp.bfloat16).astype(jnp.float32)
        pieces = jnp.where(place == row, piece, pieces)
        total = total - piece
    end_out[16:32, :] = pieces.astype(end_out.dtype)


def local_states(mixer_in, rim8, delta_in, kernel, bias, delta_bias, decay_log, extra, b_wide):
    tokens, channels = mixer_in.shape
    width = 1024
    rows = lambda n: pl.BlockSpec((n, width), lambda j: (0, j))
    return launch(
        functools.partial(by_blocks, state_kernel, [1] * 8 + [0] + [1] * 3 + [0]),
        [],
        [mixer_in, rim8, delta_in, kernel, bias, delta_bias, decay_log, extra, b_wide],
        [
            rows(tokens),
            rows(8),
            rows(tokens),
            rows(kernel.shape[0]),
            rows(1),
            rows(1),
            rows(16),
            rows(1),
            pl.BlockSpec((tokens * 16, LANES), lambda j: (0, 0)),
        ],
        [rows(tokens), rows(tokens), rows(STATE_ROWS)],
        [
            jax.ShapeDtypeStruct((tokens, channels), jnp.float32),
            jax.ShapeDtypeStruct((tokens, channels), jnp.float32),
            jax.ShapeDtypeStruct((STATE_ROWS, channels), jnp.bfloat16),
        ],
        grid=(channels // width,),
        scratch=[pltpu.VMEM((tokens + 8, BLOCK), jnp.float32)],
        cost_estimate=cost(
            tokens * channels * 16 * 5, tokens * channels * 12, tokens * channels * 18
        ),
        name="local_states",
    )


def gains_kernel(masks, me, *refs):
    parts, out = refs[: len(masks)], refs[-1]
    width = out.shape[2]
    for mask, part in zip(masks, parts):
        row = part[...].astype(jnp.float32)[3:4, :]
        gain = row[:, 0:width] + row[:, width : 2 * width] + row[:, 2 * width : 3 * width]
        out[me[0] ^ mask] = 1.0 / gain


def inverse_gains(me, ends, width):
    return launch(
        functools.partial(gains_kernel, [mask for mask, _, _ in ends]),
        [me],
        [end for _, _, end in ends],
        [pl.BlockSpec((16, 3 * width), lambda j, me: (1, 0))] * len(ends),
        pl.BlockSpec((len(ends), 1, width), lambda j, me: (0, 0, 0)),
        jax.ShapeDtypeStruct((len(ends), 1, width), jnp.float32),
        limit=16,
        name="inverse_gains",
    )


def fold_rows(tiles):
    place = lax.broadcasted_iota(jnp.int32, (8, LANES), 0)
    for shift in (1, 2, 4):
        first = (place & shift) == 0
        tiles = [
            jnp.where(first, a, b) + pltpu.roll(jnp.where(first, b, a), shift, 0)
            for a, b in zip(tiles[0::2], tiles[1::2])
        ]
    return tiles[0]


def readout_kernel(
    masks, me, step_in, conv_in, gate_in, decay_log, skip, b_wide, c_wide, entering, *refs
):
    ends = refs[: len(masks)]
    gated, leaving, scanned = refs[len(masks) : len(masks) + 3]
    tokens, width = step_in.shape
    blocks = width // LANES
    rate = [
        -jnp.exp(decay_log[:, k * LANES : (k + 1) * LANES]) * LOG2E for k in range(blocks)
    ]
    start = [entering[:, k * LANES : (k + 1) * LANES] for k in range(blocks)]
    if masks:
        held = refs[-1]
        for mask, end in zip(masks, ends):
            held[mask] = end[...].astype(jnp.float32)
        for owner in range(len(masks) - 1):
            end = held[me[0] ^ owner]
            total = end[16:17, :] + end[17:18, :] + end[18:19, :]
            for k in range(blocks):
                lanes = slice(k * LANES, (k + 1) * LANES)
                later = jnp.exp2(total[:, lanes] * rate[k]) * start[k] + end[0:16, lanes]
                start[k] = jnp.where(owner < me[0], later, start[k])

    def group(index, states):
        base = pl.multiple_of(index * GROUP, GROUP)
        step = step_in[pl.ds(base, GROUP), :]
        conv_act = conv_in[pl.ds(base, GROUP), :]
        drive = step * conv_act
        states = list(states)
        for half in range(GROUP // 8):
            tiles = [[] for _ in range(blocks)]
            for i in range(half * 8, half * 8 + 8):
                spot = pl.ds(pl.multiple_of((base + i) * 16, 16), 16)
                b_tile = b_wide[spot, :]
                c_tile = c_wide[spot, :]
                for k in range(blocks):
                    lanes = slice(k * LANES, (k + 1) * LANES)
                    states[k] = (
                        jnp.exp2(step[i : i + 1, lanes] * rate[k]) * states[k]
                        + b_tile * drive[i : i + 1, lanes]
                    )
                    read = c_tile * states[k]
                    tiles[k].append(read[0:8] + read[8:16])
            for k in range(blocks):
                scanned[
                    pl.ds(pl.multiple_of(base + half * 8, 8), 8), k * LANES : (k + 1) * LANES
                ] = fold_rows(tiles[k])
        gate = gate_in[pl.ds(base, GROUP), :].astype(jnp.float32)
        mixed = scanned[pl.ds(base, GROUP), :] + skip[...] * conv_act
        gated[pl.ds(base, GROUP), :] = (mixed * silu(gate)).astype(gated.dtype)
        return tuple(states)

    states = lax.fori_loop(0, tokens // GROUP, group, tuple(start))
    for k in range(blocks):
        leaving[:, k * LANES : (k + 1) * LANES] = states[k]


def read_out(
    me, chunk, chunks, step, conv_act, gate_in, decay_log, skip, b_wide, c_wide, entering, ends,
    after=(),
):
    tokens, channels = step.shape
    tokens = tokens // chunks
    width = 1024
    some = pl.BlockSpec((tokens, width), lambda j, me: (chunk, j))
    rows = lambda n: pl.BlockSpec((n, width), lambda j, me: (0, j))
    wide = pl.BlockSpec((tokens * 16, LANES), lambda j, me: (chunk, 0))
    masks = [mask for mask, _, _ in ends]
    scratch = [pltpu.VMEM((tokens, BLOCK), jnp.float32)]
    if ends:
        scratch.append(pltpu.VMEM((len(ends), STATE_ROWS, BLOCK), jnp.float32))
    split = [0] + [1] * 5 + [0, 0, 1] + [1] * len(ends) + [1, 1] + [0] * len(scratch)
    return launch(
        functools.partial(by_blocks, functools.partial(readout_kernel, masks), split),
        [me],
        [step, conv_act, gate_in, decay_log, skip, b_wide, c_wide, entering]
        + [end for _, _, end in ends],
        [some, some, some, rows(16), rows(1), wide, wide, rows(16)]
        + [rows(STATE_ROWS)] * len(ends),
        [rows(tokens), rows(16)],
        [
            jax.ShapeDtypeStruct((tokens, channels), jnp.bfloat16),
            jax.ShapeDtypeStruct((16, channels), jnp.float32),
        ],
        after=after,
        grid=(channels // width,),
        scratch=scratch,
        cost_estimate=cost(
            tokens * channels * 16 * 7, tokens * channels * 12, tokens * channels * 18
        ),
        name="read_out",
    )


def project_kernel(layout, me, weight, *refs):
    parts, (out, held, sems) = refs[: len(layout)], refs[len(layout) :]
    rows = held.shape[0] // (1 + max(mask for mask, _ in layout))

    @pl.when(pl.program_id(0) == 0)
    def _():
        copies = []
        for place, (mask, column) in enumerate(layout):
            part = parts[place]
            owner = me[0] ^ mask
            copies.append(
                pltpu.make_async_copy(
                    part,
                    held.at[
                        pl.ds(pl.multiple_of(owner * rows, rows), rows),
                        pl.ds(column, part.shape[1]),
                    ],
                    sems.at[place],
                )
            )
        for copy in copies:
            copy.start()
        for copy in copies:
            copy.wait()

    out[...] = jnp.dot(held[...], weight[...], preferred_element_type=jnp.float32).astype(
        out.dtype
    )


def project(me, parts, weight, after=()):
    depth, columns = weight.shape
    rows = parts[0][2].shape[0]
    total = rows * lax.axis_size("ctx")
    layout = [(mask, (which or 0) * depth // 2) for mask, which, _ in parts]
    tile = min(256, columns)
    return launch(
        functools.partial(project_kernel, layout),
        [me],
        [weight] + [part for _, _, part in parts],
        [pl.BlockSpec((depth, tile), lambda j, me: (0, j))] + [ANY] * len(parts),
        pl.BlockSpec((total, tile), lambda j, me: (0, j)),
        jax.ShapeDtypeStruct((total, columns), jnp.bfloat16),
        after=after,
        grid=(columns // tile,),
        scratch=[
            pltpu.VMEM((total, depth), jnp.bfloat16),
            pltpu.SemaphoreType.DMA((len(parts),)),
        ],
        limit=40,
        cost_estimate=cost(
            2 * total * depth * columns, 2 * (total * depth + depth * columns + total * columns)
        ),
        name="project",
    )


def hidden_kernel(layout, me, gain, gate_rows, up_rows, *refs):
    parts, (out, held, total, squares, sems) = refs[: len(layout)], refs[len(layout) :]
    turn = pl.program_id(0)

    def copy_of(place):
        mask, row = layout[place]
        part = parts[place]
        column = ((me[0] ^ mask) & 1) * part.shape[1]
        return pltpu.make_async_copy(
            part,
            held.at[
                mask // 2,
                pl.ds(row, part.shape[0]),
                pl.ds(pl.multiple_of(column, LANES), part.shape[1]),
            ],
            sems.at[place],
        )

    @pl.when(turn == 0)
    def _():
        for place in range(len(layout)):
            copy_of(place).start()
        total[...] = jnp.zeros_like(total)
        squares[...] = jnp.zeros_like(squares)

    for place, (mask, _) in enumerate(layout):

        @pl.when(turn == mask // 2)
        def _():
            copy_of(place).wait()

    width = out.shape[1]
    both = jnp.concatenate([gate_rows[...], up_rows[...]], axis=1)
    total[...] += jnp.dot(held[turn], both, preferred_element_type=jnp.float32)
    slots = out.shape[0]
    for row in range(0, slots, 64):
        mixer_square = squares[row : row + 64, :]
        for lane in range(0, held.shape[2], LANES):
            value = held[turn, row : row + 64, lane : lane + LANES].astype(jnp.float32)
            spot = lane % gain.shape[2]
            value = value * gain[lane // gain.shape[2], :, spot : spot + LANES]
            mixer_square += value * value
        squares[row : row + 64, :] = mixer_square

    @pl.when(turn == pl.num_programs(0) - 1)
    def _():
        def finish(index, _):
            spot = pl.ds(pl.multiple_of(index * 64, 64), 64)
            mean = jnp.sum(squares[spot, :], axis=1, keepdims=True) / D
            factor = lax.rsqrt(mean + 1e-05)
            gate_act = total[spot, 0:width] * factor
            up_act = total[spot, width:] * factor
            out[spot, :] = (silu(gate_act) * up_act).astype(out.dtype)
            return 0

        lax.fori_loop(0, out.shape[0] // 64, finish, 0)


def hidden_units(me, groups, one_over_gain, gate, up, after=()):
    depth = groups[0][0][2].shape[1]
    count = lax.axis_size("ctx")
    width = gate.shape[1]
    layout, parts, slots = [], [], 0
    for group in groups:
        rows = group[0][2].shape[0]
        layout += [(mask, slots + (which or 0) * rows // 2) for mask, which, _ in group]
        parts += group
        slots += rows
    block = pl.BlockSpec((2 * depth, width), lambda k, me: ((me[0] // 2) ^ k, 0))
    return launch(
        functools.partial(hidden_kernel, layout),
        [me],
        [one_over_gain, gate, up] + [part for _, _, part in parts],
        [
            pl.BlockSpec((2, 1, depth), lambda k, me: ((me[0] // 2) ^ k, 0, 0)),
            block,
            block,
        ] + [ANY] * len(parts),
        pl.BlockSpec((slots, width), lambda k, me: (0, 0)),
        jax.ShapeDtypeStruct((slots, width), jnp.bfloat16),
        after=after,
        grid=(count // 2,),
        scratch=[
            pltpu.VMEM((count // 2, slots, 2 * depth), jnp.bfloat16),
            pltpu.VMEM((slots, 2 * width), jnp.float32),
            pltpu.VMEM((slots, LANES), jnp.float32),
            pltpu.SemaphoreType.DMA((len(parts),)),
        ],
        limit=40,
        cost_estimate=cost(
            4 * slots * depth * count * width, 2 * count * depth * (slots + 2 * width)
        ),
        name="hidden_units",
    )


def down_kernel(layout, me, *refs):
    count = len(layout)
    units, weights, (out, held, sems) = refs[:count], refs[count:-3], refs[-3:]
    width = weights[0].shape[0]

    @pl.when(pl.program_id(0) == 0)
    def _():
        copies = []
        for place, (mask, row) in enumerate(layout):
            unit = units[place]
            copies.append(
                pltpu.make_async_copy(
                    unit,
                    held.at[pl.ds(row, unit.shape[0]), pl.ds(mask * width, width)],
                    sems.at[place],
                )
            )
        for copy in copies:
            copy.start()
        for copy in copies:
            copy.wait()

    tall = jnp.concatenate([weight[...] for weight in weights], axis=0)
    out[...] = jnp.dot(held[...], tall, preferred_element_type=jnp.float32).astype(out.dtype)


def down(me, parts, weights, own, after=()):
    columns = weights[-1].shape[1]
    width = own.shape[0]
    depth = width * len(weights)
    slots = parts[0][2].shape[0]
    tile = min(256, columns)
    layout = [(mask, (which or 0) * slots // 2) for mask, which, _ in parts]
    units = [part for _, _, part in parts]
    steps = columns // tile
    return launch(
        functools.partial(down_kernel, layout),
        [me],
        units + [own] + list(weights[1:]),
        [ANY] * len(units)
        + [pl.BlockSpec((width, tile), lambda j, me: (0, me[0] * steps + j))]
        + [pl.BlockSpec((width, tile), lambda j, me: (0, j))] * (len(weights) - 1),
        pl.BlockSpec((slots, tile), lambda j, me: (0, j)),
        jax.ShapeDtypeStruct((slots, columns), jnp.bfloat16),
        after=after,
        grid=(steps,),
        scratch=[
            pltpu.VMEM((slots, depth), jnp.bfloat16),
            pltpu.SemaphoreType.DMA((len(units),)),
        ],
        limit=40,
        cost_estimate=cost(
            2 * slots * depth * columns, 2 * (slots * depth + depth * columns + slots * columns)
        ),
        name="down",
    )


def cross_kernel(me, *refs):
    units, (own, *sent), refs = refs[:6], refs[6:12], refs[12:]
    keep, give_a, give_b, held, sems = refs
    width = own.shape[0]
    turn = pl.program_id(0)

    @pl.when(turn == 0)
    def _():
        copies = []
        for mask, unit in enumerate(units):
            column = (2, 3, 0, 1, 4, 5)[mask] * width
            copies.append(
                pltpu.make_async_copy(unit, held.at[:, pl.ds(column, width)], sems.at[mask])
            )
        for copy in copies:
            copy.start()
        for copy in copies:
            copy.wait()

    def summed(first, weights):
        tall = jnp.concatenate([weight[...] for weight in weights], axis=0)
        rows = held[:, first * width : (first + 4) * width]
        return jnp.dot(rows, tall, preferred_element_type=jnp.float32).astype(keep.dtype)

    for step, out in enumerate((keep, give_a, keep, give_b)):

        @pl.when(turn == step)
        def _():
            if step < 2:
                out[...] = summed(0, [sent[1], sent[2], own, sent[0]])
            else:
                out[...] = summed(2, [own, sent[0], sent[3], sent[4]])


def cross_down(me, units, weights, own, after=()):
    width = own.shape[0]
    half = weights[2].shape[1] // 2
    slots = units[0].shape[0]

    def mine(j, me):
        return (0, (me[0] ^ (jnp.where(j == 1, 4, 0) + jnp.where(j == 3, 2, 0))) * 2 + j // 2)

    front = pl.BlockSpec((width, half), lambda j, me: (0, jnp.minimum(j, 1)))
    back = pl.BlockSpec((width, half), lambda j, me: (0, jnp.maximum(j - 2, 0)))
    given = pl.BlockSpec((slots, half), lambda j, me: (0, 0))
    return launch(
        cross_kernel,
        [me],
        [units[mask] for mask in range(6)] + [own] + [weights[mask] for mask in range(1, 6)],
        [ANY] * 6
        + [
            pl.BlockSpec((width, half), mine),
            pl.BlockSpec((width, half), lambda j, me: (0, j)),
            front,
            front,
            back,
            back,
        ],
        [pl.BlockSpec((slots, half), lambda j, me: (0, j // 2)), given, given],
        [
            jax.ShapeDtypeStruct((slots, 2 * half), jnp.bfloat16),
            jax.ShapeDtypeStruct((slots, half), jnp.bfloat16),
            jax.ShapeDtypeStruct((slots, half), jnp.bfloat16),
        ],
        after=after,
        grid=(4,),
        scratch=[
            pltpu.VMEM((slots, 6 * width), jnp.bfloat16),
            pltpu.SemaphoreType.DMA((6,)),
        ],
        limit=40,
        cost_estimate=cost(16 * slots * 4 * width * half, 24 * width * half * 2),
        name="cross_down",
    )


def settle_kernel(keep, first, second, *outs):
    half = first.shape[1]
    rows = outs[0].shape[0]
    for place, out in enumerate(outs):
        spot = slice(place * rows, (place + 1) * rows)
        for column, other in ((0, first), (half, second)):
            total = keep[spot, column : column + half].astype(jnp.float32)
            out[:, column : column + half] = (
                total + other[spot, :].astype(jnp.float32)
            ).astype(out.dtype)


def settle(keep, first, second, count, after=()):
    slots, columns = keep.shape
    whole = lambda array: pl.BlockSpec(array.shape, lambda j: (0, 0))
    shape = (slots // count, columns)
    return launch(
        settle_kernel,
        [],
        [keep, first, second],
        [whole(keep), whole(first), whole(second)],
        [pl.BlockSpec(shape, lambda j: (0, 0))] * count,
        [jax.ShapeDtypeStruct(shape, keep.dtype)] * count,
        after=after,
        limit=24,
        cost_estimate=cost(2 * keep.size, 6 * keep.size),
        name="settle",
    )


def pick_kernel(count, rows, *refs):
    for picks, out in zip(refs[:count], refs[count:]):
        out[...] = lax.dot_general(
            picks[...], rows[...], (((0,), (0,)), ((), ())), preferred_element_type=jnp.float32
        ).astype(out.dtype)


def pick_rows(picks, rows, after=()):
    shape = (picks[0].shape[1], rows.shape[1])
    whole = lambda shape: pl.BlockSpec(shape, lambda j: (0, 0))
    return launch(
        functools.partial(pick_kernel, len(picks)),
        [],
        [rows] + list(picks),
        [whole(rows.shape)] + [whole(pick.shape) for pick in picks],
        [whole(shape)] * len(picks),
        [jax.ShapeDtypeStruct(shape, rows.dtype)] * len(picks),
        after=after,
        limit=24,
        cost_estimate=cost(2 * rows.size * shape[0] * len(picks), 4 * rows.size),
        name="pick_rows",
    )


def combine_kernel(me, mixer, ids, gates, *refs):
    out = refs[-1]
    count = len(refs) // 2
    total = mixer[...].astype(jnp.float32)
    for mask in range(count):
        named = ids[...] == (me[0] ^ mask)
        gate = jnp.sum(jnp.where(named, gates[...], 0.0), axis=1, keepdims=True)
        total += gate * jnp.dot(
            refs[mask][...], refs[count + mask][...], preferred_element_type=jnp.float32
        )
    out[...] = total.astype(out.dtype)


def combine(me, mixer_out, ids, gates, picks, answers):
    operands = [mixer_out, ids, gates] + list(picks) + list(answers)
    return launch(
        combine_kernel,
        [me],
        operands,
        [pl.BlockSpec(array.shape, lambda j, me: (0, 0)) for array in operands],
        pl.BlockSpec(mixer_out.shape, lambda j, me: (0, 0)),
        jax.ShapeDtypeStruct(mixer_out.shape, jnp.bfloat16),
        cost_estimate=cost(
            2 * mixer_out.size * answers[0].shape[0] * len(answers), 4 * mixer_out.size
        ),
        limit=24,
        name="combine",
    )


def shards(
    mixer_in,
    gate_in,
    delta_in,
    b_proj,
    c_proj,
    conv_kernel,
    conv_bias,
    delta_bias,
    decay_log,
    skip_gain,
    prefix_state,
    prefix_tail,
    out_proj,
    residual,
    norm_gain,
    expert_gate,
    expert_up,
    expert_down,
    expert_ids,
    route_gates,
):
    tokens = mixer_in.shape[0]
    rim = prefix_tail.shape[0]
    ctx_count = lax.axis_size("ctx")
    exp_count = lax.axis_size("exp")
    ctx_me = lax.axis_index("ctx")
    exp_me = lax.axis_index("exp")
    me = ctx_me.astype(jnp.int32).reshape(1)

    rim_rows = from_behind(mixer_in[tokens - rim :], "ctx", 1)
    rim_rows = jnp.where(ctx_me == 0, prefix_tail, rim_rows).astype(jnp.float32)
    rim8 = jnp.pad(rim_rows, ((8 - rim, 0), (0, 0)))

    width = out_proj.shape[1]
    down_rows = expert_down[0]
    down_parts = {}
    crossing = ctx_count == 8

    def send_columns(masks, after=()):
        if crossing:
            layouts = {1: [(1, 0), (5, 0), (1, 1), (3, 1)]}
            layouts.update({mask: [(mask, 0), (mask ^ 4, 0)] for mask in (2, 3)})
            layouts.update({mask: [(mask, 1), (mask ^ 2, 1)] for mask in (4, 5)})
            cuts = cut_columns(me, down_rows, width // 2, [layouts[m] for m in masks], after)
        else:
            cuts = cut_columns(me, down_rows, width, [[(m, 0)] for m in masks], after)
        for mask, cut in zip(masks, cuts):
            down_parts[mask] = swap(cut, "ctx", mask)
        return tuple(down_parts[mask] for mask in masks)


    extra, left = [], norm_gain
    for _ in range(3):
        extra.append(lax.reduce_precision(left, 8, 7))
        left = left - extra[-1]
    extra = jnp.concatenate(extra)
    extra = jnp.pad(extra, (0, mixer_in.shape[1] - extra.shape[0]))[None, :]

    wide = lambda proj: jnp.broadcast_to(proj.T[:, :, None], (tokens, 16, LANES)).reshape(
        tokens * 16, LANES
    )
    b_wide, c_wide = wide(b_proj), wide(c_proj)
    step, conv_act, end = local_states(
        mixer_in,
        rim8,
        delta_in,
        conv_kernel,
        conv_bias[None, :],
        delta_bias[None, :],
        decay_log,
        extra,
        b_wide,
    )
    chunks = 2
    state, ends = prefix_state, gather_parts(end)
    one_over_gain = inverse_gains(me, ends, width)
    gated = []
    for chunk in range(chunks):
        rows, state = read_out(
            me,
            chunk,
            chunks,
            step,
            conv_act,
            gate_in,
            decay_log,
            skip_gain[None, :],
            b_wide,
            c_wide,
            state,
            ends,
        )
        ends = []
        gated.append(rows)
    near = lambda parts: [part for mask, _, part in parts if mask in (2, 4)]
    far = lambda parts: [part for mask, which, part in parts if which is not None][::2]
    scatter = lambda rows: lax.psum_scatter(rows, "exp", scatter_dimension=0, tiled=True)
    front = gather_parts(gated[0], 1, gated[1:])
    late = send_columns([3, 5, 1, 2, 4] if crossing else list(range(1, ctx_count)), near(front))
    back = gather_parts(gated[1], 1, far(front))
    partial = project(me, front, out_proj, near(back))
    projected = [scatter(partial)]
    partial = project(me, back, out_proj, [partial])
    projected.append(scatter(partial))

    block_rows = residual.shape[0]
    owners = block_rows // tokens
    projected = jnp.stack(
        [piece.reshape(owners, tokens // chunks, width) for piece in projected], axis=1
    ).reshape(block_rows, width)
    mixer_out = (residual.astype(jnp.float32) + projected.astype(jnp.float32)).astype(
        jnp.bfloat16
    )
    mixer_wide = mixer_out.astype(jnp.float32)
    scaled = (mixer_wide * norm_gain[None, :]).astype(jnp.bfloat16)
    experts = expert_gate.shape[0] * exp_count
    capacity = 3 * block_rows * expert_ids.shape[1] // (2 * experts)
    spots = jnp.arange(capacity, dtype=jnp.int32)
    picked = []
    for mask in range(exp_count):
        here = jnp.any(expert_ids == (exp_me ^ mask), axis=1)
        place = jnp.cumsum(here.astype(jnp.int32)) - 1
        pick = here[:, None] & (place[:, None] == spots[None, :])
        picked.append(pick.astype(jnp.bfloat16))

    groups = [[0], list(range(1, exp_count))]
    sent = pick_rows(picked, scaled, late)
    pieces = [rows if mask == 0 else swap(rows, "exp", mask) for mask, rows in enumerate(sent)]
    weights = [None] + [down_parts[mask] for mask in sorted(down_parts)]
    gathered_units, arrived, order, ready = [], (), (), ()
    for group in groups:
        rows = [pieces[mask] for mask in group]
        rows = join(rows, arrived) if len(group) > 1 else rows[0]
        parts = gather_parts(rows, 0, order)
        arrived = far(parts)
        hidden = hidden_units(me, [parts], one_over_gain, expert_gate[0], expert_up[0], ready)
        order = [hidden]
        if crossing:
            units = {0: hidden, 2: swap(hidden, "ctx", 2), 4: swap(hidden, "ctx", 4)}
            units.update({mask + 1: swap(units[mask], "ctx", 1) for mask in (0, 2, 4)})
            ready = [units[2], units[4]]
        else:
            units = gather_parts(hidden)
        gathered_units.append(units)
    answers, order, before = {}, (), ()
    for group, units in list(zip(groups, gathered_units))[::-1]:
        if crossing:
            keep, first, second = cross_down(me, units, weights, down_rows, order)
            first, second = swap(first, "ctx", 4), swap(second, "ctx", 2)
            before = settle(keep, first, second, len(group), before)
        else:
            keep = down(me, units, weights, down_rows, order)
            before = jnp.split(keep, len(group))
        order = [keep]
        for mask, piece in zip(group, before):
            answers[mask] = piece if mask == 0 else swap(piece, "exp", mask)
    block_out = combine(
        exp_me.astype(jnp.int32).reshape(1),
        mixer_out,
        expert_ids,
        route_gates,
        picked,
        [answers[mask] for mask in range(exp_count)],
    )
    return (mixer_out, block_out)


def solution(mesh):
    placed = (
        P("ctx", "exp"),
        P("ctx", "exp"),
        P("ctx", "exp"),
        P(None, "ctx"),
        P(None, "ctx"),
        P(None, "exp"),
        P("exp"),
        P("exp"),
        P(None, "exp"),
        P("exp"),
        P(None, "exp"),
        P(None, "exp"),
        P("exp", "ctx"),
        P("exp", "ctx"),
        P("ctx"),
        P("exp", None, "ctx"),
        P("exp", None, "ctx"),
        P("exp", "ctx", None),
        P("exp", None),
        P("exp", None),
    )
    return jax.shard_map(
        shards,
        mesh=mesh,
        in_specs=placed,
        out_specs=(P("exp", "ctx"), P("exp", "ctx")),
        check_vma=False,
    )
```

```python
import functools

import jax
import jax.numpy as jnp
from jax import lax
from jax.experimental import pallas as pl
from jax.experimental.pallas import tpu as pltpu
from jax.sharding import PartitionSpec as P

D = 8192
LOG2E = 1.4426950408889634
LANES = 128
MIB = 1 << 20


def from_behind(array, axis, by):
    length = lax.axis_size(axis)
    pairs = [(i, i + by) for i in range(length) if 0 <= i + by < length]
    return lax.ppermute(array, axis, pairs)


def swap(array, axis, mask):
    return lax.ppermute(array, axis, [(i, i ^ mask) for i in range(lax.axis_size(axis))])


def halves_kernel(split_dim, first, second, low, high):
    half = low.shape[split_dim]
    if split_dim == 0:
        low[...] = first[0:half, :]
        high[...] = second[half:, :]
    else:
        low[...] = first[:, 0:half]
        high[...] = second[:, half:]


def halves(first, second, split_dim, after=()):
    shape = list(first.shape)
    shape[split_dim] //= 2
    whole = pl.BlockSpec(first.shape, lambda j: (0, 0))
    part = pl.BlockSpec(tuple(shape), lambda j: (0, 0))
    return launch(
        functools.partial(halves_kernel, split_dim),
        [],
        [first, second],
        [whole, whole],
        [part, part],
        [jax.ShapeDtypeStruct(tuple(shape), first.dtype)] * 2,
        after=after,
        limit=16,
        cost_estimate=cost(0, 6 * first.size),
        name="halves",
    )


def gather_parts(array, split_dim=None, after=()):
    count = lax.axis_size("ctx")
    if count != 8:
        return [(0, None, array)] + [(m, None, swap(array, "ctx", m)) for m in range(1, count)]
    over_a = swap(array, "ctx", 2)
    over_b = swap(array, "ctx", 4)
    if split_dim is None:
        crossed = [(6, None, swap(array, "ctx", 6))]
    else:
        low, high = halves(over_a, over_b, split_dim, after)
        crossed = [(6, 0, swap(low, "ctx", 4)), (6, 1, swap(high, "ctx", 2))]
    parts = []
    for mask, which, part in [(0, None, array), (2, None, over_a), (4, None, over_b)] + crossed:
        parts.append((mask, which, part))
        parts.append((mask + 1, which, swap(part, "ctx", 1)))
    return parts


def silu(value):
    return value / (1.0 + jnp.exp(-value))


def cost(flops, moved, transcendentals=0):
    return pl.CostEstimate(
        flops=int(flops), bytes_accessed=int(moved), transcendentals=int(transcendentals)
    )


ANY = pl.BlockSpec(memory_space=pl.ANY)


def launch(
    kernel, scalars, operands, in_specs, out_specs, out_shape, after=(), grid=(1,), scratch=(),
    limit=56, **rest
):
    taken = len(scalars) + len(operands)

    def body(*refs):
        kernel(*refs[:taken], *refs[taken + len(after) :])

    return pl.pallas_call(
        body,
        grid_spec=pltpu.PrefetchScalarGridSpec(
            num_scalar_prefetch=len(scalars),
            grid=grid,
            in_specs=list(in_specs) + [ANY] * len(after),
            out_specs=out_specs,
            scratch_shapes=list(scratch),
        ),
        out_shape=out_shape,
        compiler_params=pltpu.CompilerParams(vmem_limit_bytes=limit * MIB),
        **rest,
    )(*scalars, *operands, *after)


def cut_kernel(layout, me, *refs):
    count = sum(len(pieces) for pieces in layout)
    sources, outs = iter(refs[:count]), refs[count:]
    for pieces, out in zip(layout, outs):
        width = out.shape[1] // len(pieces)
        for place in range(len(pieces)):
            out[:, place * width : (place + 1) * width] = next(sources)[...]


def cut_columns(me, rows, width, layout, after=()):
    step = rows.shape[0] // 3
    parts = rows.shape[1] // lax.axis_size("ctx") // width

    def block(mask, part):
        return pl.BlockSpec((step, width), lambda i, me: (i, (me[0] ^ mask) * parts + part))

    flat = [piece for pieces in layout for piece in pieces]
    widths = [width * len(pieces) for pieces in layout]
    return launch(
        functools.partial(cut_kernel, layout),
        [me],
        [rows] * len(flat),
        [block(*piece) for piece in flat],
        [pl.BlockSpec((step, wide), lambda i, me: (i, 0)) for wide in widths],
        [jax.ShapeDtypeStruct((rows.shape[0], wide), rows.dtype) for wide in widths],
        after=after,
        grid=(3,),
        cost_estimate=cost(0, 4 * rows.shape[0] * width * len(flat)),
        name="cut_columns",
    )


def join_kernel(count, *refs):
    pieces, out, sems = refs[:count], refs[count], refs[count + 1]
    copies, row = [], 0
    for place, piece in enumerate(pieces):
        copies.append(
            pltpu.make_async_copy(piece, out.at[pl.ds(row, piece.shape[0]), :], sems.at[place])
        )
        row += piece.shape[0]
    for copy in copies:
        copy.start()
    for copy in copies:
        copy.wait()


def join(pieces, after=()):
    rows = sum(piece.shape[0] for piece in pieces)
    columns = pieces[0].shape[1]
    return launch(
        functools.partial(join_kernel, len(pieces)),
        [],
        list(pieces),
        [ANY] * len(pieces),
        pl.BlockSpec((rows, columns), lambda j: (0, 0)),
        jax.ShapeDtypeStruct((rows, columns), pieces[0].dtype),
        after=after,
        scratch=[pltpu.SemaphoreType.DMA((len(pieces),))],
        limit=16,
        cost_estimate=cost(0, 4 * rows * columns),
        name="join",
    )


BLOCK = 512


def by_blocks(kernel, split, *refs):
    width = next(ref for ref, cut in zip(refs, split) if cut).shape[1]

    def one(index, _):
        lanes = pl.ds(pl.multiple_of(index * BLOCK, BLOCK), BLOCK)
        kernel(*[ref.at[:, lanes] if cut else ref for ref, cut in zip(refs, split)])
        return 0

    lax.fori_loop(0, width // BLOCK, one, 0)


GROUP = 16
STATE_ROWS = 32


def state_kernel(
    mixer, rim, delta, kernel, bias, delta_bias, decay_log, extra, b_wide, step_out, conv_out,
    end_out, padded,
):
    tokens, width = mixer.shape
    blocks = width // LANES
    padded[0:8, :] = rim[...]
    padded[8:, :] = mixer[...].astype(jnp.float32)
    rate = [
        -jnp.exp(decay_log[:, k * LANES : (k + 1) * LANES]) * LOG2E for k in range(blocks)
    ]
    taps = kernel.shape[0]

    def group(index, carry):
        states, total = carry
        base = pl.multiple_of(index * GROUP, GROUP)
        window = padded[pl.ds(base, GROUP + 8), :]
        convolved = bias[...] + sum(
            kernel[k : k + 1, :] * window[9 - taps + k : 9 - taps + k + GROUP, :]
            for k in range(taps)
        )
        conv_act = silu(convolved)
        step = jnp.log(
            1.0 + jnp.exp(delta[pl.ds(base, GROUP), :].astype(jnp.float32) + delta_bias[...])
        )
        step_out[pl.ds(base, GROUP), :] = step
        conv_out[pl.ds(base, GROUP), :] = conv_act
        drive = step * conv_act
        states = list(states)
        for i in range(GROUP):
            b_tile = b_wide[pl.ds(pl.multiple_of((base + i) * 16, 16), 16), :]
            for k in range(blocks):
                lanes = slice(k * LANES, (k + 1) * LANES)
                states[k] = (
                    jnp.exp2(step[i : i + 1, lanes] * rate[k]) * states[k]
                    + b_tile * drive[i : i + 1, lanes]
                )
        return tuple(states), total + step[0:8, :] + step[8:16, :]

    start = tuple(jnp.zeros((16, LANES), jnp.float32) for _ in range(blocks))
    states, total = lax.fori_loop(
        0, tokens // GROUP, group, (start, jnp.zeros((8, width), jnp.float32))
    )
    for k in range(blocks):
        end_out[0:16, k * LANES : (k + 1) * LANES] = states[k].astype(end_out.dtype)
    total = jnp.sum(total, axis=0, keepdims=True)
    place = lax.broadcasted_iota(jnp.int32, (16, width), 0)
    pieces = jnp.where(place == 3, extra[...], 0.0)
    for row in range(3):
        piece = total.astype(jnp.bfloat16).astype(jnp.float32)
        pieces = jnp.where(place == row, piece, pieces)
        total = total - piece
    end_out[16:32, :] = pieces.astype(end_out.dtype)


def local_states(mixer_in, rim8, delta_in, kernel, bias, delta_bias, decay_log, extra, b_wide):
    tokens, channels = mixer_in.shape
    width = 1024
    rows = lambda n: pl.BlockSpec((n, width), lambda j: (0, j))
    return launch(
        functools.partial(by_blocks, state_kernel, [1] * 8 + [0] + [1] * 3 + [0]),
        [],
        [mixer_in, rim8, delta_in, kernel, bias, delta_bias, decay_log, extra, b_wide],
        [
            rows(tokens),
            rows(8),
            rows(tokens),
            rows(kernel.shape[0]),
            rows(1),
            rows(1),
            rows(16),
            rows(1),
            pl.BlockSpec((tokens * 16, LANES), lambda j: (0, 0)),
        ],
        [rows(tokens), rows(tokens), rows(STATE_ROWS)],
        [
            jax.ShapeDtypeStruct((tokens, channels), jnp.float32),
            jax.ShapeDtypeStruct((tokens, channels), jnp.float32),
            jax.ShapeDtypeStruct((STATE_ROWS, channels), jnp.bfloat16),
        ],
        grid=(channels // width,),
        scratch=[pltpu.VMEM((tokens + 8, BLOCK), jnp.float32)],
        cost_estimate=cost(
            tokens * channels * 16 * 5, tokens * channels * 12, tokens * channels * 18
        ),
        name="local_states",
    )


def gains_kernel(masks, me, *refs):
    parts, out = refs[: len(masks)], refs[-1]
    width = out.shape[2]
    for mask, part in zip(masks, parts):
        row = part[...].astype(jnp.float32)[3:4, :]
        gain = row[:, 0:width] + row[:, width : 2 * width] + row[:, 2 * width : 3 * width]
        out[me[0] ^ mask] = 1.0 / gain


def inverse_gains(me, ends, width):
    return launch(
        functools.partial(gains_kernel, [mask for mask, _, _ in ends]),
        [me],
        [end for _, _, end in ends],
        [pl.BlockSpec((16, 3 * width), lambda j, me: (1, 0))] * len(ends),
        pl.BlockSpec((len(ends), 1, width), lambda j, me: (0, 0, 0)),
        jax.ShapeDtypeStruct((len(ends), 1, width), jnp.float32),
        limit=16,
        name="inverse_gains",
    )


def fold_rows(tiles):
    place = lax.broadcasted_iota(jnp.int32, (8, LANES), 0)
    for shift in (1, 2, 4):
        first = (place & shift) == 0
        tiles = [
            jnp.where(first, a, b) + pltpu.roll(jnp.where(first, b, a), shift, 0)
            for a, b in zip(tiles[0::2], tiles[1::2])
        ]
    return tiles[0]


def readout_kernel(
    masks, me, step_in, conv_in, gate_in, decay_log, skip, b_wide, c_wide, entering, *refs
):
    ends = refs[: len(masks)]
    gated, leaving, scanned = refs[len(masks) : len(masks) + 3]
    tokens, width = step_in.shape
    blocks = width // LANES
    rate = [
        -jnp.exp(decay_log[:, k * LANES : (k + 1) * LANES]) * LOG2E for k in range(blocks)
    ]
    start = [entering[:, k * LANES : (k + 1) * LANES] for k in range(blocks)]
    if masks:
        held = refs[-1]
        for mask, end in zip(masks, ends):
            held[mask] = end[...].astype(jnp.float32)
        for owner in range(len(masks) - 1):
            end = held[me[0] ^ owner]
            total = end[16:17, :] + end[17:18, :] + end[18:19, :]
            for k in range(blocks):
                lanes = slice(k * LANES, (k + 1) * LANES)
                later = jnp.exp2(total[:, lanes] * rate[k]) * start[k] + end[0:16, lanes]
                start[k] = jnp.where(owner < me[0], later, start[k])

    def group(index, states):
        base = pl.multiple_of(index * GROUP, GROUP)
        step = step_in[pl.ds(base, GROUP), :]
        conv_act = conv_in[pl.ds(base, GROUP), :]
        drive = step * conv_act
        states = list(states)
        for half in range(GROUP // 8):
            tiles = [[] for _ in range(blocks)]
            for i in range(half * 8, half * 8 + 8):
                spot = pl.ds(pl.multiple_of((base + i) * 16, 16), 16)
                b_tile = b_wide[spot, :]
                c_tile = c_wide[spot, :]
                for k in range(blocks):
                    lanes = slice(k * LANES, (k + 1) * LANES)
                    states[k] = (
                        jnp.exp2(step[i : i + 1, lanes] * rate[k]) * states[k]
                        + b_tile * drive[i : i + 1, lanes]
                    )
                    read = c_tile * states[k]
                    tiles[k].append(read[0:8] + read[8:16])
            for k in range(blocks):
                scanned[
                    pl.ds(pl.multiple_of(base + half * 8, 8), 8), k * LANES : (k + 1) * LANES
                ] = fold_rows(tiles[k])
        gate = gate_in[pl.ds(base, GROUP), :].astype(jnp.float32)
        mixed = scanned[pl.ds(base, GROUP), :] + skip[...] * conv_act
        gated[pl.ds(base, GROUP), :] = (mixed * silu(gate)).astype(gated.dtype)
        return tuple(states)

    states = lax.fori_loop(0, tokens // GROUP, group, tuple(start))
    for k in range(blocks):
        leaving[:, k * LANES : (k + 1) * LANES] = states[k]


def read_out(
    me, chunk, chunks, step, conv_act, gate_in, decay_log, skip, b_wide, c_wide, entering, ends,
    after=(),
):
    tokens, channels = step.shape
    tokens = tokens // chunks
    width = 1024
    some = pl.BlockSpec((tokens, width), lambda j, me: (chunk, j))
    rows = lambda n: pl.BlockSpec((n, width), lambda j, me: (0, j))
    wide = pl.BlockSpec((tokens * 16, LANES), lambda j, me: (chunk, 0))
    masks = [mask for mask, _, _ in ends]
    scratch = [pltpu.VMEM((tokens, BLOCK), jnp.float32)]
    if ends:
        scratch.append(pltpu.VMEM((len(ends), STATE_ROWS, BLOCK), jnp.float32))
    split = [0] + [1] * 5 + [0, 0, 1] + [1] * len(ends) + [1, 1] + [0] * len(scratch)
    return launch(
        functools.partial(by_blocks, functools.partial(readout_kernel, masks), split),
        [me],
        [step, conv_act, gate_in, decay_log, skip, b_wide, c_wide, entering]
        + [end for _, _, end in ends],
        [some, some, some, rows(16), rows(1), wide, wide, rows(16)]
        + [rows(STATE_ROWS)] * len(ends),
        [rows(tokens), rows(16)],
        [
            jax.ShapeDtypeStruct((tokens, channels), jnp.bfloat16),
            jax.ShapeDtypeStruct((16, channels), jnp.float32),
        ],
        after=after,
        grid=(channels // width,),
        scratch=scratch,
        cost_estimate=cost(
            tokens * channels * 16 * 7, tokens * channels * 12, tokens * channels * 18
        ),
        name="read_out",
    )


def project_kernel(layout, me, weight, *refs):
    parts, (out, held, sems) = refs[: len(layout)], refs[len(layout) :]
    rows = held.shape[0] // (1 + max(mask for mask, _ in layout))

    @pl.when(pl.program_id(0) == 0)
    def _():
        copies = []
        for place, (mask, column) in enumerate(layout):
            part = parts[place]
            owner = me[0] ^ mask
            copies.append(
                pltpu.make_async_copy(
                    part,
                    held.at[
                        pl.ds(pl.multiple_of(owner * rows, rows), rows),
                        pl.ds(column, part.shape[1]),
                    ],
                    sems.at[place],
                )
            )
        for copy in copies:
            copy.start()
        for copy in copies:
            copy.wait()

    out[...] = jnp.dot(held[...], weight[...], preferred_element_type=jnp.float32).astype(
        out.dtype
    )


def project(me, parts, weight, after=()):
    depth, columns = weight.shape
    rows = parts[0][2].shape[0]
    total = rows * lax.axis_size("ctx")
    layout = [(mask, (which or 0) * depth // 2) for mask, which, _ in parts]
    tile = min(256, columns)
    return launch(
        functools.partial(project_kernel, layout),
        [me],
        [weight] + [part for _, _, part in parts],
        [pl.BlockSpec((depth, tile), lambda j, me: (0, j))] + [ANY] * len(parts),
        pl.BlockSpec((total, tile), lambda j, me: (0, j)),
        jax.ShapeDtypeStruct((total, columns), jnp.bfloat16),
        after=after,
        grid=(columns // tile,),
        scratch=[
            pltpu.VMEM((total, depth), jnp.bfloat16),
            pltpu.SemaphoreType.DMA((len(parts),)),
        ],
        limit=40,
        cost_estimate=cost(
            2 * total * depth * columns, 2 * (total * depth + depth * columns + total * columns)
        ),
        name="project",
    )


def hidden_kernel(layout, me, gain, gate_rows, up_rows, *refs):
    parts, (out, held, total, squares, sems) = refs[: len(layout)], refs[len(layout) :]
    turn = pl.program_id(0)

    def copy_of(place):
        mask, row = layout[place]
        part = parts[place]
        column = ((me[0] ^ mask) & 1) * part.shape[1]
        return pltpu.make_async_copy(
            part,
            held.at[
                mask // 2,
                pl.ds(row, part.shape[0]),
                pl.ds(pl.multiple_of(column, LANES), part.shape[1]),
            ],
            sems.at[place],
        )

    @pl.when(turn == 0)
    def _():
        for place in range(len(layout)):
            copy_of(place).start()
        total[...] = jnp.zeros_like(total)
        squares[...] = jnp.zeros_like(squares)

    for place, (mask, _) in enumerate(layout):

        @pl.when(turn == mask // 2)
        def _():
            copy_of(place).wait()

    width = out.shape[1]
    both = jnp.concatenate([gate_rows[...], up_rows[...]], axis=1)
    total[...] += jnp.dot(held[turn], both, preferred_element_type=jnp.float32)
    slots = out.shape[0]
    for row in range(0, slots, 64):
        mixer_square = squares[row : row + 64, :]
        for lane in range(0, held.shape[2], LANES):
            value = held[turn, row : row + 64, lane : lane + LANES].astype(jnp.float32)
            spot = lane % gain.shape[2]
            value = value * gain[lane // gain.shape[2], :, spot : spot + LANES]
            mixer_square += value * value
        squares[row : row + 64, :] = mixer_square

    @pl.when(turn == pl.num_programs(0) - 1)
    def _():
        def finish(index, _):
            spot = pl.ds(pl.multiple_of(index * 64, 64), 64)
            mean = jnp.sum(squares[spot, :], axis=1, keepdims=True) / D
            factor = lax.rsqrt(mean + 1e-05)
            gate_act = total[spot, 0:width] * factor
            up_act = total[spot, width:] * factor
            out[spot, :] = (silu(gate_act) * up_act).astype(out.dtype)
            return 0

        lax.fori_loop(0, out.shape[0] // 64, finish, 0)


def hidden_units(me, groups, one_over_gain, gate, up, after=()):
    depth = groups[0][0][2].shape[1]
    count = lax.axis_size("ctx")
    width = gate.shape[1]
    layout, parts, slots = [], [], 0
    for group in groups:
        rows = group[0][2].shape[0]
        layout += [(mask, slots + (which or 0) * rows // 2) for mask, which, _ in group]
        parts += group
        slots += rows
    block = pl.BlockSpec((2 * depth, width), lambda k, me: ((me[0] // 2) ^ k, 0))
    return launch(
        functools.partial(hidden_kernel, layout),
        [me],
        [one_over_gain, gate, up] + [part for _, _, part in parts],
        [
            pl.BlockSpec((2, 1, depth), lambda k, me: ((me[0] // 2) ^ k, 0, 0)),
            block,
            block,
        ] + [ANY] * len(parts),
        pl.BlockSpec((slots, width), lambda k, me: (0, 0)),
        jax.ShapeDtypeStruct((slots, width), jnp.bfloat16),
        after=after,
        grid=(count // 2,),
        scratch=[
            pltpu.VMEM((count // 2, slots, 2 * depth), jnp.bfloat16),
            pltpu.VMEM((slots, 2 * width), jnp.float32),
            pltpu.VMEM((slots, LANES), jnp.float32),
            pltpu.SemaphoreType.DMA((len(parts),)),
        ],
        limit=40,
        cost_estimate=cost(
            4 * slots * depth * count * width, 2 * count * depth * (slots + 2 * width)
        ),
        name="hidden_units",
    )


def down_kernel(layout, me, *refs):
    count = len(layout)
    units, weights, (out, held, sems) = refs[:count], refs[count:-3], refs[-3:]
    width = weights[0].shape[0]

    @pl.when(pl.program_id(0) == 0)
    def _():
        copies = []
        for place, (mask, row) in enumerate(layout):
            unit = units[place]
            copies.append(
                pltpu.make_async_copy(
                    unit,
                    held.at[pl.ds(row, unit.shape[0]), pl.ds(mask * width, width)],
                    sems.at[place],
                )
            )
        for copy in copies:
            copy.start()
        for copy in copies:
            copy.wait()

    tall = jnp.concatenate([weight[...] for weight in weights], axis=0)
    out[...] = jnp.dot(held[...], tall, preferred_element_type=jnp.float32).astype(out.dtype)


def down(me, parts, weights, own, after=()):
    columns = weights[-1].shape[1]
    width = own.shape[0]
    depth = width * len(weights)
    slots = parts[0][2].shape[0]
    tile = min(256, columns)
    layout = [(mask, (which or 0) * slots // 2) for mask, which, _ in parts]
    units = [part for _, _, part in parts]
    steps = columns // tile
    return launch(
        functools.partial(down_kernel, layout),
        [me],
        units + [own] + list(weights[1:]),
        [ANY] * len(units)
        + [pl.BlockSpec((width, tile), lambda j, me: (0, me[0] * steps + j))]
        + [pl.BlockSpec((width, tile), lambda j, me: (0, j))] * (len(weights) - 1),
        pl.BlockSpec((slots, tile), lambda j, me: (0, j)),
        jax.ShapeDtypeStruct((slots, columns), jnp.bfloat16),
        after=after,
        grid=(steps,),
        scratch=[
            pltpu.VMEM((slots, depth), jnp.bfloat16),
            pltpu.SemaphoreType.DMA((len(units),)),
        ],
        limit=40,
        cost_estimate=cost(
            2 * slots * depth * columns, 2 * (slots * depth + depth * columns + slots * columns)
        ),
        name="down",
    )


def cross_kernel(begin, me, *refs):
    units, (own, *sent), refs = refs[:6], refs[6:12], refs[12:]
    keep, give_a, give_b, held, sems = refs
    width = own.shape[0]
    turn = pl.program_id(0)

    @pl.when(turn == 0)
    def _():
        copies = []
        for mask, unit in enumerate(units):
            column = (2, 3, 0, 1, 4, 5)[mask] * width
            copies.append(
                pltpu.make_async_copy(
                    unit.at[pl.ds(begin, held.shape[0]), :],
                    held.at[:, pl.ds(column, width)],
                    sems.at[mask],
                )
            )
        for copy in copies:
            copy.start()
        for copy in copies:
            copy.wait()

    def summed(first, weights):
        tall = jnp.concatenate([weight[...] for weight in weights], axis=0)
        rows = held[:, first * width : (first + 4) * width]
        return jnp.dot(rows, tall, preferred_element_type=jnp.float32).astype(keep.dtype)

    for step, out in enumerate((keep, give_a, keep, give_b)):

        @pl.when(turn == step)
        def _():
            if step < 2:
                out[...] = summed(0, [sent[1], sent[2], own, sent[0]])
            else:
                out[...] = summed(2, [own, sent[0], sent[3], sent[4]])


def cross_down(me, units, begin, slots, weights, own, after=()):
    width = own.shape[0]
    half = weights[2].shape[1] // 2

    def mine(j, me):
        return (0, (me[0] ^ (jnp.where(j == 1, 4, 0) + jnp.where(j == 3, 2, 0))) * 2 + j // 2)

    front = pl.BlockSpec((width, half), lambda j, me: (0, jnp.minimum(j, 1)))
    back = pl.BlockSpec((width, half), lambda j, me: (0, jnp.maximum(j - 2, 0)))
    given = pl.BlockSpec((slots, half), lambda j, me: (0, 0))
    return launch(
        functools.partial(cross_kernel, begin),
        [me],
        [units[mask] for mask in range(6)] + [own] + [weights[mask] for mask in range(1, 6)],
        [ANY] * 6
        + [
            pl.BlockSpec((width, half), mine),
            pl.BlockSpec((width, half), lambda j, me: (0, j)),
            front,
            front,
            back,
            back,
        ],
        [pl.BlockSpec((slots, half), lambda j, me: (0, j // 2)), given, given],
        [
            jax.ShapeDtypeStruct((slots, 2 * half), jnp.bfloat16),
            jax.ShapeDtypeStruct((slots, half), jnp.bfloat16),
            jax.ShapeDtypeStruct((slots, half), jnp.bfloat16),
        ],
        after=after,
        grid=(4,),
        scratch=[
            pltpu.VMEM((slots, 6 * width), jnp.bfloat16),
            pltpu.SemaphoreType.DMA((6,)),
        ],
        limit=40,
        cost_estimate=cost(16 * slots * 4 * width * half, 24 * width * half * 2),
        name="cross_down",
    )


def settle_kernel(keep, first, second, *outs):
    half = first.shape[1]
    rows = outs[0].shape[0]
    for place, out in enumerate(outs):
        spot = slice(place * rows, (place + 1) * rows)
        for column, other in ((0, first), (half, second)):
            total = keep[spot, column : column + half].astype(jnp.float32)
            out[:, column : column + half] = (
                total + other[spot, :].astype(jnp.float32)
            ).astype(out.dtype)


def settle(keep, first, second, count, after=()):
    slots, columns = keep.shape
    whole = lambda array: pl.BlockSpec(array.shape, lambda j: (0, 0))
    shape = (slots // count, columns)
    return launch(
        settle_kernel,
        [],
        [keep, first, second],
        [whole(keep), whole(first), whole(second)],
        [pl.BlockSpec(shape, lambda j: (0, 0))] * count,
        [jax.ShapeDtypeStruct(shape, keep.dtype)] * count,
        after=after,
        limit=24,
        cost_estimate=cost(2 * keep.size, 6 * keep.size),
        name="settle",
    )


def pick_kernel(count, rows, *refs):
    for picks, out in zip(refs[:count], refs[count:]):
        out[...] = lax.dot_general(
            picks[...], rows[...], (((0,), (0,)), ((), ())), preferred_element_type=jnp.float32
        ).astype(out.dtype)


def pick_rows(picks, rows, after=()):
    shape = (picks[0].shape[1], rows.shape[1])
    whole = lambda shape: pl.BlockSpec(shape, lambda j: (0, 0))
    return launch(
        functools.partial(pick_kernel, len(picks)),
        [],
        [rows] + list(picks),
        [whole(rows.shape)] + [whole(pick.shape) for pick in picks],
        [whole(shape)] * len(picks),
        [jax.ShapeDtypeStruct(shape, rows.dtype)] * len(picks),
        after=after,
        limit=24,
        cost_estimate=cost(2 * rows.size * shape[0] * len(picks), 4 * rows.size),
        name="pick_rows",
    )


def combine_kernel(me, mixer, ids, gates, *refs):
    out = refs[-1]
    count = len(refs) // 2
    total = mixer[...].astype(jnp.float32)
    for mask in range(count):
        named = ids[...] == (me[0] ^ mask)
        gate = jnp.sum(jnp.where(named, gates[...], 0.0), axis=1, keepdims=True)
        total += gate * jnp.dot(
            refs[mask][...], refs[count + mask][...], preferred_element_type=jnp.float32
        )
    out[...] = total.astype(out.dtype)


def combine(me, mixer_out, ids, gates, picks, answers):
    operands = [mixer_out, ids, gates] + list(picks) + list(answers)
    return launch(
        combine_kernel,
        [me],
        operands,
        [pl.BlockSpec(array.shape, lambda j, me: (0, 0)) for array in operands],
        pl.BlockSpec(mixer_out.shape, lambda j, me: (0, 0)),
        jax.ShapeDtypeStruct(mixer_out.shape, jnp.bfloat16),
        cost_estimate=cost(
            2 * mixer_out.size * answers[0].shape[0] * len(answers), 4 * mixer_out.size
        ),
        limit=24,
        name="combine",
    )


def shards(
    mixer_in,
    gate_in,
    delta_in,
    b_proj,
    c_proj,
    conv_kernel,
    conv_bias,
    delta_bias,
    decay_log,
    skip_gain,
    prefix_state,
    prefix_tail,
    out_proj,
    residual,
    norm_gain,
    expert_gate,
    expert_up,
    expert_down,
    expert_ids,
    route_gates,
):
    tokens = mixer_in.shape[0]
    rim = prefix_tail.shape[0]
    ctx_count = lax.axis_size("ctx")
    exp_count = lax.axis_size("exp")
    ctx_me = lax.axis_index("ctx")
    exp_me = lax.axis_index("exp")
    me = ctx_me.astype(jnp.int32).reshape(1)

    rim_rows = from_behind(mixer_in[tokens - rim :], "ctx", 1)
    rim_rows = jnp.where(ctx_me == 0, prefix_tail, rim_rows).astype(jnp.float32)
    rim8 = jnp.pad(rim_rows, ((8 - rim, 0), (0, 0)))

    width = out_proj.shape[1]
    down_rows = expert_down[0]
    down_parts = {}
    crossing = ctx_count == 8

    def send_columns(masks, after=()):
        if crossing:
            layouts = {1: [(1, 0), (5, 0), (1, 1), (3, 1)]}
            layouts.update({mask: [(mask, 0), (mask ^ 4, 0)] for mask in (2, 3)})
            layouts.update({mask: [(mask, 1), (mask ^ 2, 1)] for mask in (4, 5)})
            cuts = cut_columns(me, down_rows, width // 2, [layouts[m] for m in masks], after)
        else:
            cuts = cut_columns(me, down_rows, width, [[(m, 0)] for m in masks], after)
        for mask, cut in zip(masks, cuts):
            down_parts[mask] = swap(cut, "ctx", mask)
        return cuts, tuple(down_parts[mask] for mask in masks)


    extra, left = [], norm_gain
    for _ in range(3):
        extra.append(lax.reduce_precision(left, 8, 7))
        left = left - extra[-1]
    extra = jnp.concatenate(extra)
    extra = jnp.pad(extra, (0, mixer_in.shape[1] - extra.shape[0]))[None, :]

    wide = lambda proj: jnp.broadcast_to(proj.T[:, :, None], (tokens, 16, LANES)).reshape(
        tokens * 16, LANES
    )
    b_wide, c_wide = wide(b_proj), wide(c_proj)
    step, conv_act, end = local_states(
        mixer_in,
        rim8,
        delta_in,
        conv_kernel,
        conv_bias[None, :],
        delta_bias[None, :],
        decay_log,
        extra,
        b_wide,
    )
    chunks = 2
    state, ends = prefix_state, gather_parts(end)
    one_over_gain = inverse_gains(me, ends, width)
    gated = []
    for chunk in range(chunks):
        rows, state = read_out(
            me,
            chunk,
            chunks,
            step,
            conv_act,
            gate_in,
            decay_log,
            skip_gain[None, :],
            b_wide,
            c_wide,
            state,
            ends,
        )
        ends = []
        gated.append(rows)
    near = lambda parts: [part for mask, _, part in parts if mask in (2, 4)]
    far = lambda parts: [part for mask, which, part in parts if which is not None][::2]
    scatter = lambda rows: lax.psum_scatter(rows, "exp", scatter_dimension=0, tiled=True)
    front = gather_parts(gated[0], 1, gated[1:])
    cuts, late = send_columns([3, 5, 1, 2, 4] if crossing else list(range(1, ctx_count)), near(front))
    back = gather_parts(gated[1], 1, far(front))
    partial = project(me, front, out_proj, near(back))
    projected = [scatter(partial)]
    partial = project(me, back, out_proj, [partial, cuts[0]])
    projected.append(scatter(partial))

    block_rows = residual.shape[0]
    owners = block_rows // tokens
    projected = jnp.stack(
        [piece.reshape(owners, tokens // chunks, width) for piece in projected], axis=1
    ).reshape(block_rows, width)
    mixer_out = (residual.astype(jnp.float32) + projected.astype(jnp.float32)).astype(
        jnp.bfloat16
    )
    mixer_wide = mixer_out.astype(jnp.float32)
    scaled = (mixer_wide * norm_gain[None, :]).astype(jnp.bfloat16)
    experts = expert_gate.shape[0] * exp_count
    capacity = 3 * block_rows * expert_ids.shape[1] // (2 * experts)
    spots = jnp.arange(capacity, dtype=jnp.int32)
    picked = []
    for mask in range(exp_count):
        here = jnp.any(expert_ids == (exp_me ^ mask), axis=1)
        place = jnp.cumsum(here.astype(jnp.int32)) - 1
        pick = here[:, None] & (place[:, None] == spots[None, :])
        picked.append(pick.astype(jnp.bfloat16))

    groups = [[0], list(range(1, exp_count))]
    sent = pick_rows(picked, scaled, late)
    pieces = [rows if mask == 0 else swap(rows, "exp", mask) for mask, rows in enumerate(sent)]
    weights = [None] + [down_parts[mask] for mask in sorted(down_parts)]
    gathered_units, arrived, order, ready = [], (), (), ()
    for group in groups:
        rows = [pieces[mask] for mask in group]
        rows = join(rows, arrived) if len(group) > 1 else rows[0]
        parts = gather_parts(rows, 0, order)
        arrived = far(parts)
        hidden = hidden_units(me, [parts], one_over_gain, expert_gate[0], expert_up[0], ready)
        order = [hidden]
        if crossing:
            units = {0: hidden, 2: swap(hidden, "ctx", 2), 4: swap(hidden, "ctx", 4)}
            units.update({mask + 1: swap(units[mask], "ctx", 1) for mask in (0, 2, 4)})
            ready = [units[2], units[4]]
        else:
            units = gather_parts(hidden)
        gathered_units.append(units)
    answers, order, before = {}, (), ()
    if crossing:
        far_masks = list(range(2, exp_count))
        work = [
            (gathered_units[1], capacity, far_masks),
            (gathered_units[1], 0, [1]),
            (gathered_units[0], 0, [0]),
        ]
    else:
        work = [(gathered_units[1], 0, groups[1]), (gathered_units[0], 0, groups[0])]
    for units, begin, masks in work:
        if crossing:
            slots = capacity * len(masks)
            keep, first, second = cross_down(me, units, begin, slots, weights, down_rows, order)
            first, second = swap(first, "ctx", 4), swap(second, "ctx", 2)
            before = settle(keep, first, second, len(masks), before)
        else:
            keep = down(me, units, weights, down_rows, order)
            before = jnp.split(keep, len(masks))
        order = [keep] if order else list(before)
        for mask, piece in zip(masks, before):
            answers[mask] = piece if mask == 0 else swap(piece, "exp", mask)
    block_out = combine(
        exp_me.astype(jnp.int32).reshape(1),
        mixer_out,
        expert_ids,
        route_gates,
        picked,
        [answers[mask] for mask in range(exp_count)],
    )
    return (mixer_out, block_out)


def solution(mesh):
    placed = (
        P("ctx", "exp"),
        P("ctx", "exp"),
        P("ctx", "exp"),
        P(None, "ctx"),
        P(None, "ctx"),
        P(None, "exp"),
        P("exp"),
        P("exp"),
        P(None, "exp"),
        P("exp"),
        P(None, "exp"),
        P(None, "exp"),
        P("exp", "ctx"),
        P("exp", "ctx"),
        P("ctx"),
        P("exp", None, "ctx"),
        P("exp", None, "ctx"),
        P("exp", "ctx", None),
        P("exp", None),
        P("exp", None),
    )
    return jax.shard_map(
        shards,
        mesh=mesh,
        in_specs=placed,
        out_specs=(P("exp", "ctx"), P("exp", "ctx")),
        check_vma=False,
    )
```
